32 devices in a mesh: dp: 4 (over x, core), fsdp: 8 (over z, y).
Axes of the slice: x: 2, y: 2, z: 4, core: 2. Of those that a mesh axis runs over, the one named last changes fastest.
Arguments:
- block_input: bfloat16 [2, 8192, 2, 1024], P(None, ('dp', 'fsdp')), may hold values from -6 to 6
- out_grad: bfloat16 [2, 8192, 2, 1024], P(None, ('dp', 'fsdp')), may hold values from -6 to 6
- item_lengths: int32 [2, 256], P(None, ('dp', 'fsdp')), may hold values from 8 to 32, as said below
- frame_offsets: int32 [2, 256], P(None, ('dp', 'fsdp')), may hold values from 0 to 24, as said below
- norm_attn: bfloat16 [2, 1024], P(None, 'fsdp'), may hold values from 0.099609375 to 1.8984375
- w_qkv: bfloat16 [2, 1024, 3072], P(None, 'fsdp'), may hold values from -0.1875 to 0.1875
- w_out: bfloat16 [2, 1024, 1024], P(None, 'fsdp'), may hold values from -0.25 to 0.25
- norm_ffn: bfloat16 [2, 1024], P(None, 'fsdp'), may hold values from 0.099609375 to 1.8984375
- w_gate_up: bfloat16 [2, 1024, 5632], P(None, 'fsdp'), may hold values from -0.1875 to 0.1875
- w_down: bfloat16 [2, 2816, 1024], P(None, 'fsdp'), may hold values from -0.109375 to 0.109375
Outputs:
- block_output: bfloat16 [2, 8192, 2, 1024], P(None, ('dp', 'fsdp'))
- input_grad: bfloat16 [2, 8192, 2, 1024], P(None, ('dp', 'fsdp'))
- grad_norm_attn: float32 [2, 1024], P(None, 'fsdp')
- grad_w_qkv: float32 [2, 1024, 3072], P(None, 'fsdp')
- grad_w_out: float32 [2, 1024, 1024], P(None, 'fsdp')
- grad_norm_ffn: float32 [2, 1024], P(None, 'fsdp')
- grad_w_gate_up: float32 [2, 1024, 5632], P(None, 'fsdp')
- grad_w_down: float32 [2, 2816, 1024], P(None, 'fsdp')
The draws below stay inside these ranges and needn't reach their ends.
Inputs may be any that keep to these rules, and one draw needn't show every extreme that they name: `item_lengths`: the first item of each micro-batch fills all 32 slots; the second holds 8 frames. `frame_offsets`: offset plus length never exceeds 32; the second item of each micro-batch starts at slot 24.
All inputs are finite; a program needn't handle non-finite values.
Results may differ from the reference program's by a relative error of at most 0.013.
Values may be sent and summed in bfloat16 or wider, within the bound.
A program may use at most 448 MiB of HBM per device.

```python
import math
import jax
import jax.numpy as jnp
from jax import lax

D = 1024
HEADS = 16
FF = 2816
POSITIONS = 2
MICRO = 2
ITEM_SLOTS = 32
FRAMES = 8192
ITEMS = 256


def item_table(key):
    first_key, second_key = jax.random.split(key)
    lengths = jax.random.randint(first_key, (MICRO, ITEMS), ITEM_SLOTS // 4, ITEM_SLOTS + 1)
    lengths = lengths.at[:, 0].set(ITEM_SLOTS)
    lengths = lengths.at[:, 1].set(ITEM_SLOTS // 4)
    offsets = jax.random.randint(second_key, (MICRO, ITEMS), 0, ITEM_SLOTS - lengths + 1)
    offsets = offsets.at[:, 1].set(ITEM_SLOTS - ITEM_SLOTS // 4)
    return (lengths.astype(jnp.int32), offsets.astype(jnp.int32))


def draw_item_lengths(key, part):
    lengths, offsets = item_table(key)
    return lengths


def draw_frame_offsets(key, part):
    lengths, offsets = item_table(key)
    return offsets


def levels(rng, dims, cuts, low, top_value):
    gain = 1.0
    for dim, parts in cuts:
        heights = jax.random.uniform(jax.random.fold_in(jax.random.fold_in(rng, 6), dim), (parts,), jnp.float32, low / len(cuts), top_value / len(cuts))
        gain = gain * jnp.repeat(jnp.exp(heights), dims[dim] // parts).reshape((-1,) + (1,) * (len(dims) - 1 - dim))
    return gain


def scatter_about(stream_key, extent, scale, most, shards=(), kind=jnp.bfloat16):
    values = scale * jax.random.normal(stream_key, extent, jnp.float32)
    if shards:
        values = values * levels(stream_key, extent, shards, -0.22, 0.18)
    return jnp.clip(values, -most, most).astype(kind)


def setup_inputs(seed: int = 0) -> dict:
    splits = jax.random.split(jax.random.key(seed), 11)
    return {
        "block_input": scatter_about(splits[0], (MICRO, FRAMES, POSITIONS, D), 1.0, 6.0, ((1, 32),)),
        "out_grad": scatter_about(splits[1], (MICRO, FRAMES, POSITIONS, D), 1.0, 6.0, ((1, 32),)),
        "item_lengths": draw_item_lengths(jax.random.fold_in(splits[10], 71), 0),
        "frame_offsets": draw_frame_offsets(jax.random.fold_in(splits[10], 71), 0),
        "norm_attn": jnp.clip(1.0 + 0.18 * jax.random.normal(splits[4], (POSITIONS, D), jnp.float32), 0.099609375, 1.8984375).astype(jnp.bfloat16),
        "w_qkv": scatter_about(splits[5], (POSITIONS, D, 3 * D), D ** -0.5, 0.1875, ((1, 8),)),
        "w_out": scatter_about(splits[6], (POSITIONS, D, D), (D // 2) ** -0.5, 0.25, ((1, 8),)),
        "norm_ffn": jnp.clip(1.0 + 0.18 * jax.random.normal(splits[7], (POSITIONS, D), jnp.float32), 0.099609375, 1.8984375).astype(jnp.bfloat16),
        "w_gate_up": scatter_about(splits[8], (POSITIONS, D, 2 * FF), D ** -0.5, 0.1875, ((1, 8),)),
        "w_down": scatter_about(splits[9], (POSITIONS, FF, D), FF ** -0.5, 0.109375, ((1, 8),)),
    }


@jax.custom_vjp
def low(v):
    return lax.optimization_barrier(v.astype(jnp.bfloat16)).astype(jnp.float32)

@jax.custom_vjp
def low_back(v):
    return v

def low_keep(v):
    return (low(v), None)

def low_pass(kept, grad):
    return (grad,)

def back_keep(v):
    return (v, None)

def back_low(kept, grad):
    return (low(grad),)
low.defvjp(low_keep, low_pass)
low_back.defvjp(back_keep, back_low)
EPSILON = 1e-05
PRECISE = lax.Precision.HIGHEST

def project(values, weight):
    return jnp.einsum('bpd,pde->bpe', values, weight, precision=PRECISE)

def rms_scale(values):
    return lax.rsqrt(lax.optimization_barrier(jnp.mean(values * values, axis=-1, keepdims=True)) + EPSILON)

def forward(inputs, norm_attn, w_qkv, w_out, norm_ffn, w_gate_up, w_down):
    frames, positions, model_width = inputs.shape
    head_dim = model_width // HEADS
    hidden_size = w_down.shape[1]
    normed = low(inputs * rms_scale(inputs) * norm_attn[None])
    qkv_proj = low_back(low(project(normed, w_qkv)))
    shape = (frames, positions, HEADS, head_dim)
    query_heads = qkv_proj[..., :model_width].reshape(shape)
    key_heads = qkv_proj[..., model_width:2 * model_width].reshape(shape)
    value_heads = qkv_proj[..., 2 * model_width:].reshape(shape)
    scores = jnp.einsum('bihd,bjhd->bhij', query_heads, key_heads, precision=PRECISE) / math.sqrt(head_dim)
    causal = jnp.arange(positions)[:, None] >= jnp.arange(positions)[None, :]
    scores = jnp.where(causal, scores, -1e+30)
    attention = low(jax.nn.softmax(scores, axis=-1))
    mixed_heads = jnp.einsum('bhij,bjhd->bihd', attention, value_heads, precision=PRECISE)
    mixed_heads = low_back(low(mixed_heads.reshape(frames, positions, model_width)))
    middle = inputs + low_back(project(mixed_heads, w_out))
    normed_two = low(middle * rms_scale(middle) * norm_ffn[None])
    gate_up = low_back(project(normed_two, w_gate_up))
    hidden = low(jax.nn.silu(gate_up[..., :hidden_size]) * gate_up[..., hidden_size:])
    return middle + low_back(project(hidden, w_down))

def reference(block_input, out_grad, item_lengths, frame_offsets, norm_attn, w_qkv, w_out, norm_ffn, w_gate_up, w_down):
    weights = tuple((weight.astype(jnp.float32) for weight in (norm_attn, w_qkv, w_out, norm_ffn, w_gate_up, w_down)))
    frame_index = jnp.arange(FRAMES)
    slot_index = frame_index % ITEM_SLOTS
    item_index = frame_index // ITEM_SLOTS
    first_slot = frame_offsets[:, item_index]
    past_slot = first_slot + item_lengths[:, item_index]
    valid_rows = ((slot_index[None] >= first_slot) & (slot_index[None] < past_slot)).astype(jnp.float32)
    block_rows = math.gcd(FRAMES, 1024)
    block_count = FRAMES // block_rows

    def scan_step(totals, pieces):
        inputs, upstream, valid_block = pieces
        result, pullback = jax.vjp(forward, inputs.astype(jnp.float32), *weights)
        gradients = pullback(upstream.astype(jnp.float32) * valid_block[:, None, None])
        totals = tuple((total + update for total, update in zip(totals, gradients[1:])))
        return (totals, (result.astype(jnp.bfloat16), gradients[0].astype(jnp.bfloat16)))
    totals = tuple((jnp.zeros(weight.shape, jnp.float32) for weight in weights))
    shape = (MICRO * block_count, block_rows, POSITIONS, D)
    totals, (outputs, input_grads) = lax.scan(scan_step, totals, (block_input.reshape(shape), out_grad.reshape(shape), valid_rows.reshape(MICRO * block_count, block_rows)))
    whole = (MICRO, FRAMES, POSITIONS, D)
    return (outputs.reshape(whole), input_grads.reshape(whole), totals[0], totals[1], totals[2], totals[3], totals[4], totals[5])
```

```python
import functools
import math

import jax
import jax.numpy as jnp
from jax import lax
from jax.experimental import pallas as pl
from jax.experimental.pallas import tpu as pltpu
from jax.sharding import PartitionSpec as P

MESH = pl.DeviceIdType.MESH
BF = jnp.bfloat16
F32 = jnp.float32
HEADS = 16
ITEM_SLOTS = 32
EPSILON = 1e-05
LANES = 3
AXES = ("dp", "fsdp")


def place(n):
    dp, f = lax.axis_index("dp"), lax.axis_index("fsdp")
    x, c = lax.div(dp, 2), lax.rem(dp, 2)
    z, h = lax.div(f, 2), lax.rem(f, 2)
    r = z * (1 - h) + (n - 1 - z) * h
    return x, c, f, r


def ring_index(r, n):
    hh = lax.div(r, n // 2)
    return (2 * r) * (1 - hh) + (2 * (n - 1 - r) + 1) * hh


class Spot:
    def __init__(self, n):
        self.n = n
        x, c, f, r = place(n)
        self.x, self.c, self.f, self.r = x, c, f, r
        self.d = 1 - 2 * c
        dp = 2 * x + c
        self.next = (dp, ring_index(lax.rem(r + self.d + n, n), n))
        self.prev = (dp, ring_index(lax.rem(r - self.d + n, n), n))
        self.sib = (2 * x + 1 - c, f)
        self.mate = (2 * (1 - x) + c, f)

    def owner(self, hop):
        return ring_index(lax.rem(self.r - self.d * (hop + 1) + self.n, self.n), self.n)

    def greet(self):
        barrier = pltpu.get_barrier_semaphore()
        for who in (self.next, self.prev, self.sib, self.mate):
            pl.semaphore_signal(barrier, inc=1, device_id=who, device_id_type=MESH)
        pl.semaphore_wait(barrier, 4)


def remote(src, dst, send, recv, who):
    return pltpu.make_async_remote_copy(src, dst, send, recv, device_id=who, device_id_type=MESH)


def cut(rows, parts):
    while parts > 1 and rows % (16 * parts):
        parts -= 1
    return parts


def pieces_of(shapes, parts):
    out = []
    for a, (shape, count) in enumerate(zip(shapes, parts)):
        count = cut(shape[0], count)
        rows = shape[0] // count
        for k in range(count):
            out.append((a, k * rows, rows, shape[1] // 2))
    return out


def lanes_of(pieces):
    return [pieces[k::LANES] for k in range(LANES)]


def gather_kernel(n, lanes, shard_rows, *refs):
    xs, xo, gs, go, wq, wo, wg, wd = refs[:8]
    xr, gr, aq, ao, ag, ad = refs[8:14]
    ring_send, ring_recv, sib_send, sib_recv, loc, swap_send, swap_recv = refs[14:]
    spot = Spot(n)
    shards, wholes = (wq, wo, wg, wd), (aq, ao, ag, ad)
    half = xo.shape[0]
    local = []
    for k, (src, dst, count) in enumerate(zip(shards, wholes, shard_rows)):
        cp = pltpu.make_async_copy(src.at[spot.x], dst.at[pl.ds(spot.f * count, count)], loc.at[k])
        cp.start()
        local.append(cp)
    for k, (src, dst) in enumerate(((xo, xr), (go, gr))):
        cp = pltpu.make_async_copy(src, dst.at[pl.ds(spot.x * half, half)], loc.at[4 + k])
        cp.start()
        local.append(cp)
    spot.greet()
    swaps = []
    for k, (src, dst) in enumerate(((xs, xr), (gs, gr))):
        cp = remote(src, dst.at[pl.ds(spot.x * half, half)], swap_send.at[k], swap_recv.at[k], spot.mate)
        cp.start()
        swaps.append(cp)

    def block(piece, owner):
        a, first, rows, cols = piece
        return wholes[a].at[pl.ds(owner * shard_rows[a] + first, rows), pl.ds(spot.c * cols, cols)]

    def send(lane, t):
        piece, hop = lanes[lane][t // (n - 1)], t % (n - 1)
        a, first, rows, cols = piece
        if hop == 0:
            src = shards[a].at[spot.x, pl.ds(first, rows), pl.ds(spot.c * cols, cols)]
            dst = block(piece, spot.f)
        else:
            src = dst = block(piece, spot.owner(hop - 1))
        cp = remote(src, dst, ring_send.at[lane, t], ring_recv.at[lane, t], spot.next)
        cp.start()
        return cp

    total = [len(lane) * (n - 1) for lane in lanes]
    flying = {lane: send(lane, 0) for lane in range(len(lanes)) if total[lane]}
    done = list(swaps)
    sent = []
    for t in range(max(total)):
        for lane in range(len(lanes)):
            if t >= total[lane]:
                continue
            flying[lane].wait_recv()
            sent.append(flying[lane])
            if t + 1 < total[lane]:
                flying[lane] = send(lane, t + 1)
            piece, hop = lanes[lane][t // (n - 1)], t % (n - 1)
            arrived = block(piece, spot.owner(hop))
            cp = remote(arrived, arrived, sib_send.at[lane, t], sib_recv.at[lane, t], spot.sib)
            cp.start()
            done.append(cp)
    for cp in local:
        cp.wait()
    for cp in sent:
        cp.wait_send()
    for cp in done:
        cp.wait()


def gather(n, xs, xo, gs, go, wq, wo, wg, wd):
    weights = (wq, wo, wg, wd)
    shapes = [w.shape[1:] for w in weights]
    lanes = lanes_of(pieces_of(shapes, (2, 1, 4, 2)))
    steps = max(len(lane) for lane in lanes) * (n - 1)
    rows = xo.shape[0]
    hbm = pl.BlockSpec(memory_space=pltpu.HBM)
    out = [jax.ShapeDtypeStruct((2 * rows, xo.shape[1]), BF)] * 2 + [
        jax.ShapeDtypeStruct((s[0] * n, s[1]), BF) for s in shapes
    ]
    return pl.pallas_call(
        functools.partial(gather_kernel, n, lanes, [s[0] for s in shapes]),
        out_shape=out,
        in_specs=[hbm] * 8,
        out_specs=[hbm] * 6,
        scratch_shapes=[pltpu.SemaphoreType.DMA((LANES, steps))] * 4
        + [pltpu.SemaphoreType.DMA((6,)), pltpu.SemaphoreType.DMA((2,)), pltpu.SemaphoreType.DMA((2,))],
        compiler_params=pltpu.CompilerParams(collective_id=0, has_side_effects=True),
        name="gather_weights",
    )(xs, xo, gs, go, *weights)


def scatter_kernel(n, lanes, shard_rows, *refs):
    mine = refs[:4]
    outs = refs[4:8]
    arrived, ends = refs[8:12], refs[12:16]
    ring_send, ring_recv, loc, sib_send, sib_recv, mate_send, mate_recv, far_send, far_recv = refs[16:]
    spot = Spot(n)
    spot.greet()

    def own(piece, owner):
        a, first, rows, cols = piece
        return mine[a].at[pl.ds(owner * shard_rows[a] + first, rows), :]

    def landing(piece, hop):
        a, first, rows, cols = piece
        return arrived[a].at[first // rows * (n - 1) + hop]

    total = [len(lane) * (n - 1) for lane in lanes]
    flying = {}
    sent = []
    tail = []

    def launch(lane, t):
        piece, hop = lanes[lane][t // (n - 1)], t % (n - 1)
        src = own(piece, spot.owner(hop))
        if hop:
            held = landing(piece, hop - 1)
            held[...] = (held[...].astype(F32) + src[...].astype(F32)).astype(BF)
            src = held
        cp = remote(src, landing(piece, hop), ring_send.at[lane, t], ring_recv.at[lane, t], spot.next)
        cp.start()
        flying[lane] = cp

    for lane in range(len(lanes)):
        if total[lane]:
            launch(lane, 0)
    mates = []
    k = 0
    for t in range(max(total)):
        for lane in range(len(lanes)):
            if t >= total[lane]:
                continue
            flying[lane].wait_recv()
            sent.append(flying[lane])
            piece, hop = lanes[lane][t // (n - 1)], t % (n - 1)
            if t + 1 < total[lane]:
                launch(lane, t + 1)
            if hop < n - 2:
                continue
            a, first, rows, cols = piece
            end = ends[a].at[pl.ds(first, rows), :]
            end[...] = (own(piece, spot.f)[...].astype(F32) + landing(piece, hop)[...].astype(F32)).astype(BF)
            spread = outs[a].at[spot.x, pl.ds(first, rows), pl.ds(spot.c * cols, cols)]
            cp = pltpu.make_async_copy(end, spread, loc.at[k])
            cp.start()
            tail.append(cp)
            cp = remote(end, spread, sib_send.at[k], sib_recv.at[k], spot.sib)
            cp.start()
            tail.append(cp)
            cp = remote(end, spread, mate_send.at[k], mate_recv.at[k], spot.mate)
            cp.start()
            mates.append((cp, piece, k))
            k += 1
    for cp, piece, k in mates:
        cp.wait()
        a, first, rows, cols = piece
        other = outs[a].at[1 - spot.x, pl.ds(first, rows), pl.ds(spot.c * cols, cols)]
        far = remote(other, other, far_send.at[k], far_recv.at[k], spot.sib)
        far.start()
        tail.append(far)
    for cp in tail:
        cp.wait()
    for cp in sent:
        cp.wait_send()


def scatter(n, grads):
    shapes = [(g.shape[0] // n, 2 * g.shape[1]) for g in grads]
    pieces = pieces_of(shapes, (2, 1, 4, 2))
    lanes = lanes_of(pieces[::-1])
    steps = max(len(lane) for lane in lanes) * (n - 1)
    vmem = pl.BlockSpec(memory_space=pltpu.VMEM)
    dma = pltpu.SemaphoreType.DMA
    count = len(pieces)
    landings = []
    for a in range(4):
        part = [p for p in pieces if p[0] == a]
        landings.append(pltpu.VMEM((len(part) * (n - 1), part[0][2], part[0][3]), BF))
    return pl.pallas_call(
        functools.partial(scatter_kernel, n, lanes, [s[0] for s in shapes]),
        out_shape=[jax.ShapeDtypeStruct((2,) + s, BF) for s in shapes],
        in_specs=[vmem] * 4,
        out_specs=[pl.BlockSpec(memory_space=pltpu.HBM)] * 4,
        scratch_shapes=landings
        + [pltpu.VMEM((s[0], s[1] // 2), BF) for s in shapes]
        + [dma((LANES, steps))] * 2
        + [dma((count,))] * 7,
        compiler_params=pltpu.CompilerParams(
            collective_id=1, has_side_effects=True, vmem_limit_bytes=60 * 2**20
        ),
        name="scatter_gradients",
    )(*grads)


def dot(left, right):
    return jnp.dot(left, right, preferred_element_type=F32)


def dot_nt(left, right):
    return lax.dot_general(left, right, (((1,), (1,)), ((), ())), preferred_element_type=F32)


def dot_tn(left, right):
    return lax.dot_general(left, right, (((0,), (0,)), ((), ())), preferred_element_type=F32)


def rms_scale(values):
    return lax.rsqrt(jnp.mean(values * values, axis=-1, keepdims=True) + EPSILON)


def norm_backward(values, scale, gain, upstream):
    weighted = gain * upstream
    return scale * weighted - values * scale**3 * jnp.mean(values * weighted, axis=-1, keepdims=True)


def swap_perm(n, kind):
    out = []
    for dp in range(4):
        for f in range(n):
            out.append((dp * n + f, (dp ^ kind) * n + f))
    return out


def valid_rows(item_lengths, frame_offsets):
    slot = jnp.arange(ITEM_SLOTS)[None, None, :]
    first = frame_offsets[:, :, None]
    valid = (slot >= first) & (slot < first + item_lengths[:, :, None])
    return valid.reshape(-1)


def by_position(n, block_input, out_grad, item_lengths, frame_offsets, norm_attn, w_qkv, w_out, norm_ffn, w_gate_up, w_down):
    x, c, f, r = place(n)
    micro, frames, positions, width = block_input.shape
    rows = micro * frames
    hidden_size = w_gate_up.shape[2] // 2
    head_dim = width // HEADS
    valid = valid_rows(item_lengths, frame_offsets)[:, None]
    inputs = block_input.reshape(rows, positions, width)
    upstream = jnp.where(valid[..., None], out_grad.reshape(rows, positions, width), 0)

    def take(array, at):
        return lax.dynamic_index_in_dim(array, at, 1, keepdims=False)

    rows_in, rows_up, all_qkv, all_out, all_gu, all_down = gather(
        n, take(inputs, 1 - x), take(inputs, x), take(upstream, 1 - x), take(upstream, x), w_qkv, w_out, w_gate_up, w_down
    )
    gains = lax.all_gather(jnp.stack([norm_attn, norm_ffn]), "fsdp", axis=2, tiled=True)
    gains = lax.dynamic_index_in_dim(gains, x, 1, keepdims=False).astype(F32)
    gain_in, gain_two = gains[0][None], gains[1][None]
    first = x == 0

    def mate(array):
        return lax.ppermute(array, AXES, swap_perm(n, 2))

    def sib(array):
        return lax.ppermute(array, AXES, swap_perm(n, 1))

    values = rows_in.astype(F32)
    scale_one = rms_scale(values)
    normed = (values * scale_one * gain_in).astype(BF)
    qkv = dot(normed, all_qkv).astype(BF)
    query, key, value = qkv[:, :width], qkv[:, width : 2 * width], qkv[:, 2 * width :]
    other = mate(qkv[:, width:])
    key_o, value_o = other[:, :width], other[:, width:]
    heads = (jnp.arange(width)[:, None] // head_dim == jnp.arange(HEADS)[None, :]).astype(F32)

    def per_head(a, b):
        return jnp.dot(a.astype(F32) * b.astype(F32), heads, precision=lax.Precision.HIGHEST)

    def spread(p):
        return jnp.dot(p, heads.T, precision=lax.Precision.HIGHEST)

    score = per_head(query, key) / math.sqrt(head_dim)
    score_o = jnp.where(first, -1e30, per_head(query, key_o) / math.sqrt(head_dim))
    top = jnp.maximum(score, score_o)
    ex, ex_o = jnp.exp(score - top), jnp.exp(score_o - top)
    prob, prob_o = ex / (ex + ex_o), ex_o / (ex + ex_o)
    low, low_o = spread(prob.astype(BF).astype(F32)), spread(prob_o.astype(BF).astype(F32))
    mixed = (low * value.astype(F32) + low_o * value_o.astype(F32)).astype(BF)
    middle = values + dot(mixed, all_out)
    scale_two = rms_scale(middle)
    normed_two = (middle * scale_two * gain_two).astype(BF)
    gate_up = dot(normed_two, all_gu)
    gate, up = gate_up[:, :hidden_size], gate_up[:, hidden_size:]
    sigma = jax.nn.sigmoid(gate)
    hidden = (gate * sigma * up).astype(BF)
    output = (middle + dot(hidden, all_down)).astype(BF)

    def halves(left, right):
        cols = right.shape[1] // 2
        theirs = lax.dynamic_slice_in_dim(right, (1 - c) * cols, cols, 1)
        ours = lax.dynamic_slice_in_dim(right, c * cols, cols, 1)
        return (dot_tn(left, ours) + sib(dot_tn(left, theirs).astype(BF)).astype(F32)).astype(BF)

    grad_down = halves(hidden, rows_up)
    grad_hidden = dot_nt(rows_up, all_down)
    grad_gate = grad_hidden * up * sigma * (1.0 + gate * (1.0 - sigma))
    grad_gu = jnp.concatenate([grad_gate, grad_hidden * gate * sigma], axis=-1).astype(BF)
    grad_w_gu = halves(normed_two, grad_gu)
    grad_normed_two = dot_nt(grad_gu, all_gu)
    grad_gain_two = jnp.sum(grad_normed_two * middle * scale_two, axis=0)
    grad_middle = rows_up.astype(F32) + norm_backward(middle, scale_two, gain_two, grad_normed_two)
    grad_branch = grad_middle.astype(BF)
    grad_w_out = halves(mixed, grad_branch)
    grad_mixed = dot_nt(grad_branch, all_out).astype(BF)
    gm = grad_mixed.astype(F32)
    grad_prob = per_head(grad_mixed, value)
    grad_prob_o = per_head(grad_mixed, value_o)
    total = prob * grad_prob + prob_o * grad_prob_o
    grad_score = spread(prob * (grad_prob - total) / math.sqrt(head_dim))
    grad_score_o = spread(prob_o * (grad_prob_o - total) / math.sqrt(head_dim))
    back = mate(jnp.concatenate([(grad_score_o * query.astype(F32)).astype(BF), (low_o * gm).astype(BF)], axis=-1))
    back = jnp.where(first, back, 0).astype(F32)
    grad_q = grad_score * key.astype(F32) + grad_score_o * key_o.astype(F32)
    grad_k = grad_score * query.astype(F32) + back[:, :width]
    grad_v = low * gm + back[:, width:]
    grad_qkv = jnp.concatenate([grad_q, grad_k, grad_v], axis=-1).astype(BF)
    grad_w_qkv = halves(normed, grad_qkv)
    grad_normed = dot_nt(grad_qkv, all_qkv)
    grad_gain_one = jnp.sum(grad_normed * values * scale_one, axis=0)
    grad_in = (grad_middle + norm_backward(values, scale_one, gain_in, grad_normed)).astype(BF)

    grads = scatter(n, [grad_w_qkv, grad_w_out, grad_w_gu, grad_down])
    grads = [g.astype(F32) for g in grads]
    gain_grads = jnp.stack([grad_gain_one, grad_gain_two])
    gain_grads = jnp.stack([jnp.where(x == p, gain_grads, 0) for p in range(2)], axis=1)
    gain_grads = lax.psum(gain_grads, AXES)
    gain_grads = lax.dynamic_slice_in_dim(gain_grads, f * (width // n), width // n, 2)

    def home(array):
        ours = lax.dynamic_slice_in_dim(array, x * rows, rows, 0)
        theirs = mate(lax.dynamic_slice_in_dim(array, (1 - x) * rows, rows, 0))
        both = jnp.where(first, jnp.stack([ours, theirs], 1), jnp.stack([theirs, ours], 1))
        return both.reshape(micro, frames, positions, width)

    return home(output), home(grad_in), gain_grads[0], grads[0], grads[1], gain_grads[1], grads[2], grads[3]


def shortened(x):

    def short(part):
        return part.astype(jnp.bfloat16) if part.dtype == jnp.float32 else part

    return jax.tree.map(short, x)


PRECISE = lax.Precision.HIGHEST
matmul, times_transposed, contract_rows = dot, dot_nt, dot_tn


def by_weights(
    block_input,
    out_grad,
    item_lengths,
    frame_offsets,
    norm_attn,
    w_qkv,
    w_out,
    norm_ffn,
    w_gate_up,
    w_down,
):
    micro, frames, positions, model_width = block_input.shape
    head_dim = model_width // HEADS
    hidden_size = w_gate_up.shape[2] // 2
    head_shape = (frames, positions, HEADS, head_dim)
    slot_index = jnp.arange(ITEM_SLOTS)[None, None, :]
    first_slot = frame_offsets[:, :, None]
    valid_rows = (slot_index >= first_slot) & (slot_index < first_slot + item_lengths[:, :, None])
    valid_rows = valid_rows.astype(jnp.float32).reshape(micro, frames)
    causal = jnp.arange(positions)[:, None] >= jnp.arange(positions)[None, :]
    totals = (
        jnp.zeros((positions, model_width), jnp.float32),
        jnp.zeros((positions, model_width, 3 * model_width), jnp.float32),
        jnp.zeros((positions, model_width, model_width), jnp.float32),
        jnp.zeros((positions, model_width), jnp.float32),
        jnp.zeros((positions, model_width, 2 * hidden_size), jnp.float32),
        jnp.zeros((positions, hidden_size, model_width), jnp.float32),
    )
    output_list = []
    input_grad_list = []
    for batch_index in range(micro):
        inputs = block_input[batch_index].astype(jnp.float32)
        qkv_all, gain_in_all = (
            lax.all_gather(w_qkv, "fsdp", axis=1, tiled=True),
            lax.all_gather(norm_attn, "fsdp", axis=1, tiled=True),
        )
        first_saved = []
        qkv_list = []
        for place in range(positions):
            rows = inputs[:, place]
            scale_one = rms_scale(rows)
            normed = (rows * scale_one * gain_in_all[place]).astype(jnp.bfloat16)
            first_saved.append((scale_one, normed))
            qkv_list.append(matmul(normed, qkv_all[place]).astype(jnp.bfloat16))
        qkv_proj = jnp.stack(qkv_list, axis=1)
        query_heads = qkv_proj[..., :model_width].reshape(head_shape)
        key_heads = qkv_proj[..., model_width : 2 * model_width].reshape(head_shape)
        value_heads = qkv_proj[..., 2 * model_width :].reshape(head_shape)
        scores = jnp.einsum(
            "fihd,fjhd->fhij", query_heads, key_heads, preferred_element_type=jnp.float32
        ) / math.sqrt(head_dim)
        scores = jnp.where(causal, scores, -1e30)
        attention = jax.nn.softmax(scores, axis=-1)
        attention_low = attention.astype(jnp.bfloat16)
        mixed_heads = jnp.einsum(
            "fhij,fjhd->fihd", attention_low, value_heads, preferred_element_type=jnp.float32
        )
        mixed_heads = mixed_heads.reshape(frames, positions, model_width).astype(jnp.bfloat16)
        out_all, gain_two_all, gu_all, down_all = (
            lax.all_gather(w_out, "fsdp", axis=1, tiled=True),
            lax.all_gather(norm_ffn, "fsdp", axis=1, tiled=True),
            lax.all_gather(w_gate_up, "fsdp", axis=1, tiled=True),
            lax.all_gather(w_down, "fsdp", axis=1, tiled=True),
        )
        second_saved = []
        output_rows = []
        for place in range(positions):
            middle = inputs[:, place] + matmul(mixed_heads[:, place], out_all[place])
            scale_two = rms_scale(middle)
            normed_two = (middle * scale_two * gain_two_all[place]).astype(jnp.bfloat16)
            gate_up = matmul(normed_two, gu_all[place])
            hidden = (jax.nn.silu(gate_up[:, :hidden_size]) * gate_up[:, hidden_size:]).astype(
                jnp.bfloat16
            )
            second_saved.append((middle, scale_two, normed_two, gate_up, hidden))
            output_rows.append((middle + matmul(hidden, down_all[place])).astype(jnp.bfloat16))
        output_list.append(jnp.stack(output_rows, axis=1))
        upstream = (
            out_grad[batch_index].astype(jnp.float32) * valid_rows[batch_index][:, None, None]
        )
        out_all, gain_two_all, gu_all, down_all = (
            lax.all_gather(w_out, "fsdp", axis=1, tiled=True),
            lax.all_gather(norm_ffn, "fsdp", axis=1, tiled=True),
            lax.all_gather(w_gate_up, "fsdp", axis=1, tiled=True),
            lax.all_gather(w_down, "fsdp", axis=1, tiled=True),
        )
        out_grads = []
        gain_two_grads = []
        gu_grads = []
        down_grads = []
        middle_grads = []
        attn_grads = []
        for place in range(positions):
            middle, scale_two, normed_two, gate_up, hidden = second_saved[place]
            gate = gate_up[:, :hidden_size]
            up_part = gate_up[:, hidden_size:]
            grad_ffn = upstream[:, place].astype(jnp.bfloat16)
            down_grads.append(contract_rows(hidden, grad_ffn))
            grad_hidden = times_transposed(grad_ffn, down_all[place])
            sigma = jax.nn.sigmoid(gate)
            grad_gate = grad_hidden * up_part * sigma * (1.0 + gate * (1.0 - sigma))
            grad_up = grad_hidden * jax.nn.silu(gate)
            grad_gate_up = jnp.concatenate([grad_gate, grad_up], axis=-1).astype(jnp.bfloat16)
            gu_grads.append(contract_rows(normed_two, grad_gate_up))
            grad_normed_two = times_transposed(grad_gate_up, gu_all[place])
            gain_two_grads.append(jnp.sum(grad_normed_two * middle * scale_two, axis=0))
            grad_middle = upstream[:, place] + norm_backward(
                middle, scale_two, gain_two_all[place], grad_normed_two
            )
            grad_branch = grad_middle.astype(jnp.bfloat16)
            out_grads.append(contract_rows(mixed_heads[:, place], grad_branch))
            attn_grads.append(times_transposed(grad_branch, out_all[place]).astype(jnp.bfloat16))
            middle_grads.append(grad_middle)
        grad_mixed = jnp.stack(attn_grads, axis=1).reshape(head_shape)
        grad_attention = jnp.einsum(
            "fihd,fjhd->fhij", grad_mixed, value_heads, preferred_element_type=jnp.float32
        )
        grad_values = jnp.einsum(
            "fhij,fihd->fjhd", attention_low, grad_mixed, preferred_element_type=jnp.float32
        )
        grad_scores = attention * (
            grad_attention - jnp.sum(attention * grad_attention, axis=-1, keepdims=True)
        )
        grad_scores = grad_scores / math.sqrt(head_dim)
        grad_query = jnp.einsum(
            "fhij,fjhd->fihd", grad_scores, key_heads.astype(jnp.float32), precision=PRECISE
        )
        grad_keys = jnp.einsum(
            "fhij,fihd->fjhd", grad_scores, query_heads.astype(jnp.float32), precision=PRECISE
        )
        flat_shape = (frames, positions, model_width)
        grad_qkv = jnp.concatenate(
            [
                grad_query.reshape(flat_shape),
                grad_keys.reshape(flat_shape),
                grad_values.reshape(flat_shape),
            ],
            axis=-1,
        ).astype(jnp.bfloat16)
        qkv_all, gain_in_all = (
            lax.all_gather(w_qkv, "fsdp", axis=1, tiled=True),
            lax.all_gather(norm_attn, "fsdp", axis=1, tiled=True),
        )
        qkv_grads = []
        gain_one_grads = []
        input_rows = []
        for place in range(positions):
            scale_one, normed = first_saved[place]
            rows = inputs[:, place]
            qkv_grads.append(contract_rows(normed, grad_qkv[:, place]))
            grad_normed = times_transposed(grad_qkv[:, place], qkv_all[place])
            gain_one_grads.append(jnp.sum(grad_normed * rows * scale_one, axis=0))
            input_rows.append(
                (
                    middle_grads[place]
                    + norm_backward(rows, scale_one, gain_in_all[place], grad_normed)
                ).astype(jnp.bfloat16)
            )
        input_grad_list.append(jnp.stack(input_rows, axis=1))
        batch_grads = (
            jnp.stack(gain_one_grads),
            jnp.stack(qkv_grads),
            jnp.stack(out_grads),
            jnp.stack(gain_two_grads),
            jnp.stack(gu_grads),
            jnp.stack(down_grads),
        )
        totals = tuple((total + update for total, update in zip(totals, batch_grads)))
    totals = (
        lax.psum_scatter(totals[0], "fsdp", scatter_dimension=1, tiled=True),
        lax.psum_scatter(totals[1], "fsdp", scatter_dimension=1, tiled=True),
        lax.psum_scatter(totals[2], "fsdp", scatter_dimension=1, tiled=True),
        lax.psum_scatter(totals[3], "fsdp", scatter_dimension=1, tiled=True),
        lax.psum_scatter(totals[4], "fsdp", scatter_dimension=1, tiled=True),
        lax.psum_scatter(totals[5], "fsdp", scatter_dimension=1, tiled=True),
    )
    totals = jax.tree.map(lambda part: part.astype(jnp.float32), lax.psum(shortened(totals), "dp"))
    return (
        jnp.stack(output_list),
        jnp.stack(input_grad_list),
        totals[0],
        totals[1],
        totals[2],
        totals[3],
        totals[4],
        totals[5],
    )


def fits(mesh, shapes):
    return mesh.shape["dp"] == 4 and all(s[1] % 16 == 0 for s in shapes)


def solution(mesh):
    n = mesh.shape["fsdp"]

    def on_device(*args):
        if fits(mesh, [args[k].shape for k in (5, 6, 8, 9)]):
            return by_position(n, *args)
        return by_weights(*args)

    placed = (
        P(None, ("dp", "fsdp"), None, None),
        P(None, ("dp", "fsdp"), None, None),
        P(None, ("dp", "fsdp")),
        P(None, ("dp", "fsdp")),
        P(None, "fsdp"),
        P(None, "fsdp", None),
        P(None, "fsdp", None),
        P(None, "fsdp"),
        P(None, "fsdp", None),
        P(None, "fsdp", None),
    )
    return jax.shard_map(
        on_device,
        mesh=mesh,
        in_specs=placed,
        out_specs=(
            P(None, ("dp", "fsdp"), None, None),
            P(None, ("dp", "fsdp"), None, None),
            P(None, "fsdp"),
            P(None, "fsdp", None),
            P(None, "fsdp", None),
            P(None, "fsdp"),
            P(None, "fsdp", None),
            P(None, "fsdp", None),
        ),
        check_vma=False,
    )
```

```python
import functools
import math

import jax
import jax.numpy as jnp
from jax import lax
from jax.experimental import pallas as pl
from jax.experimental.pallas import tpu as pltpu
from jax.sharding import PartitionSpec as P

MESH = pl.DeviceIdType.MESH
BF = jnp.bfloat16
F32 = jnp.float32
HEADS = 16
ITEM_SLOTS = 32
EPSILON = 1e-05
LANES = 3
AXES = ("dp", "fsdp")


def rem(a, b):
    return a % b if isinstance(a, int) else lax.rem(a, b)


def div(a, b):
    return a // b if isinstance(a, int) else lax.div(a, b)


def place(n):
    dp, f = lax.axis_index("dp"), lax.axis_index("fsdp")
    x, c = lax.div(dp, 2), lax.rem(dp, 2)
    z, h = lax.div(f, 2), lax.rem(f, 2)
    r = z * (1 - h) + (n - 1 - z) * h
    return x, c, f, r


def ring_index(r, n):
    hh = lax.div(r, n // 2)
    return (2 * r) * (1 - hh) + (2 * (n - 1 - r) + 1) * hh


class Spot:
    def __init__(self, n):
        self.n = n
        x, c, f, r = place(n)
        self.x, self.c, self.f, self.r = x, c, f, r
        self.d = 1 - 2 * c
        dp = 2 * x + c
        self.next = (dp, ring_index(lax.rem(r + self.d + n, n), n))
        self.prev = (dp, ring_index(lax.rem(r - self.d + n, n), n))
        self.sib = (2 * x + 1 - c, f)
        self.mate = (2 * (1 - x) + c, f)

    def owner(self, hop):
        return ring_index(lax.rem(self.r - self.d * (hop + 1) + self.n, self.n), self.n)

    def greet(self):
        barrier = pltpu.get_barrier_semaphore()
        for who in (self.next, self.prev, self.sib, self.mate):
            pl.semaphore_signal(barrier, inc=1, device_id=who, device_id_type=MESH)
        pl.semaphore_wait(barrier, 4)


def remote(src, dst, send, recv, who):
    return pltpu.make_async_remote_copy(src, dst, send, recv, device_id=who, device_id_type=MESH)


def pieces_of(shapes, parts):
    out = []
    for a, (shape, count) in enumerate(zip(shapes, parts)):
        tiles = shape[0] // 16
        cuts = [16 * (tiles * k // count) for k in range(count + 1)]
        for k in range(count):
            out.append((a, cuts[k], cuts[k + 1] - cuts[k], shape[1] // 2))
    return out


def lanes_of(pieces):
    return [pieces[k::LANES] for k in range(LANES)]


class Weights:
    def __init__(self, spot, lanes, shard_rows, shards, wholes, ring_send, ring_recv, sib_send, sib_recv):
        self.spot, self.lanes, self.shard_rows = spot, lanes, shard_rows
        self.shards, self.wholes = shards, wholes
        self.sems = ring_send, ring_recv, sib_send, sib_recv
        self.hops = spot.n - 1
        self.total = [len(lane) * self.hops for lane in lanes]
        self.events = [(lane, t) for t in range(max(self.total)) for lane in range(len(lanes)) if t < self.total[lane]]
        self.flying, self.sent, self.handed = {}, [], []

    def block(self, piece, owner):
        a, first, rows, cols = piece
        return self.wholes[a].at[pl.ds(owner * self.shard_rows[a] + first, rows), pl.ds(self.spot.c * cols, cols)]

    def send(self, lane, t):
        piece, hop = self.lanes[lane][t // self.hops], t % self.hops
        a, first, rows, cols = piece
        spot = self.spot
        if hop == 0:
            src = self.shards[a].at[spot.x, pl.ds(first, rows), pl.ds(spot.c * cols, cols)]
            dst = self.block(piece, spot.f)
        else:
            src = dst = self.block(piece, spot.owner(hop - 1))
        cp = remote(src, dst, self.sems[0].at[lane, t], self.sems[1].at[lane, t], spot.next)
        cp.start()
        self.flying[lane] = cp

    def start(self):
        for lane in range(len(self.lanes)):
            self.send(lane, 0)

    def tick(self, count):
        for lane, t in self.events[:count]:
            self.flying[lane].wait_recv()
            self.sent.append(self.flying[lane])
            if t + 1 < self.total[lane]:
                self.send(lane, t + 1)
            piece, hop = self.lanes[lane][t // self.hops], t % self.hops
            here = self.block(piece, self.spot.owner(hop))
            cp = remote(here, here, self.sems[2].at[lane, t], self.sems[3].at[lane, t], self.spot.sib)
            cp.start()
            self.handed.append((piece[0], cp))
        self.events = self.events[count:]

    def until(self, array):
        while any(self.lanes[lane][t // self.hops][0] <= array for lane, t in self.events):
            self.tick(1)
        later = []
        for a, cp in self.handed:
            if a <= array:
                cp.wait_recv()
                self.sent.append(cp)
            else:
                later.append((a, cp))
        self.handed = later

    def finish(self):
        for cp in self.sent:
            cp.wait_send()


def dot(left, right):
    return jnp.dot(left, right, preferred_element_type=F32)


def dot_nt(left, right):
    return lax.dot_general(left, right, (((1,), (1,)), ((), ())), preferred_element_type=F32)


def dot_tn(left, right):
    return lax.dot_general(left, right, (((0,), (0,)), ((), ())), preferred_element_type=F32)


def rms_scale(values):
    return lax.rsqrt(jnp.mean(values * values, axis=-1, keepdims=True) + EPSILON)


def norm_backward(values, scale, gain, upstream):
    weighted = gain * upstream
    return scale * weighted - values * scale**3 * jnp.mean(values * weighted, axis=-1, keepdims=True)


def head_table(ref):
    width = ref.shape[0]
    rows = lax.broadcasted_iota(jnp.int32, ref.shape, 0)
    cols = lax.broadcasted_iota(jnp.int32, ref.shape, 1)
    ref[...] = (lax.div(rows, width // HEADS) == cols).astype(F32).astype(BF)


def per_head(product, table):
    high = product.astype(BF)
    rest = (product - high.astype(F32)).astype(BF)
    return dot(high, table[...]) + dot(rest, table[...])


def spread(per, table):
    return dot_nt(per, table[...])


def spread_two(per, table):
    high = per.astype(BF)
    rest = (per - high.astype(F32)).astype(BF)
    return dot_nt(high, table[...]) + dot_nt(rest, table[...])


def pair(a, b):
    top = jnp.maximum(a, b)
    ea, eb = jnp.exp(a - top), jnp.exp(b - top)
    return ea / (ea + eb), eb / (ea + eb)


def flat(scores):
    return scores.T[:HEADS]


def tall(scores):
    return jnp.concatenate([scores, jnp.zeros((128 - HEADS, scores.shape[1]), F32)], axis=0).T


CHUNK = 256


class Refs:
    def __init__(self, names, refs):
        assert len(names) == len(refs)
        self.__dict__.update(zip(names, refs))


def forward_kernel(n, lanes, shard_rows, names, *refs):
    k = Refs(names, refs)
    spot = Spot(n)
    x, c, f = spot.x, spot.c, spot.f
    tokens, width = k.X.shape
    half, chunks = tokens // 2, tokens // CHUNK
    ff = k.HID.shape[1]
    position_one = x == 1
    ring = Weights(
        spot, lanes, shard_rows, (k.wq, k.wo, k.wg, k.wd), (k.Wq, k.Wo, k.Wg, k.Wd),
        k.ring_send, k.ring_recv, k.sib_send, k.sib_recv,
    )

    local = []
    for i, (src, dst) in enumerate((
        (k.xo, k.X.at[pl.ds(x * half, half)]),
        (k.gn, k.GA.at[f]),
        (k.wq.at[x], k.Wq.at[pl.ds(f * shard_rows[0], shard_rows[0])]),
        (k.wo.at[x], k.Wo.at[pl.ds(f * shard_rows[1], shard_rows[1])]),
        (k.wg.at[x], k.Wg.at[pl.ds(f * shard_rows[2], shard_rows[2])]),
        (k.wd.at[x], k.Wd.at[pl.ds(f * shard_rows[3], shard_rows[3])]),
        (k.go, k.GY.at[pl.ds(x * half, half)]),
    )):
        cp = pltpu.make_async_copy(src, dst, k.loc.at[i])
        cp.start()
        local.append(cp)

    others = greet_all(spot)

    gains = []
    for i, who in enumerate(others):
        cp = remote(k.gn, k.GA.at[f], k.gain_send.at[i], k.gain_recv.at[i], who)
        cp.start()
        gains.append(cp)
    ring.start()
    swaps = [
        remote(src, dst.at[pl.ds(x * half, half)], k.swap_send.at[i], k.swap_recv.at[i], spot.mate)
        for i, (src, dst) in enumerate(((k.xs, k.X), (k.gs, k.GY)))
    ]
    swaps[0].start()

    @pl.when(x == 0)
    def _():
        swaps[1].start()

    outs = []

    def put(src, dst):
        cp = pltpu.make_async_copy(src, dst, k.put.at[len(outs)])
        cp.start()
        outs.append(cp)
        return cp

    head_table(k.E)
    k.G[...] = jnp.zeros_like(k.G)
    local[0].wait()
    local[1].wait()
    for cp in gains:
        cp.wait()
    for j in range(n):
        block = k.GA[j].astype(F32)
        for row in range(2):
            k.G[pl.ds(row, 1), pl.ds(j * 128, 128)] = block[row : row + 1]
    put(k.G, k.o_gain)

    def rows_of(j):
        return pl.ds(pl.multiple_of(j * CHUNK, CHUNK), CHUNK)

    def first_norm(at):
        def step(i, carry):
            rows = pl.ds(pl.multiple_of(at * half + i * CHUNK, CHUNK), CHUNK)
            values = k.X[rows].astype(F32)
            k.N1[rows] = (values * rms_scale(values) * k.G[0:1]).astype(BF)
            return carry

        lax.fori_loop(0, half // CHUNK, step, 0)

    ring.tick(4)
    first_norm(x)
    ring.tick(14)
    swaps[0].wait()
    first_norm(1 - x)
    put(k.X, k.o_x)
    put(k.N1, k.o_n1)
    local[2].wait()
    local[3].wait()
    ring.until(1)
    put(k.Wq, k.o_wq)
    put(k.Wo, k.o_wo)

    def project(first, count):
        def step(i, carry):
            cols = pl.ds(pl.multiple_of(first + i * 256, 256), 256)
            k.QKV[:, cols] = dot(k.N1[...], k.Wq[:, cols]).astype(BF)
            return carry

        lax.fori_loop(0, count // 256, step, 0)

    def across(src, j):
        return remote(src, k.CR.at[rows_of(j)], k.cross_send.at[j], k.cross_recv.at[j], spot.mate)

    def across_scores(j):
        return remote(k.SS.at[j], k.SR.at[j], k.score_send.at[j], k.score_recv.at[j], spot.mate)

    def query(j):
        return k.QKV.at[rows_of(j), pl.ds(0, width)]

    scaling = 1.0 / math.sqrt(width // HEADS)

    def own_score(j):
        rows = rows_of(j)
        q, key = k.QKV[rows, 0:width].astype(F32), k.QKV[rows, width : 2 * width].astype(F32)
        score = per_head(q * key, k.E) * scaling
        k.S[rows] = score

        @pl.when(position_one)
        def _():
            k.SS[j] = flat(score)
            across_scores(j).start()
            if j + 1 < chunks:
                across(query(j + 1), j + 1).start()
            else:
                swaps[1].start()

    def serve(j):
        @pl.when(x == 0)
        def _():
            rows = rows_of(j)
            across(query(j), j).wait_recv()
            across_scores(j).wait_recv()
            score = per_head(k.CR[rows].astype(F32) * k.QKV[rows, width : 2 * width].astype(F32), k.E) * scaling
            k.SS[j] = flat(score)
            across_scores(j).start()
            here, there = pair(score, tall(k.SR[j]))
            k.PR[1, rows] = here
            k.PR[2, rows] = there
            part = spread(here.astype(BF), k.E) * k.QKV[rows, 2 * width : 3 * width].astype(F32)
            k.CS[rows] = part.astype(BF)
            across(k.CS.at[rows], j).start()

    mids = {}

    def attend(j):
        rows = rows_of(j)

        @pl.when(position_one)
        def _():
            across(query(j), j).wait_recv()
            across_scores(j).wait_recv()

        other = jnp.where(position_one, tall(k.SR[j]), -1e30)
        here, there = pair(k.S[rows], other)
        k.PR[0, rows] = here
        mixed = spread(here.astype(BF), k.E) * k.QKV[rows, 2 * width : 3 * width].astype(F32)
        mixed = mixed + jnp.where(position_one, k.CR[rows].astype(F32), 0.0)
        k.ATT[rows] = mixed.astype(BF)
        if j - 2 in mids:
            mids[j - 2].wait()
        middle = k.X[rows].astype(F32) + dot(k.ATT[rows], k.Wo[...])
        k.MID[j % 2] = middle
        k.N2[rows] = (middle * rms_scale(middle) * k.G[1:2]).astype(BF)
        cp = pltpu.make_async_copy(k.MID.at[j % 2], k.o_mid.at[rows], k.mid.at[j % 2])
        cp.start()
        mids[j] = cp

    project(0, width // 2)
    ring.tick(1)
    project(width // 2, width // 2)

    @pl.when(position_one)
    def _():
        across(query(0), 0).start()

    ring.tick(2)
    project(width, width // 2)
    ring.tick(1)
    project(width + width // 2, width // 2)
    ring.tick(1)
    for j in range(chunks):
        own_score(j)
        ring.tick(1)
    project(2 * width, width)
    put(k.QKV, k.o_qkv)
    ring.tick(2)

    serve(0)
    ring.tick(4)
    serve(1)
    ring.tick(1)
    attend(0)
    ring.tick(4)
    serve(2)
    ring.tick(1)
    attend(1)
    ring.tick(4)
    local[4].wait()
    ring.until(2)
    put(k.Wg, k.o_wg)
    serve(3)

    def gate_copies(step):
        slot = rem(step, 2)
        for part in range(2):
            yield pltpu.make_async_copy(k.GU.at[slot, part], k.o_gu.at[step, part], k.gu.at[slot, part])

    def feed(h, first, last):
        def step(t, carry):
            rows = pl.ds(h * half, half)
            at = h * (ff // 256) + t
            slot = lax.rem(at, 2)
            gate = dot(k.N2[rows], k.Wg[:, pl.ds(pl.multiple_of(t * 256, 256), 256)])
            up = dot(k.N2[rows], k.Wg[:, pl.ds(pl.multiple_of(ff + t * 256, 256), 256)])
            k.HID[rows, pl.ds(pl.multiple_of(t * 256, 256), 256)] = (gate * jax.nn.sigmoid(gate) * up).astype(BF)

            @pl.when(at >= 2)
            def _():
                for cp in gate_copies(at - 2):
                    cp.wait()

            k.GU[slot, 0] = gate.astype(BF)
            k.GU[slot, 1] = up.astype(BF)
            for cp in gate_copies(at):
                cp.start()
            return carry

        lax.fori_loop(first, last, step, 0)

    tiles = ff // 256
    for t in range(tiles):
        feed(0, t, t + 1)
        ring.tick(1)
        if t == 7:
            attend(2)
            ring.tick(1)
    attend(3)
    put(k.N2, k.o_n2)
    put(k.ATT, k.o_att)
    put(k.PR, k.o_p)
    for t in range(tiles):
        feed(1, t, t + 1)
        ring.tick(1)
    put(k.HID, k.o_hid)
    local[6].wait()
    swaps[1].wait()
    put(k.GY, k.o_gy)

    cols = width // 2

    def down_copies(m):
        slot = rem(m, 4)
        rows = pl.ds(pl.multiple_of(m * 256, 256), 256)
        theirs = remote(
            k.DW.at[slot, :, pl.ds(pl.multiple_of((1 - c) * cols, cols), cols)],
            k.o_sib.at[rows], k.down_send.at[slot], k.down_recv.at[m], spot.sib,
        )
        ours = pltpu.make_async_copy(
            k.DW.at[slot, :, pl.ds(pl.multiple_of(c * cols, cols), cols)], k.o_dwd.at[rows], k.down.at[slot]
        )
        return theirs, ours

    def down_grad(first, last):
        def step(m, carry):
            part = dot_tn(k.HID[:, pl.ds(pl.multiple_of(m * 256, 256), 256)], k.GY[...]).astype(BF)

            @pl.when(m >= 4)
            def _():
                theirs, ours = down_copies(m - 4)
                theirs.wait_send()
                ours.wait()

            k.DW[lax.rem(m, 4)] = part
            for cp in down_copies(m):
                cp.start()
            return carry

        lax.fori_loop(first, last, step, 0)

    for m in range(tiles):
        down_grad(m, m + 1)
        ring.tick(1)
    local[5].wait()
    ring.until(3)
    put(k.Wd, k.o_wd)
    for m in range(tiles - 4, tiles):
        theirs, ours = down_copies(m)
        theirs.wait_send()
        ours.wait()
    for m in range(tiles):
        down_copies(m)[0].wait_recv()
    put(k.CR, k.o_cr)
    for at in (2 * tiles - 2, 2 * tiles - 1):
        for cp in gate_copies(at):
            cp.wait()
    for j in (chunks - 2, chunks - 1):
        mids[j].wait()
    for j in range(chunks):
        across(query(j), j).wait_send()
        across_scores(j).wait_send()
    ring.finish()
    for cp in outs:
        cp.wait()


def forward(n, xs, xo, gs, go, wq, wo, wg, wd, gn):
    weights = (wq, wo, wg, wd)
    shapes = [w.shape[1:] for w in weights]
    parts = [
        [p for p in pieces_of(shapes, (4, 1, 4, 4)) if p[0] == a] for a in range(4)
    ]
    lanes = [[parts[0][i], parts[2][i], parts[3][i]] for i in range(4)] + [parts[1]]
    steps = 3 * (n - 1)
    half, width = xo.shape
    tokens, ff = 2 * half, wd.shape[1] * n
    tiles, chunks = ff // 256, tokens // CHUNK
    wholes = [(s[0] * n, s[1]) for s in shapes]
    square = (tokens, width)
    out = dict(
        o_wq=(wholes[0], BF), o_wo=(wholes[1], BF), o_wg=(wholes[2], BF), o_wd=(wholes[3], BF),
        o_x=(square, BF), o_gy=(square, BF), o_n1=(square, BF), o_qkv=((tokens, 3 * width), BF),
        o_cr=(square, BF), o_p=((3, tokens, 128), F32), o_att=(square, BF), o_mid=(square, F32),
        o_n2=(square, BF), o_gu=((2 * tiles, 2, half, 256), BF), o_hid=((tokens, ff), BF),
        o_dwd=((ff, width // 2), BF), o_sib=((ff, width // 2), BF), o_gain=((8, width), F32),
    )
    vmem = dict(
        Wq=(wholes[0], BF), Wo=(wholes[1], BF), Wg=(wholes[2], BF), Wd=(wholes[3], BF),
        X=(square, BF), GY=(square, BF), N1=(square, BF), QKV=((tokens, 3 * width), BF),
        CR=(square, BF), CS=(square, BF), ATT=(square, BF), MID=((2, CHUNK, width), F32),
        N2=(square, BF), GU=((2, 2, half, 256), BF), HID=((tokens, ff), BF), DW=((4, 256, width), BF),
        E=((width, 128), BF), G=((8, width), F32), GA=((n, 16, 128), BF), S=((tokens, 128), F32),
        SS=((chunks, HEADS, CHUNK), F32), SR=((chunks, HEADS, CHUNK), F32), PR=((3, tokens, 128), F32),
    )
    sems = dict(
        ring_send=(len(lanes), steps), ring_recv=(len(lanes), steps), sib_send=(len(lanes), steps),
        sib_recv=(len(lanes), steps), loc=(7,), gain_send=(n - 1,), gain_recv=(n - 1,),
        swap_send=(2,), swap_recv=(2,), put=(20,), cross_send=(chunks,), cross_recv=(chunks,),
        score_send=(chunks,), score_recv=(chunks,), mid=(2,), gu=(2, 2), down_send=(4,),
        down_recv=(tiles,), down=(4,),
    )
    ins = dict(xs=xs, xo=xo, gs=gs, go=go, wq=wq, wo=wo, wg=wg, wd=wd, gn=gn)
    return call(forward_kernel, (n, lanes, [s[0] for s in shapes]), ins, out, vmem, sems, 0)


class Sums:
    def __init__(self, spot, lanes, shard_rows, half_cols, ours, theirs, outs, landing, k):
        self.spot, self.lanes, self.shard_rows, self.half_cols = spot, lanes, shard_rows, half_cols
        self.ours, self.theirs, self.outs, self.landing, self.k = ours, theirs, outs, landing, k
        self.hops = spot.n - 1
        self.ready = set()
        self.loaded = [0] * len(lanes)
        self.used = [0] * len(lanes)
        self.flying = [None] * len(lanes)
        self.at = [0] * len(lanes)
        self.first = [None] * len(lanes)
        self.queue, self.sent, self.tail, self.mates = [], [], [], []
        self.count = 0

    def term_copies(self, lane, u):
        piece = self.lanes[lane][u // (self.hops + 1)]
        a, row, rows, col, cols = piece
        owner = self.spot.owner(u % (self.hops + 1))
        at = (pl.ds(owner * self.shard_rows[a] + row, rows), pl.ds(col, cols))
        for side, ref in enumerate((self.ours[a], self.theirs[a])):
            dst = self.k.TERM.at[lane, u % 2, side, pl.ds(0, rows), pl.ds(0, cols)]
            yield pltpu.make_async_copy(ref.at[at], dst, self.k.term.at[lane, u % 2, side])

    def prefetch(self, lane):
        per = self.hops + 1
        while self.loaded[lane] < min(self.used[lane] + 2, per * len(self.lanes[lane])):
            u = self.loaded[lane]
            if self.lanes[lane][u // per] not in self.ready:
                return
            for cp in self.term_copies(lane, u):
                cp.start()
            self.loaded[lane] += 1

    def term(self, lane):
        u = self.used[lane]
        assert u < self.loaded[lane]
        _, _, rows, _, cols = self.lanes[lane][u // (self.hops + 1)]
        for cp in self.term_copies(lane, u):
            cp.wait()
        ours, theirs = (self.k.TERM[lane, u % 2, side, 0:rows, 0:cols].astype(F32) for side in range(2))
        return ours + theirs

    def step(self, lane):
        t = self.at[lane]
        if t == self.hops * len(self.lanes[lane]):
            return
        piece = self.lanes[lane][t // self.hops]
        if piece not in self.ready:
            self.flying[lane] = None
            return
        hop = t % self.hops
        slots = self.landing[piece]
        value = self.term(lane)
        if hop == 0:
            if self.first[lane] is not None:
                self.first[lane].wait_send()
            buf = self.k.FIRST.at[lane, pl.ds(0, piece[2]), pl.ds(0, piece[4])]
        else:
            buf = slots.at[hop - 1]
            value = value + buf[...].astype(F32)
        buf[...] = value.astype(BF)
        self.used[lane] += 1
        cp = remote(buf, slots.at[hop], self.k.ring_send.at[lane, t], self.k.ring_recv.at[lane, t], self.spot.next)
        cp.start()
        self.prefetch(lane)
        if hop == 0:
            self.first[lane] = cp
        else:
            self.sent.append(cp)
        self.flying[lane] = cp
        self.at[lane] += 1
        self.queue.append(lane)

    def offer(self, pieces):
        self.ready.update(pieces)
        for lane in range(len(self.lanes)):
            if self.flying[lane] is None and self.at[lane] < self.hops * len(self.lanes[lane]):
                self.prefetch(lane)
                self.step(lane)
            else:
                self.prefetch(lane)

    def finish_piece(self, lane, piece):
        a, row, rows, col, cols = piece
        spot, k, i = self.spot, self.k, self.count
        self.count += 1
        end = self.landing[piece].at[self.hops - 1]
        end[...] = (end[...].astype(F32) + self.term(lane)).astype(BF)
        self.used[lane] += 1
        self.prefetch(lane)
        at = (pl.ds(row, rows), pl.ds(spot.c * self.half_cols[a] + col, cols))
        place = self.outs[a].at[(spot.x,) + at]
        cp = pltpu.make_async_copy(end, place, k.end.at[i])
        cp.start()
        self.tail.append(cp)
        cp = remote(end, place, k.end_sib_send.at[i], k.end_sib_recv.at[i], spot.sib)
        cp.start()
        self.tail.append(cp)
        cp = remote(end, place, k.end_mate_send.at[i], k.end_mate_recv.at[i], spot.mate)
        cp.start()
        self.mates.append((cp, self.outs[a].at[(1 - spot.x,) + at], i))

    def pass_on(self, keep):
        while len(self.mates) > keep:
            cp, place, i = self.mates.pop(0)
            cp.wait()
            far = remote(place, place, self.k.far_send.at[i], self.k.far_recv.at[i], self.spot.sib)
            far.start()
            self.tail.append(far)

    def tick(self, count, least=3):
        for _ in range(count):
            if len(self.queue) < least:
                return
            lane = self.queue.pop(0)
            self.flying[lane].wait_recv()
            t = self.at[lane]
            if t % self.hops == 0:
                self.finish_piece(lane, self.lanes[lane][t // self.hops - 1])
            self.step(lane)

    def finish(self):
        while self.queue:
            self.tick(1, 1)
        self.pass_on(0)
        for cp in self.tail:
            cp.wait()
        for cp in self.sent + [cp for cp in self.first if cp is not None]:
            cp.wait_send()


def sum_scratch(n, lanes, most):
    count = sum(len(lane) for lane in lanes)
    steps = max(len(lane) for lane in lanes) * (n - 1)
    vmem = dict(TERM=((len(lanes), 2, 2) + most, BF), FIRST=((len(lanes),) + most, BF))
    sems = dict(
        term=(len(lanes), 2, 2), ring_send=(len(lanes), steps), ring_recv=(len(lanes), steps), end=(count,),
        end_sib_send=(count,), end_sib_recv=(count,), end_mate_send=(count,), end_mate_recv=(count,), far_send=(count,),
        far_recv=(count,),
    )
    landing = {p: ("L%d_%d" % (p[0], p[1] + p[3]), ((n - 1,) + (p[2], p[4]), BF)) for lane in lanes for p in lane}
    vmem.update(landing.values())
    return vmem, sems, {p: name for p, (name, _) in landing.items()}


def tokens_at(j):
    return pl.ds(pl.multiple_of(j * CHUNK, CHUNK), CHUNK)


class Exchange:
    def __init__(self, spot, k):
        self.spot, self.k = spot, k

    def rows(self, src, j):
        k = self.k
        return remote(src, k.CR.at[tokens_at(j)], k.cross_send.at[j], k.cross_recv.at[j], self.spot.mate)

    def numbers(self, j):
        k = self.k
        return remote(k.SS.at[j], k.SR.at[j], k.score_send.at[j], k.score_recv.at[j], self.spot.mate)

    def send(self, src, numbers, j):
        self.k.SS[j] = flat(numbers)
        self.numbers(j).start()
        self.rows(src, j).start()

    def wait_recv(self, src, j):
        self.numbers(j).wait_recv()
        self.rows(src, j).wait_recv()

    def wait_send(self, src, j):
        self.numbers(j).wait_send()
        self.rows(src, j).wait_send()


def greet(spot):
    barrier = pltpu.get_barrier_semaphore()
    for who in (spot.next, spot.prev, spot.sib, spot.mate):
        pl.semaphore_signal(barrier, inc=1, device_id=who, device_id_type=MESH)
    pl.semaphore_wait(barrier, 4)


def greet_all(spot):
    barrier = pltpu.get_barrier_semaphore()
    others = [(2 * spot.x + spot.c, lax.rem(spot.f + i, spot.n)) for i in range(1, spot.n)]
    for who in [spot.sib, spot.mate] + others:
        pl.semaphore_signal(barrier, inc=1, device_id=who, device_id_type=MESH)
    pl.semaphore_wait(barrier, spot.n + 1)
    return others


class Products:
    def __init__(self, spot, k, tiles):
        self.spot, self.k, self.tiles = spot, k, tiles
        self.busy = {}
        self.next = 0

    def tile(self, value, ref, at, index, away):
        k = self.k
        slot = self.next % k.DW.shape[0]
        self.next += 1
        if slot in self.busy:
            cp, was_away = self.busy.pop(slot)
            cp.wait_send() if was_away else cp.wait()
        buf = k.DW.at[slot, pl.ds(0, value.shape[0]), pl.ds(0, value.shape[1])]
        buf[...] = value.astype(BF)
        if away:
            cp = remote(buf, ref.at[at], k.dw.at[slot], k.dw_recv.at[index], self.spot.sib)
        else:
            cp = pltpu.make_async_copy(buf, ref.at[at], k.dw.at[slot])
        cp.start()
        self.busy[slot] = (cp, away)
        return cp

    def grid(self, left, right, first, cols, half_cols, step, ours, theirs, index, tick):
        c = self.spot.c
        waits = []
        for away in (True, False):
            side = (1 - c) if away else c
            for m in range(left.shape[1] // step):
                at_right = pl.ds(pl.multiple_of(side * half_cols + first, 256), cols)
                value = dot_tn(left[:, pl.ds(m * step, step)], right[:, at_right])
                at = (pl.ds(m * step, step), pl.ds(first, cols))
                cp = self.tile(value, theirs if away else ours, at, index + m, away)
                if away:
                    waits.append(cp)
                tick()
        return waits

    def settle(self):
        for cp, away in self.busy.values():
            cp.wait_send() if away else cp.wait()
        self.busy = {}


def backward_kernel(n, lanes, shard_rows, groups, landing, names, *refs):
    k = Refs(names, refs)
    spot = Spot(n)
    x, c = spot.x, spot.c
    tokens, width = k.GA.shape
    half, chunks = tokens // 2, tokens // CHUNK
    ff = k.GG.shape[1] // 2
    tiles = ff // 256
    scaling = 1.0 / math.sqrt(width // HEADS)
    loads = {}

    def load(name, src, dst, sem):
        cp = pltpu.make_async_copy(src, dst, sem)
        cp.start()
        loads[name] = cp

    def load_tile(t):
        slot = t % 2
        load(("wd", t), k.wd.at[pl.ds(t * 256, 256)], k.WT.at[slot], k.tile.at[slot, 0])
        for h in range(2):
            load(("gu", t, h), k.gu.at[h * tiles + t], k.GT.at[slot, h], k.tile.at[slot, 1 + h])

    load("gy", k.gy, k.GY, k.load.at[0])
    load_tile(0)
    load_tile(1)
    load("n2", k.n2, k.N2, k.load.at[1])
    load("gain", k.gain, k.G, k.load.at[2])
    load("p", k.p, k.P, k.load.at[3])
    load("wo", k.wo, k.Wo, k.load.at[4])
    head_table(k.E)
    k.GS[...] = jnp.zeros_like(k.GS)
    greet(spot)

    ring = Sums(
        spot, lanes, shard_rows, (width // 2, ff), (k.dwd, k.o_own), (k.sib, k.o_sib), (k.o_rwd, k.o_rwg),
        {p: getattr(k, name) for p, name in landing.items()}, k,
    )
    ring.offer([lane[0] for lane in lanes])
    swap = Exchange(spot, k)

    loads["gy"].wait()
    for t in range(tiles):
        slot = t % 2
        loads["wd", t].wait()
        for h in range(2):
            loads["gu", t, h].wait()
            rows = pl.ds(h * half, half)
            grad = dot_nt(k.GY[rows], k.WT[slot])
            gate, up = k.GT[slot, h, 0].astype(F32), k.GT[slot, h, 1].astype(F32)
            sigma = jax.nn.sigmoid(gate)
            k.GG[rows, pl.ds(t * 256, 256)] = (grad * up * sigma * (1.0 + gate * (1.0 - sigma))).astype(BF)
            k.GG[rows, pl.ds(ff + t * 256, 256)] = (grad * gate * sigma).astype(BF)
            if h:
                ring.tick(1)
        if t + 2 < tiles:
            load_tile(t + 2)
        if t == 2:
            load("wg", k.wg, k.Wg, k.load.at[5])

    products = Products(spot, k, None)
    made = []

    def weight_group(g):
        first, cols = groups[g]
        made.append((g, products.grid(
            k.N2, k.GG, first, cols, ff, 512, k.o_own, k.o_sib, 2 * g, lambda: ring.tick(1)
        )))

    def offer_groups():
        if made:
            products.settle()
        while made:
            g, waits = made.pop(0)
            for cp in waits:
                cp.wait_recv()
            ring.offer([lanes[g][1]])

    def load_rows(j):
        load(("mid", j), k.mid.at[tokens_at(j)], k.MID, k.load.at[6])
        load(("v", j), k.qkv.at[tokens_at(j), pl.ds(2 * width, width)], k.V, k.load.at[7])

    load_rows(0)
    loads["gain"].wait()
    loads["wg"].wait()
    loads["wo"].wait()
    outs = {}

    def norm_chunk(j):
        rows = tokens_at(j)
        for m in range(4):
            part = pl.ds(m * 256, 256)
            k.GN[:, part] = dot_nt(k.GG[rows], k.Wg[part])
            if m % 2:
                ring.tick(1)
            if m == 0:
                offer_groups()
        for name in ("mid", "v"):
            loads[name, j].wait()
        middle, upstream = k.MID[...], k.GN[...]
        scale = rms_scale(middle)
        k.GS[0:1] += jnp.sum(upstream * middle * scale, axis=0, keepdims=True)
        grad = k.GY[rows].astype(F32) + norm_backward(middle, scale, k.G[1:2], upstream)
        if j:
            for cp in outs[j - 1]:
                cp.wait()
        k.GM[...] = grad
        k.GB[...] = grad.astype(BF)
        outs[j] = [
            pltpu.make_async_copy(k.GM, k.o_gm.at[rows], k.put.at[0]),
            pltpu.make_async_copy(k.GB, k.o_gb.at[rows], k.put.at[1]),
        ]
        for cp in outs[j]:
            cp.start()
        k.GA[rows] = dot_nt(k.GB[...], k.Wo[...]).astype(BF)
        numbers = per_head(k.GA[rows].astype(F32) * k.V[...].astype(F32), k.E)
        k.GP[rows] = numbers
        if j + 1 < chunks:
            load_rows(j + 1)

        @pl.when(x == 1)
        def _():
            swap.send(k.GA.at[rows], numbers, j)

        ring.tick(1)

    loads["n2"].wait()
    for g in range(4):
        weight_group(g)
        if g: offer_groups()
    for j in range(chunks):
        norm_chunk(j)
    loads["p"].wait()

    for j in range(chunks):
        rows = tokens_at(j)
        load(("qkv", j), k.qkv.at[rows], k.Wg.at[rows, pl.ds(0, 3 * width)], k.again.at[0, j])
        load(("cr", j), k.cr.at[rows], k.Wg.at[rows, pl.ds(3 * width, width)], k.again.at[1, j])

    def parts(rows):
        return (k.Wg[rows, i * width : (i + 1) * width].astype(F32) for i in range(3))

    def store(rows, j, *grads):
        for i, grad in enumerate(grads):
            k.Wg[rows, i * width : (i + 1) * width] = grad.astype(BF)
        pltpu.make_async_copy(k.Wg.at[rows, pl.ds(0, 3 * width)], k.o_gqkv.at[rows], k.back.at[j]).start()

    def serve(j):
        rows = tokens_at(j)

        @pl.when(x == 0)
        def _():
            swap.wait_recv(k.GA.at[rows], j)
            query, key, value = parts(rows)
            there = k.CR[rows].astype(F32)
            prob, prob_c, prob_d = k.P[0, rows], k.P[1, rows], k.P[2, rows]
            grad_c = per_head(there * value, k.E)
            total_c = prob_c * grad_c + prob_d * tall(k.SR[j])
            score_c = spread_two(prob_c * (grad_c - total_c) * scaling, k.E)
            k.CS[rows] = (score_c * key).astype(BF)
            swap.send(k.CS.at[rows], total_c, j)
            grad = k.GP[rows]
            score = spread_two(prob * (grad - prob * grad) * scaling, k.E)
            ours = k.GA[rows].astype(F32)
            store(
                rows, j, score * key, score * query + score_c * k.Wg[rows, 3 * width : 4 * width].astype(F32),
                spread(prob.astype(BF), k.E) * ours + spread(prob_c.astype(BF), k.E) * there,
            )

    def close(j):
        rows = tokens_at(j)

        @pl.when(x == 1)
        def _():
            swap.wait_recv(k.GA.at[rows], j)
            query, key, value = parts(rows)
            prob = k.P[0, rows]
            score = spread_two(prob * (k.GP[rows] - tall(k.SR[j])) * scaling, k.E)
            store(
                rows, j, score * key + k.CR[rows].astype(F32), score * query,
                spread(prob.astype(BF), k.E) * k.GA[rows].astype(F32),
            )

    for j in range(chunks):
        loads["qkv", j].wait()
        loads["cr", j].wait()
        serve(j)
        if j:
            close(j - 1)
        offer_groups()
        ring.tick(4)
    close(chunks - 1)
    while ring.queue:
        ring.tick(1, 1)
    ring.finish()
    for cp in outs[chunks - 1]:
        cp.wait()
    cp = pltpu.make_async_copy(k.GS, k.o_gain, k.load.at[0])
    cp.start()
    cp.wait()
    for j in range(chunks):
        rows = tokens_at(j)
        swap.wait_send(k.GA.at[rows], j)
        pltpu.make_async_copy(k.Wg.at[rows, pl.ds(0, 3 * width)], k.o_gqkv.at[rows], k.back.at[j]).wait()


def backward(n, fw):
    tokens, width = fw.o_x.shape
    ff = fw.o_hid.shape[1]
    chunks = tokens // CHUNK
    shard_rows = (ff // n, width // n)
    cuts = [256 * ((ff // 256 * i + 3) // 4) for i in range(5)]
    groups = [(cuts[i], cuts[i + 1] - cuts[i]) for i in range(4)]
    down = [p for p in pieces_of([(shard_rows[0], width)], (4,))]
    lanes = [
        [(0, down[i][1], down[i][2], 0, width // 2), (1, 0, shard_rows[1], groups[i][0], groups[i][1])] for i in range(4)
    ]
    most = (max(p[2] for lane in lanes for p in lane), max(p[4] for lane in lanes for p in lane))
    ring_vmem, ring_sems, landing = sum_scratch(n, lanes, most)
    square = (tokens, width)
    ins = dict(
        gy=fw.o_gy, n2=fw.o_n2, gu=fw.o_gu, wd=fw.o_wd, wg=fw.o_wg, wo=fw.o_wo, mid=fw.o_mid,
        qkv=fw.o_qkv, p=fw.o_p, cr=fw.o_cr, dwd=fw.o_dwd, sib=fw.o_sib, gain=fw.o_gain,
    )
    out = dict(
        o_gb=(square, BF), o_gm=(square, F32), o_gqkv=((tokens, 3 * width), BF), o_gain=((8, width), F32),
        o_own=((width, ff), BF), o_sib=((width, ff), BF), o_rwd=((2, shard_rows[0], width), BF),
        o_rwg=((2, shard_rows[1], 2 * ff), BF),
    )
    vmem = dict(
        GY=(square, BF), N2=(square, BF), GG=((tokens, 2 * ff), BF), Wg=((width, 2 * ff), BF),
        Wo=((width, width), BF), WT=((2, 256, width), BF), GT=((2, 2, 2, tokens // 2, 256), BF),
        DW=((3, 512, max(g[1] for g in groups)), BF), GN=((CHUNK, width), F32), MID=((CHUNK, width), F32),
        V=((CHUNK, width), BF), GM=((CHUNK, width), F32), GB=((CHUNK, width), BF), GA=(square, BF),
        CR=(square, BF), CS=(square, BF), P=((3, tokens, 128), F32), GP=((tokens, 128), F32),
        SS=((chunks, HEADS, CHUNK), F32), SR=((chunks, HEADS, CHUNK), F32), E=((width, 128), BF),
        G=((8, width), F32), GS=((8, width), F32), **ring_vmem,
    )
    sems = dict(
        tile=(2, 3), load=(8,), put=(2,), dw=(3,), dw_recv=(8,), again=(2, chunks), back=(chunks,),
        cross_send=(chunks,), cross_recv=(chunks,), score_send=(chunks,), score_recv=(chunks,), **ring_sems,
    )
    return call(backward_kernel, (n, lanes, shard_rows, groups, landing), ins, out, vmem, sems, 1)


def call(kernel, static, ins, out, vmem, sems, number):
    hbm = pl.BlockSpec(memory_space=pltpu.HBM)
    dma = pltpu.SemaphoreType.DMA
    names = list(ins) + list(out) + list(vmem) + list(sems)
    outs = pl.pallas_call(
        functools.partial(kernel, *static, names),
        out_shape=[jax.ShapeDtypeStruct(*o) for o in out.values()],
        in_specs=[hbm] * len(ins),
        out_specs=[hbm] * len(out),
        scratch_shapes=[pltpu.VMEM(*v) for v in vmem.values()] + [dma(v) for v in sems.values()],
        compiler_params=pltpu.CompilerParams(
            collective_id=number, has_side_effects=True, vmem_limit_bytes=64 * 2**20 - 2**16
        ),
        name=kernel.__name__,
    )(*ins.values())
    return Refs(list(out), outs)


def closing_kernel(n, lanes, shard_rows, landing, names, *refs):
    k = Refs(names, refs)
    spot = Spot(n)
    x, c = spot.x, spot.c
    tokens, width = k.N1.shape
    half, chunks = tokens // 2, tokens // CHUNK
    ff = k.HID.shape[1]
    loads = {}
    for i, (name, src, dst) in enumerate((
        ("att", k.att, k.ATT), ("gb", k.gb, k.GB), ("hid", k.hid, k.HID), ("wd", k.wd, k.Wd), ("n1", k.n1, k.N1),
        ("gqkv", k.gqkv, k.GQ), ("gain", k.gain, k.G), ("wq", k.wq, k.Wq), ("x", k.x, k.X), ("gs", k.gf, k.GF),
    )):
        loads[name] = pltpu.make_async_copy(src, dst, k.load.at[i])
        loads[name].start()
    k.GS[...] = jnp.zeros_like(k.GS)
    others = greet_all(spot)
    ring = Sums(
        spot, lanes, shard_rows, (width // 2, 3 * width // 2), (k.o_own, k.q_own), (k.o_sib, k.q_sib), (k.o_rwo, k.o_rwq),
        {p: getattr(k, name) for p, name in landing.items()}, k,
    )

    sends = []

    def row_chunk(i):
        j = i % (chunks // 2)
        block = (1 - x) if i < chunks // 2 else x
        return pl.ds(pl.multiple_of(block * half + j * CHUNK, CHUNK), CHUNK), pl.ds(j * CHUNK, CHUNK)

    def deliver(buf, whole, i, first):
        _, at = row_chunk(i)
        if i < chunks // 2:
            cp = remote(buf, whole.at[x, at], k.far_rows_send.at[first + i], k.far_rows_recv.at[first + i], spot.mate)
        else:
            cp = pltpu.make_async_copy(buf, whole.at[x, at], k.near_rows.at[first + i])
        cp.start()
        sends.append(cp)

    mids = {}

    def load_mid(i):
        rows, _ = row_chunk(i)
        mids[i] = pltpu.make_async_copy(k.mid.at[rows], k.MID.at[i % 2], k.rows.at[i % 2, 1])
        mids[i].start()

    grads_in = {}

    def load_grad(i):
        rows, _ = row_chunk(i)
        grads_in[i] = pltpu.make_async_copy(k.gm.at[rows], k.GM.at[i % 2], k.rows.at[i % 2, 0])
        grads_in[i].start()

    def output_chunk(i):
        rows, _ = row_chunk(i)
        for m in range(2):
            part = pl.ds(m * 512, 512)
            k.GN[:, part] = dot(k.HID[rows], k.Wd[:, part])
            ring.tick(1)
        mids[i].wait()
        k.OUT[i] = (k.MID[i % 2] + k.GN[...]).astype(BF)
        deliver(k.OUT.at[i], k.o_out, i, chunks)
        if i + 2 < chunks:
            load_mid(i + 2)

    def input_chunk(i):
        rows, _ = row_chunk(i)
        for m in range(4):
            part = pl.ds(m * 256, 256)
            k.GN[:, part] = dot_nt(k.GQ[rows], k.Wq[part])
            if m % 2:
                ring.tick(1)
        values, upstream = k.X[rows].astype(F32), k.GN[...]
        scale = rms_scale(values)
        k.GS[0:1] += jnp.sum(upstream * values * scale, axis=0, keepdims=True)
        grads_in[i].wait()
        k.IN[i] = (k.GM[i % 2] + norm_backward(values, scale, k.G[0:1], upstream)).astype(BF)
        deliver(k.IN.at[i], k.o_in, i, 0)
        ring.tick(1)
        if i + 2 < chunks:
            load_grad(i + 2)

    load_mid(0)
    load_mid(1)
    load_grad(0)
    load_grad(1)
    products = Products(spot, k, None)
    loads["att"].wait()
    loads["gb"].wait()
    waits = products.grid(k.ATT, k.GB, 0, width // 2, width // 2, 512, k.o_own, k.o_sib, 0, lambda: None)
    loads["hid"].wait()
    loads["wd"].wait()
    output_chunk(0)
    output_chunk(1)
    loads["n1"].wait()
    loads["gqkv"].wait()
    products.settle()
    for cp in waits:
        cp.wait_recv()
    ring.offer([p for lane in lanes for p in lane if p[0] == 0])
    queue = []
    cols = 3 * width // 4
    for g in range(2):
        waits = products.grid(
            k.N1, k.GQ, g * cols, cols, 2 * cols, 512, k.q_own, k.q_sib, 2 + 2 * g, lambda: ring.tick(1)
        )
        queue.append((waits, [p for lane in lanes for p in lane if p[0] == 1 and p[3] // cols == g]))
    products.settle()
    for waits, pieces in queue:
        for cp in waits:
            cp.wait_recv()
        ring.offer(pieces)

    loads["gain"].wait()
    loads["wq"].wait()
    loads["x"].wait()
    for i in range(chunks):
        input_chunk(i)
    for i in range(chunks // 2, chunks):
        output_chunk(i)
        ring.tick(2)
    part = width // n
    loads["gs"].wait()
    for j in range(n):
        k.GP[j] = jnp.zeros_like(k.GP[j])
        for row, ref in enumerate((k.GS, k.GF)):
            k.GP[j, pl.ds(row, 1)] = ref[0:1, j * part : (j + 1) * part]
    gains = []
    for i, who in enumerate(others):
        to = who[1]
        cp = remote(k.GP.at[to], k.GR.at[i], k.gain_send.at[i], k.gain_recv.at[i], who)
        cp.start()
        gains.append(cp)
    ring.tick(2)
    total = k.GP[spot.f]
    for i, cp in enumerate(gains):
        cp.wait()
        total = total + k.GR[i]
    k.GT[0] = total
    cp = remote(k.GT.at[0], k.GT.at[1], k.gain_send.at[n - 1], k.gain_recv.at[n - 1], spot.sib)
    cp.start()
    ring.tick(2)
    cp.wait()
    k.GT[2] = jnp.where(c == 0, k.GT[0], k.GT[1]) + jnp.where(c == 0, k.GT[1], k.GT[0])
    cp = remote(k.GT.at[2], k.o_gain.at[x], k.gain_send.at[n], k.gain_recv.at[n], spot.mate)
    cp.start()
    near = pltpu.make_async_copy(k.GT.at[2], k.o_gain.at[x], k.rows.at[0, 0])
    near.start()
    ring.finish()
    cp.wait()
    near.wait()
    for cp in sends:
        cp.wait()


def closing(n, fw, bw):
    tokens, width = fw.o_x.shape
    ff = fw.o_hid.shape[1]
    chunks = tokens // CHUNK
    shard_rows = (width // n, width // n)
    cols = 3 * width // 8
    lanes = [[(1, 0, shard_rows[1], i * cols, cols)] for i in range(4)] + [
        [(0, 0, shard_rows[0], i * width // 4, width // 4)] for i in range(2)
    ]
    most = (max(p[2] for lane in lanes for p in lane), max(p[4] for lane in lanes for p in lane))
    ring_vmem, ring_sems, landing = sum_scratch(n, lanes, most)
    square = (tokens, width)
    ins = dict(
        att=fw.o_att, gb=bw.o_gb, n1=fw.o_n1, gqkv=bw.o_gqkv, gain=fw.o_gain, wq=fw.o_wq, x=fw.o_x,
        hid=fw.o_hid, wd=fw.o_wd, gm=bw.o_gm, mid=fw.o_mid, gf=bw.o_gain,
    )
    out = dict(
        o_own=((width, width // 2), BF), o_sib=((width, width // 2), BF), q_own=((width, 3 * width // 2), BF),
        q_sib=((width, 3 * width // 2), BF), o_rwo=((2, shard_rows[0], width), BF),
        o_rwq=((2, shard_rows[1], 3 * width), BF), o_in=((2, tokens // 2, width), BF),
        o_out=((2, tokens // 2, width), BF), o_gain=((2, 8, width // n), F32),
    )
    vmem = dict(
        ATT=(square, BF), GB=(square, BF), N1=(square, BF), GQ=((tokens, 3 * width), BF), G=((8, width), F32),
        GS=((8, width), F32), GF=((8, width), F32), GP=((n, 8, width // n), F32), GR=((n - 1, 8, width // n), F32),
        GT=((3, 8, width // n), F32), Wq=((width, 3 * width), BF), X=(square, BF), HID=((tokens, ff), BF),
        Wd=((ff, width), BF), GN=((CHUNK, width), F32), GM=((2, CHUNK, width), F32), MID=((2, CHUNK, width), F32),
        IN=((chunks, CHUNK, width), BF), OUT=((chunks, CHUNK, width), BF), DW=((4, 512, 3 * width // 4), BF),
        **ring_vmem,
    )
    sems = dict(
        load=(10,), gain_send=(n + 1,), gain_recv=(n + 1,), rows=(2, 2), far_rows_send=(2 * chunks,), far_rows_recv=(2 * chunks,),
        near_rows=(2 * chunks,), dw=(4,), dw_recv=(6,), **ring_sems,
    )
    return call(closing_kernel, (n, lanes, shard_rows, landing), ins, out, vmem, sems, 2)


def valid_rows(item_lengths, frame_offsets):
    slot = jnp.arange(ITEM_SLOTS)[None, None, :]
    first = frame_offsets[:, :, None]
    valid = (slot >= first) & (slot < first + item_lengths[:, :, None])
    return valid.reshape(-1)


def by_position(n, block_input, out_grad, item_lengths, frame_offsets, norm_attn, w_qkv, w_out, norm_ffn, w_gate_up, w_down):
    x, c, f, r = place(n)
    micro, frames, positions, width = block_input.shape
    rows = micro * frames
    valid = valid_rows(item_lengths, frame_offsets)[:, None]
    inputs = block_input.reshape(rows, positions, width)
    upstream = jnp.where(valid[..., None], out_grad.reshape(rows, positions, width), 0)

    def take(array, at):
        return lax.dynamic_index_in_dim(array, at, 1, keepdims=False)

    gn = jnp.stack([norm_attn, norm_ffn], axis=1)
    gn = jnp.pad(lax.dynamic_index_in_dim(gn, x, 0, keepdims=False), ((0, 14), (0, 0)))
    fw = forward(
        n, take(inputs, 1 - x), take(inputs, x), take(upstream, 1 - x), take(upstream, x), w_qkv, w_out, w_gate_up, w_down, gn
    )
    bw = backward(n, fw)
    cl = closing(n, fw, bw)
    grads = [g.astype(F32) for g in (cl.o_rwq, cl.o_rwo, bw.o_rwg, bw.o_rwd)]
    def home(array):
        return array.transpose(1, 0, 2).reshape(micro, frames, positions, width)

    return home(cl.o_out), home(cl.o_in), cl.o_gain[:, 0], grads[0], grads[1], cl.o_gain[:, 1], grads[2], grads[3]


def shortened(x):

    def short(part):
        return part.astype(jnp.bfloat16) if part.dtype == jnp.float32 else part

    return jax.tree.map(short, x)


PRECISE = lax.Precision.HIGHEST
matmul, times_transposed, contract_rows = dot, dot_nt, dot_tn


def by_weights(
    block_input,
    out_grad,
    item_lengths,
    frame_offsets,
    norm_attn,
    w_qkv,
    w_out,
    norm_ffn,
    w_gate_up,
    w_down,
):
    micro, frames, positions, model_width = block_input.shape
    head_dim = model_width // HEADS
    hidden_size = w_gate_up.shape[2] // 2
    head_shape = (frames, positions, HEADS, head_dim)
    slot_index = jnp.arange(ITEM_SLOTS)[None, None, :]
    first_slot = frame_offsets[:, :, None]
    valid_rows = (slot_index >= first_slot) & (slot_index < first_slot + item_lengths[:, :, None])
    valid_rows = valid_rows.astype(jnp.float32).reshape(micro, frames)
    causal = jnp.arange(positions)[:, None] >= jnp.arange(positions)[None, :]
    totals = (
        jnp.zeros((positions, model_width), jnp.float32),
        jnp.zeros((positions, model_width, 3 * model_width), jnp.float32),
        jnp.zeros((positions, model_width, model_width), jnp.float32),
        jnp.zeros((positions, model_width), jnp.float32),
        jnp.zeros((positions, model_width, 2 * hidden_size), jnp.float32),
        jnp.zeros((positions, hidden_size, model_width), jnp.float32),
    )
    output_list = []
    input_grad_list = []
    for batch_index in range(micro):
        inputs = block_input[batch_index].astype(jnp.float32)
        qkv_all, gain_in_all = (
            lax.all_gather(w_qkv, "fsdp", axis=1, tiled=True),
            lax.all_gather(norm_attn, "fsdp", axis=1, tiled=True),
        )
        first_saved = []
        qkv_list = []
        for place in range(positions):
            rows = inputs[:, place]
            scale_one = rms_scale(rows)
            normed = (rows * scale_one * gain_in_all[place]).astype(jnp.bfloat16)
            first_saved.append((scale_one, normed))
            qkv_list.append(matmul(normed, qkv_all[place]).astype(jnp.bfloat16))
        qkv_proj = jnp.stack(qkv_list, axis=1)
        query_heads = qkv_proj[..., :model_width].reshape(head_shape)
        key_heads = qkv_proj[..., model_width : 2 * model_width].reshape(head_shape)
        value_heads = qkv_proj[..., 2 * model_width :].reshape(head_shape)
        scores = jnp.einsum(
            "fihd,fjhd->fhij", query_heads, key_heads, preferred_element_type=jnp.float32
        ) / math.sqrt(head_dim)
        scores = jnp.where(causal, scores, -1e30)
        attention = jax.nn.softmax(scores, axis=-1)
        attention_low = attention.astype(jnp.bfloat16)
        mixed_heads = jnp.einsum(
            "fhij,fjhd->fihd", attention_low, value_heads, preferred_element_type=jnp.float32
        )
        mixed_heads = mixed_heads.reshape(frames, positions, model_width).astype(jnp.bfloat16)
        out_all, gain_two_all, gu_all, down_all = (
            lax.all_gather(w_out, "fsdp", axis=1, tiled=True),
            lax.all_gather(norm_ffn, "fsdp", axis=1, tiled=True),
            lax.all_gather(w_gate_up, "fsdp", axis=1, tiled=True),
            lax.all_gather(w_down, "fsdp", axis=1, tiled=True),
        )
        second_saved = []
        output_rows = []
        for place in range(positions):
            middle = inputs[:, place] + matmul(mixed_heads[:, place], out_all[place])
            scale_two = rms_scale(middle)
            normed_two = (middle * scale_two * gain_two_all[place]).astype(jnp.bfloat16)
            gate_up = matmul(normed_two, gu_all[place])
            hidden = (jax.nn.silu(gate_up[:, :hidden_size]) * gate_up[:, hidden_size:]).astype(
                jnp.bfloat16
            )
            second_saved.append((middle, scale_two, normed_two, gate_up, hidden))
            output_rows.append((middle + matmul(hidden, down_all[place])).astype(jnp.bfloat16))
        output_list.append(jnp.stack(output_rows, axis=1))
        upstream = (
            out_grad[batch_index].astype(jnp.float32) * valid_rows[batch_index][:, None, None]
        )
        out_all, gain_two_all, gu_all, down_all = (
            lax.all_gather(w_out, "fsdp", axis=1, tiled=True),
            lax.all_gather(norm_ffn, "fsdp", axis=1, tiled=True),
            lax.all_gather(w_gate_up, "fsdp", axis=1, tiled=True),
            lax.all_gather(w_down, "fsdp", axis=1, tiled=True),
        )
        out_grads = []
        gain_two_grads = []
        gu_grads = []
        down_grads = []
        middle_grads = []
        attn_grads = []
        for place in range(positions):
            middle, scale_two, normed_two, gate_up, hidden = second_saved[place]
            gate = gate_up[:, :hidden_size]
            up_part = gate_up[:, hidden_size:]
            grad_ffn = upstream[:, place].astype(jnp.bfloat16)
            down_grads.append(contract_rows(hidden, grad_ffn))
            grad_hidden = times_transposed(grad_ffn, down_all[place])
            sigma = jax.nn.sigmoid(gate)
            grad_gate = grad_hidden * up_part * sigma * (1.0 + gate * (1.0 - sigma))
            grad_up = grad_hidden * jax.nn.silu(gate)
            grad_gate_up = jnp.concatenate([grad_gate, grad_up], axis=-1).astype(jnp.bfloat16)
            gu_grads.append(contract_rows(normed_two, grad_gate_up))
            grad_normed_two = times_transposed(grad_gate_up, gu_all[place])
            gain_two_grads.append(jnp.sum(grad_normed_two * middle * scale_two, axis=0))
            grad_middle = upstream[:, place] + norm_backward(
                middle, scale_two, gain_two_all[place], grad_normed_two
            )
            grad_branch = grad_middle.astype(jnp.bfloat16)
            out_grads.append(contract_rows(mixed_heads[:, place], grad_branch))
            attn_grads.append(times_transposed(grad_branch, out_all[place]).astype(jnp.bfloat16))
            middle_grads.append(grad_middle)
        grad_mixed = jnp.stack(attn_grads, axis=1).reshape(head_shape)
        grad_attention = jnp.einsum(
            "fihd,fjhd->fhij", grad_mixed, value_heads, preferred_element_type=jnp.float32
        )
        grad_values = jnp.einsum(
            "fhij,fihd->fjhd", attention_low, grad_mixed, preferred_element_type=jnp.float32
        )
        grad_scores = attention * (
            grad_attention - jnp.sum(attention * grad_attention, axis=-1, keepdims=True)
        )
        grad_scores = grad_scores / math.sqrt(head_dim)
        grad_query = jnp.einsum(
            "fhij,fjhd->fihd", grad_scores, key_heads.astype(jnp.float32), precision=PRECISE
        )
        grad_keys = jnp.einsum(
            "fhij,fihd->fjhd", grad_scores, query_heads.astype(jnp.float32), precision=PRECISE
        )
        flat_shape = (frames, positions, model_width)
        grad_qkv = jnp.concatenate(
            [
                grad_query.reshape(flat_shape),
                grad_keys.reshape(flat_shape),
                grad_values.reshape(flat_shape),
            ],
            axis=-1,
        ).astype(jnp.bfloat16)
        qkv_all, gain_in_all = (
            lax.all_gather(w_qkv, "fsdp", axis=1, tiled=True),
            lax.all_gather(norm_attn, "fsdp", axis=1, tiled=True),
        )
        qkv_grads = []
        gain_one_grads = []
        input_rows = []
        for place in range(positions):
            scale_one, normed = first_saved[place]
            rows = inputs[:, place]
            qkv_grads.append(contract_rows(normed, grad_qkv[:, place]))
            grad_normed = times_transposed(grad_qkv[:, place], qkv_all[place])
            gain_one_grads.append(jnp.sum(grad_normed * rows * scale_one, axis=0))
            input_rows.append(
                (
                    middle_grads[place]
                    + norm_backward(rows, scale_one, gain_in_all[place], grad_normed)
                ).astype(jnp.bfloat16)
            )
        input_grad_list.append(jnp.stack(input_rows, axis=1))
        batch_grads = (
            jnp.stack(gain_one_grads),
            jnp.stack(qkv_grads),
            jnp.stack(out_grads),
            jnp.stack(gain_two_grads),
            jnp.stack(gu_grads),
            jnp.stack(down_grads),
        )
        totals = tuple((total + update for total, update in zip(totals, batch_grads)))
    totals = (
        lax.psum_scatter(totals[0], "fsdp", scatter_dimension=1, tiled=True),
        lax.psum_scatter(totals[1], "fsdp", scatter_dimension=1, tiled=True),
        lax.psum_scatter(totals[2], "fsdp", scatter_dimension=1, tiled=True),
        lax.psum_scatter(totals[3], "fsdp", scatter_dimension=1, tiled=True),
        lax.psum_scatter(totals[4], "fsdp", scatter_dimension=1, tiled=True),
        lax.psum_scatter(totals[5], "fsdp", scatter_dimension=1, tiled=True),
    )
    totals = jax.tree.map(lambda part: part.astype(jnp.float32), lax.psum(shortened(totals), "dp"))
    return (
        jnp.stack(output_list),
        jnp.stack(input_grad_list),
        totals[0],
        totals[1],
        totals[2],
        totals[3],
        totals[4],
        totals[5],
    )


def fits(mesh, shapes):
    return mesh.shape["dp"] == 4 and all(s[1] % 16 == 0 for s in shapes) and shapes[0][1] % 128 == 0


def solution(mesh):
    n = mesh.shape["fsdp"]

    def on_device(*args):
        if fits(mesh, [args[k].shape for k in (5, 6, 8, 9)]):
            return by_position(n, *args)
        return by_weights(*args)

    placed = (
        P(None, ("dp", "fsdp"), None, None),
        P(None, ("dp", "fsdp"), None, None),
        P(None, ("dp", "fsdp")),
        P(None, ("dp", "fsdp")),
        P(None, "fsdp"),
        P(None, "fsdp", None),
        P(None, "fsdp", None),
        P(None, "fsdp"),
        P(None, "fsdp", None),
        P(None, "fsdp", None),
    )
    return jax.shard_map(
        on_device,
        mesh=mesh,
        in_specs=placed,
        out_specs=(
            P(None, ("dp", "fsdp"), None, None),
            P(None, ("dp", "fsdp"), None, None),
            P(None, "fsdp"),
            P(None, "fsdp", None),
            P(None, "fsdp", None),
            P(None, "fsdp"),
            P(None, "fsdp", None),
            P(None, "fsdp", None),
        ),
        check_vma=False,
    )
```

```python
import functools
import math

import jax
import jax.numpy as jnp
from jax import lax
from jax.experimental import pallas as pl
from jax.experimental.pallas import tpu as pltpu
from jax.sharding import PartitionSpec as P

MESH = pl.DeviceIdType.MESH
BF = jnp.bfloat16
F32 = jnp.float32
HEADS = 16
ITEM_SLOTS = 32
EPSILON = 1e-05
LANES = 3
AXES = ("dp", "fsdp")


def rem(a, b):
    return a % b if isinstance(a, int) else lax.rem(a, b)


def div(a, b):
    return a // b if isinstance(a, int) else lax.div(a, b)


def place(n):
    dp, f = lax.axis_index("dp"), lax.axis_index("fsdp")
    x, c = lax.div(dp, 2), lax.rem(dp, 2)
    z, h = lax.div(f, 2), lax.rem(f, 2)
    r = z * (1 - h) + (n - 1 - z) * h
    return x, c, f, r


def ring_index(r, n):
    hh = lax.div(r, n // 2)
    return (2 * r) * (1 - hh) + (2 * (n - 1 - r) + 1) * hh


class Spot:
    def __init__(self, n):
        self.n = n
        x, c, f, r = place(n)
        self.x, self.c, self.f, self.r = x, c, f, r
        self.d = 1 - 2 * c
        dp = 2 * x + c
        self.next = (dp, ring_index(lax.rem(r + self.d + n, n), n))
        self.prev = (dp, ring_index(lax.rem(r - self.d + n, n), n))
        self.sib = (2 * x + 1 - c, f)
        self.mate = (2 * (1 - x) + c, f)

    def owner(self, hop):
        return ring_index(lax.rem(self.r - self.d * (hop + 1) + self.n, self.n), self.n)

    def greet(self):
        barrier = pltpu.get_barrier_semaphore()
        for who in (self.next, self.prev, self.sib, self.mate):
            pl.semaphore_signal(barrier, inc=1, device_id=who, device_id_type=MESH)
        pl.semaphore_wait(barrier, 4)


def remote(src, dst, send, recv, who):
    return pltpu.make_async_remote_copy(src, dst, send, recv, device_id=who, device_id_type=MESH)


def pieces_of(shapes, parts):
    out = []
    for a, (shape, count) in enumerate(zip(shapes, parts)):
        tiles = shape[0] // 16
        cuts = [16 * (tiles * k // count) for k in range(count + 1)]
        for k in range(count):
            out.append((a, cuts[k], cuts[k + 1] - cuts[k], shape[1] // 2))
    return out


def lanes_of(pieces):
    return [pieces[k::LANES] for k in range(LANES)]


class Weights:
    def __init__(self, spot, lanes, shard_rows, shards, wholes, ring_send, ring_recv, sib_send, sib_recv):
        self.spot, self.lanes, self.shard_rows = spot, lanes, shard_rows
        self.shards, self.wholes = shards, wholes
        self.sems = ring_send, ring_recv, sib_send, sib_recv
        self.hops = spot.n - 1
        self.total = [len(lane) * self.hops for lane in lanes]
        self.events = [(lane, t) for t in range(max(self.total)) for lane in range(len(lanes)) if t < self.total[lane]]
        self.flying, self.sent, self.handed = {}, [], []

    def block(self, piece, owner):
        a, first, rows, cols = piece
        return self.wholes[a].at[pl.ds(owner * self.shard_rows[a] + first, rows), pl.ds(self.spot.c * cols, cols)]

    def send(self, lane, t):
        piece, hop = self.lanes[lane][t // self.hops], t % self.hops
        a, first, rows, cols = piece
        spot = self.spot
        if hop == 0:
            src = self.shards[a].at[spot.x, pl.ds(first, rows), pl.ds(spot.c * cols, cols)]
            dst = self.block(piece, spot.f)
        else:
            src = dst = self.block(piece, spot.owner(hop - 1))
        cp = remote(src, dst, self.sems[0].at[lane, t], self.sems[1].at[lane, t], spot.next)
        cp.start()
        self.flying[lane] = cp

    def start(self):
        for lane in range(len(self.lanes)):
            self.send(lane, 0)

    def tick(self, count):
        for lane, t in self.events[:count]:
            self.flying[lane].wait_recv()
            self.sent.append(self.flying[lane])
            if t + 1 < self.total[lane]:
                self.send(lane, t + 1)
            piece, hop = self.lanes[lane][t // self.hops], t % self.hops
            here = self.block(piece, self.spot.owner(hop))
            cp = remote(here, here, self.sems[2].at[lane, t], self.sems[3].at[lane, t], self.spot.sib)
            cp.start()
            self.handed.append((piece[0], cp))
        self.events = self.events[count:]

    def until(self, array):
        while any(self.lanes[lane][t // self.hops][0] <= array for lane, t in self.events):
            self.tick(1)
        later = []
        for a, cp in self.handed:
            if a <= array:
                cp.wait_recv()
                self.sent.append(cp)
            else:
                later.append((a, cp))
        self.handed = later

    def finish(self):
        for cp in self.sent:
            cp.wait_send()


def dot(left, right):
    return jnp.dot(left, right, preferred_element_type=F32)


def dot_nt(left, right):
    return lax.dot_general(left, right, (((1,), (1,)), ((), ())), preferred_element_type=F32)


def dot_tn(left, right):
    return lax.dot_general(left, right, (((0,), (0,)), ((), ())), preferred_element_type=F32)


def rms_scale(values):
    return lax.rsqrt(jnp.mean(values * values, axis=-1, keepdims=True) + EPSILON)


def norm_backward(values, scale, gain, upstream):
    weighted = gain * upstream
    return scale * weighted - values * scale**3 * jnp.mean(values * weighted, axis=-1, keepdims=True)


def head_table(ref):
    width = ref.shape[0]
    rows = lax.broadcasted_iota(jnp.int32, ref.shape, 0)
    cols = lax.broadcasted_iota(jnp.int32, ref.shape, 1)
    ref[...] = (lax.div(rows, width // HEADS) == cols).astype(F32).astype(BF)


def per_head(product, table):
    high = product.astype(BF)
    rest = (product - high.astype(F32)).astype(BF)
    return dot(high, table[...]) + dot(rest, table[...])


def spread(per, table):
    return dot_nt(per, table[...])


def spread_two(per, table):
    high = per.astype(BF)
    rest = (per - high.astype(F32)).astype(BF)
    return dot_nt(high, table[...]) + dot_nt(rest, table[...])


def pair(a, b):
    top = jnp.maximum(a, b)
    ea, eb = jnp.exp(a - top), jnp.exp(b - top)
    return ea / (ea + eb), eb / (ea + eb)


def flat(scores):
    return scores.T[:HEADS]


def tall(scores):
    return jnp.concatenate([scores, jnp.zeros((128 - HEADS, scores.shape[1]), F32)], axis=0).T


CHUNK = 256


class Refs:
    def __init__(self, names, refs):
        assert len(names) == len(refs)
        self.__dict__.update(zip(names, refs))


def forward_kernel(n, lanes, shard_rows, names, *refs):
    k = Refs(names, refs)
    spot = Spot(n)
    x, c, f = spot.x, spot.c, spot.f
    tokens, width = k.X.shape
    half, chunks = tokens // 2, tokens // CHUNK
    ff = k.HID.shape[1]
    position_one = x == 1
    ring = Weights(
        spot, lanes, shard_rows, (k.wq, k.wo, k.wg, k.wd), (k.Wq, k.Wo, k.Wg, k.Wd),
        k.ring_send, k.ring_recv, k.sib_send, k.sib_recv,
    )

    local = []
    for i, (src, dst) in enumerate((
        (k.xo, k.X.at[pl.ds(x * half, half)]),
        (k.gn, k.GA.at[f]),
        (k.wq.at[x], k.Wq.at[pl.ds(f * shard_rows[0], shard_rows[0])]),
        (k.wo.at[x], k.Wo.at[pl.ds(f * shard_rows[1], shard_rows[1])]),
        (k.wg.at[x], k.Wg.at[pl.ds(f * shard_rows[2], shard_rows[2])]),
        (k.wd.at[x], k.Wd.at[pl.ds(f * shard_rows[3], shard_rows[3])]),
        (k.go, k.GY.at[pl.ds(x * half, half)]),
    )):
        cp = pltpu.make_async_copy(src, dst, k.loc.at[i])
        cp.start()
        local.append(cp)

    others = greet_all(spot)

    gains = []
    for i, who in enumerate(others):
        cp = remote(k.gn, k.GA.at[f], k.gain_send.at[i], k.gain_recv.at[i], who)
        cp.start()
        gains.append(cp)
    ring.start()
    swaps = [
        remote(src, dst.at[pl.ds(x * half, half)], k.swap_send.at[i], k.swap_recv.at[i], spot.mate)
        for i, (src, dst) in enumerate(((k.xs, k.X), (k.gs, k.GY)))
    ]
    swaps[0].start()

    @pl.when(x == 0)
    def _():
        swaps[1].start()

    outs = []

    def put(src, dst):
        cp = pltpu.make_async_copy(src, dst, k.put.at[len(outs)])
        cp.start()
        outs.append(cp)
        return cp

    head_table(k.E)
    k.G[...] = jnp.zeros_like(k.G)
    local[0].wait()
    local[1].wait()
    for cp in gains:
        cp.wait()
    for j in range(n):
        block = k.GA[j].astype(F32)
        for row in range(2):
            k.G[pl.ds(row, 1), pl.ds(j * 128, 128)] = block[row : row + 1]
    put(k.G, k.o_gain)

    def rows_of(j):
        return pl.ds(pl.multiple_of(j * CHUNK, CHUNK), CHUNK)

    def first_norm(at):
        def step(i, carry):
            rows = pl.ds(pl.multiple_of(at * half + i * CHUNK, CHUNK), CHUNK)
            values = k.X[rows].astype(F32)
            k.N1[rows] = (values * rms_scale(values) * k.G[0:1]).astype(BF)
            return carry

        lax.fori_loop(0, half // CHUNK, step, 0)

    ring.tick(4)
    first_norm(x)
    ring.tick(14)
    swaps[0].wait()
    first_norm(1 - x)
    put(k.X, k.o_x)
    put(k.N1, k.o_n1)
    local[2].wait()
    local[3].wait()
    ring.until(1)
    put(k.Wq, k.o_wq)
    put(k.Wo, k.o_wo)

    def project(first, count):
        def step(i, carry):
            cols = pl.ds(pl.multiple_of(first + i * 256, 256), 256)
            k.QKV[:, cols] = dot(k.N1[...], k.Wq[:, cols]).astype(BF)
            return carry

        lax.fori_loop(0, count // 256, step, 0)

    def across(src, j):
        return remote(src, k.CR.at[rows_of(j)], k.cross_send.at[j], k.cross_recv.at[j], spot.mate)

    def across_scores(j):
        return remote(k.SS.at[j], k.SR.at[j], k.score_send.at[j], k.score_recv.at[j], spot.mate)

    def query(j):
        return k.QKV.at[rows_of(j), pl.ds(0, width)]

    scaling = 1.0 / math.sqrt(width // HEADS)

    def own_score(j):
        rows = rows_of(j)
        q, key = k.QKV[rows, 0:width].astype(F32), k.QKV[rows, width : 2 * width].astype(F32)
        score = per_head(q * key, k.E) * scaling
        k.S[rows] = score

        @pl.when(position_one)
        def _():
            k.SS[j] = flat(score)
            across_scores(j).start()
            if j + 1 < chunks:
                across(query(j + 1), j + 1).start()
            else:
                swaps[1].start()

    def serve(j):
        @pl.when(x == 0)
        def _():
            rows = rows_of(j)
            across(query(j), j).wait_recv()
            across_scores(j).wait_recv()
            score = per_head(k.CR[rows].astype(F32) * k.QKV[rows, width : 2 * width].astype(F32), k.E) * scaling
            k.SS[j] = flat(score)
            across_scores(j).start()
            here, there = pair(score, tall(k.SR[j]))
            k.PR[1, rows] = here
            k.PR[2, rows] = there
            part = spread(here.astype(BF), k.E) * k.QKV[rows, 2 * width : 3 * width].astype(F32)
            k.CS[rows] = part.astype(BF)
            across(k.CS.at[rows], j).start()

    mids = {}

    def attend(j):
        rows = rows_of(j)

        @pl.when(position_one)
        def _():
            across(query(j), j).wait_recv()
            across_scores(j).wait_recv()

        other = jnp.where(position_one, tall(k.SR[j]), -1e30)
        here, there = pair(k.S[rows], other)
        k.PR[0, rows] = here
        mixed = spread(here.astype(BF), k.E) * k.QKV[rows, 2 * width : 3 * width].astype(F32)
        mixed = mixed + jnp.where(position_one, k.CR[rows].astype(F32), 0.0)
        k.ATT[rows] = mixed.astype(BF)
        if j - 2 in mids:
            mids[j - 2].wait()
        middle = k.X[rows].astype(F32) + dot(k.ATT[rows], k.Wo[...])
        k.MID[j % 2] = middle
        k.N2[rows] = (middle * rms_scale(middle) * k.G[1:2]).astype(BF)
        cp = pltpu.make_async_copy(k.MID.at[j % 2], k.o_mid.at[rows], k.mid.at[j % 2])
        cp.start()
        mids[j] = cp

    project(0, width // 2)
    ring.tick(1)
    project(width // 2, width // 2)

    @pl.when(position_one)
    def _():
        across(query(0), 0).start()

    ring.tick(2)
    project(width, width // 2)
    ring.tick(1)
    project(width + width // 2, width // 2)
    ring.tick(1)
    for j in range(chunks):
        own_score(j)
        ring.tick(1)
    project(2 * width, width)
    put(k.QKV, k.o_qkv)
    ring.tick(2)

    serve(0)
    ring.tick(4)
    serve(1)
    ring.tick(1)
    attend(0)
    ring.tick(4)
    serve(2)
    ring.tick(1)
    attend(1)
    ring.tick(4)
    local[4].wait()
    ring.until(2)
    put(k.Wg, k.o_wg)
    serve(3)

    def gate_copies(step):
        slot = rem(step, 2)
        for part in range(2):
            yield pltpu.make_async_copy(k.GU.at[slot, part], k.o_gu.at[step, part], k.gu.at[slot, part])

    def feed(h, first, last):
        def step(t, carry):
            rows = pl.ds(h * half, half)
            at = h * (ff // 256) + t
            slot = lax.rem(at, 2)
            gate = dot(k.N2[rows], k.Wg[:, pl.ds(pl.multiple_of(t * 256, 256), 256)])
            up = dot(k.N2[rows], k.Wg[:, pl.ds(pl.multiple_of(ff + t * 256, 256), 256)])
            k.HID[rows, pl.ds(pl.multiple_of(t * 256, 256), 256)] = (gate * jax.nn.sigmoid(gate) * up).astype(BF)

            @pl.when(at >= 2)
            def _():
                for cp in gate_copies(at - 2):
                    cp.wait()

            k.GU[slot, 0] = gate.astype(BF)
            k.GU[slot, 1] = up.astype(BF)
            for cp in gate_copies(at):
                cp.start()
            return carry

        lax.fori_loop(first, last, step, 0)

    tiles = ff // 256
    for t in range(tiles):
        feed(0, t, t + 1)
        ring.tick(1)
        if t == 7:
            attend(2)
            ring.tick(1)
    attend(3)
    put(k.N2, k.o_n2)
    put(k.ATT, k.o_att)
    put(k.PR, k.o_p)
    for t in range(tiles):
        feed(1, t, t + 1)
        ring.tick(1)
    put(k.HID, k.o_hid)
    local[6].wait()
    swaps[1].wait()
    put(k.GY, k.o_gy)

    cols = width // 2

    def down_copies(m):
        slot = rem(m, 4)
        rows = pl.ds(pl.multiple_of(m * 256, 256), 256)
        theirs = remote(
            k.DW.at[slot, :, pl.ds(pl.multiple_of((1 - c) * cols, cols), cols)],
            k.o_sib.at[rows], k.down_send.at[slot], k.down_recv.at[m], spot.sib,
        )
        ours = pltpu.make_async_copy(
            k.DW.at[slot, :, pl.ds(pl.multiple_of(c * cols, cols), cols)], k.o_dwd.at[rows], k.down.at[slot]
        )
        return theirs, ours

    def down_grad(first, last):
        def step(m, carry):
            part = dot_tn(k.HID[:, pl.ds(pl.multiple_of(m * 256, 256), 256)], k.GY[...]).astype(BF)

            @pl.when(m >= 4)
            def _():
                theirs, ours = down_copies(m - 4)
                theirs.wait_send()
                ours.wait()

            k.DW[lax.rem(m, 4)] = part
            for cp in down_copies(m):
                cp.start()
            return carry

        lax.fori_loop(first, last, step, 0)

    for m in range(tiles):
        down_grad(m, m + 1)
        ring.tick(1)
    local[5].wait()
    ring.until(3)
    put(k.Wd, k.o_wd)
    for m in range(tiles - 4, tiles):
        theirs, ours = down_copies(m)
        theirs.wait_send()
        ours.wait()
    for m in range(tiles):
        down_copies(m)[0].wait_recv()
    put(k.CR, k.o_cr)
    for at in (2 * tiles - 2, 2 * tiles - 1):
        for cp in gate_copies(at):
            cp.wait()
    for j in (chunks - 2, chunks - 1):
        mids[j].wait()
    for j in range(chunks):
        across(query(j), j).wait_send()
        across_scores(j).wait_send()
    ring.finish()
    for cp in outs:
        cp.wait()


def forward(n, xs, xo, gs, go, wq, wo, wg, wd, gn):
    weights = (wq, wo, wg, wd)
    shapes = [w.shape[1:] for w in weights]
    parts = [
        [p for p in pieces_of(shapes, (4, 1, 4, 4)) if p[0] == a] for a in range(4)
    ]
    lanes = [[parts[0][i], parts[2][i], parts[3][i]] for i in range(4)] + [parts[1]]
    steps = 3 * (n - 1)
    half, width = xo.shape
    tokens, ff = 2 * half, wd.shape[1] * n
    tiles, chunks = ff // 256, tokens // CHUNK
    wholes = [(s[0] * n, s[1]) for s in shapes]
    square = (tokens, width)
    out = dict(
        o_wq=(wholes[0], BF), o_wo=(wholes[1], BF), o_wg=(wholes[2], BF), o_wd=(wholes[3], BF),
        o_x=(square, BF), o_gy=(square, BF), o_n1=(square, BF), o_qkv=((tokens, 3 * width), BF),
        o_cr=(square, BF), o_p=((3, tokens, 128), F32), o_att=(square, BF), o_mid=(square, F32),
        o_n2=(square, BF), o_gu=((2 * tiles, 2, half, 256), BF), o_hid=((tokens, ff), BF),
        o_dwd=((ff, width // 2), BF), o_sib=((ff, width // 2), BF), o_gain=((8, width), F32),
    )
    vmem = dict(
        Wq=(wholes[0], BF), Wo=(wholes[1], BF), Wg=(wholes[2], BF), Wd=(wholes[3], BF),
        X=(square, BF), GY=(square, BF), N1=(square, BF), QKV=((tokens, 3 * width), BF),
        CR=(square, BF), CS=(square, BF), ATT=(square, BF), MID=((2, CHUNK, width), F32),
        N2=(square, BF), GU=((2, 2, half, 256), BF), HID=((tokens, ff), BF), DW=((4, 256, width), BF),
        E=((width, 128), BF), G=((8, width), F32), GA=((n, 16, 128), BF), S=((tokens, 128), F32),
        SS=((chunks, HEADS, CHUNK), F32), SR=((chunks, HEADS, CHUNK), F32), PR=((3, tokens, 128), F32),
    )
    sems = dict(
        ring_send=(len(lanes), steps), ring_recv=(len(lanes), steps), sib_send=(len(lanes), steps),
        sib_recv=(len(lanes), steps), loc=(7,), gain_send=(n - 1,), gain_recv=(n - 1,),
        swap_send=(2,), swap_recv=(2,), put=(20,), cross_send=(chunks,), cross_recv=(chunks,),
        score_send=(chunks,), score_recv=(chunks,), mid=(2,), gu=(2, 2), down_send=(4,),
        down_recv=(tiles,), down=(4,),
    )
    ins = dict(xs=xs, xo=xo, gs=gs, go=go, wq=wq, wo=wo, wg=wg, wd=wd, gn=gn)
    return call(forward_kernel, (n, lanes, [s[0] for s in shapes]), ins, out, vmem, sems, 0)


class Sums:
    def __init__(self, spot, lanes, shard_rows, half_cols, ours, theirs, outs, landing, k):
        self.spot, self.lanes, self.shard_rows, self.half_cols = spot, lanes, shard_rows, half_cols
        self.ours, self.theirs, self.outs, self.landing, self.k = ours, theirs, outs, landing, k
        self.hops = spot.n - 1
        self.ready = set()
        self.loaded = [0] * len(lanes)
        self.used = [0] * len(lanes)
        self.flying = [None] * len(lanes)
        self.at = [0] * len(lanes)
        self.first = [None] * len(lanes)
        self.queue, self.sent, self.tail, self.mates = [], [], [], []
        self.count = 0

    def term_copies(self, lane, u):
        piece = self.lanes[lane][u // (self.hops + 1)]
        a, row, rows, col, cols = piece
        owner = self.spot.owner(u % (self.hops + 1))
        at = (pl.ds(owner * self.shard_rows[a] + row, rows), pl.ds(col, cols))
        for side, ref in enumerate((self.ours[a], self.theirs[a])):
            dst = self.k.TERM.at[lane, u % 2, side, pl.ds(0, rows), pl.ds(0, cols)]
            yield pltpu.make_async_copy(ref.at[at], dst, self.k.term.at[lane, u % 2, side])

    def prefetch(self, lane):
        per = self.hops + 1
        while self.loaded[lane] < min(self.used[lane] + 2, per * len(self.lanes[lane])):
            u = self.loaded[lane]
            if self.lanes[lane][u // per] not in self.ready:
                return
            for cp in self.term_copies(lane, u):
                cp.start()
            self.loaded[lane] += 1

    def term(self, lane):
        u = self.used[lane]
        assert u < self.loaded[lane]
        _, _, rows, _, cols = self.lanes[lane][u // (self.hops + 1)]
        for cp in self.term_copies(lane, u):
            cp.wait()
        ours, theirs = (self.k.TERM[lane, u % 2, side, 0:rows, 0:cols].astype(F32) for side in range(2))
        return ours + theirs

    def step(self, lane):
        t = self.at[lane]
        if t == self.hops * len(self.lanes[lane]):
            return
        piece = self.lanes[lane][t // self.hops]
        if piece not in self.ready:
            self.flying[lane] = None
            return
        hop = t % self.hops
        slots = self.landing[piece]
        value = self.term(lane)
        if hop == 0:
            if self.first[lane] is not None:
                self.first[lane].wait_send()
            buf = self.k.FIRST.at[lane, pl.ds(0, piece[2]), pl.ds(0, piece[4])]
        else:
            buf = slots.at[hop - 1]
            value = value + buf[...].astype(F32)
        buf[...] = value.astype(BF)
        self.used[lane] += 1
        cp = remote(buf, slots.at[hop], self.k.ring_send.at[lane, t], self.k.ring_recv.at[lane, t], self.spot.next)
        cp.start()
        self.prefetch(lane)
        if hop == 0:
            self.first[lane] = cp
        else:
            self.sent.append(cp)
        self.flying[lane] = cp
        self.at[lane] += 1
        self.queue.append(lane)

    def offer(self, pieces):
        self.ready.update(pieces)
        for lane in range(len(self.lanes)):
            if self.flying[lane] is None and self.at[lane] < self.hops * len(self.lanes[lane]):
                self.prefetch(lane)
                self.step(lane)
            else:
                self.prefetch(lane)

    def finish_piece(self, lane, piece):
        a, row, rows, col, cols = piece
        spot, k, i = self.spot, self.k, self.count
        self.count += 1
        end = self.landing[piece].at[self.hops - 1]
        end[...] = (end[...].astype(F32) + self.term(lane)).astype(BF)
        self.used[lane] += 1
        self.prefetch(lane)
        at = (pl.ds(row, rows), pl.ds(spot.c * self.half_cols[a] + col, cols))
        place = self.outs[a].at[(spot.x,) + at]
        cp = pltpu.make_async_copy(end, place, k.end.at[i])
        cp.start()
        self.tail.append(cp)
        cp = remote(end, place, k.end_sib_send.at[i], k.end_sib_recv.at[i], spot.sib)
        cp.start()
        self.tail.append(cp)
        cp = remote(end, place, k.end_mate_send.at[i], k.end_mate_recv.at[i], spot.mate)
        cp.start()
        self.mates.append((cp, self.outs[a].at[(1 - spot.x,) + at], i))

    def pass_on(self, keep):
        while len(self.mates) > keep:
            cp, place, i = self.mates.pop(0)
            cp.wait()
            far = remote(place, place, self.k.far_send.at[i], self.k.far_recv.at[i], self.spot.sib)
            far.start()
            self.tail.append(far)

    def tick(self, count, least=3):
        for _ in range(count):
            if len(self.queue) < least:
                return
            lane = self.queue.pop(0)
            self.flying[lane].wait_recv()
            t = self.at[lane]
            if t % self.hops == 0:
                self.finish_piece(lane, self.lanes[lane][t // self.hops - 1])
            self.step(lane)

    def finish(self):
        while self.queue:
            self.tick(1, 1)
        self.pass_on(0)
        for cp in self.tail:
            cp.wait()
        for cp in self.sent + [cp for cp in self.first if cp is not None]:
            cp.wait_send()


def sum_scratch(n, lanes, most):
    count = sum(len(lane) for lane in lanes)
    steps = max(len(lane) for lane in lanes) * (n - 1)
    vmem = dict(TERM=((len(lanes), 2, 2) + most, BF), FIRST=((len(lanes),) + most, BF))
    sems = dict(
        term=(len(lanes), 2, 2), ring_send=(len(lanes), steps), ring_recv=(len(lanes), steps), end=(count,),
        end_sib_send=(count,), end_sib_recv=(count,), end_mate_send=(count,), end_mate_recv=(count,), far_send=(count,),
        far_recv=(count,),
    )
    landing = {p: ("L%d_%d" % (p[0], p[1] + p[3]), ((n - 1,) + (p[2], p[4]), BF)) for lane in lanes for p in lane}
    vmem.update(landing.values())
    return vmem, sems, {p: name for p, (name, _) in landing.items()}


def tokens_at(j):
    return pl.ds(pl.multiple_of(j * CHUNK, CHUNK), CHUNK)


class Exchange:
    def __init__(self, spot, k):
        self.spot, self.k = spot, k

    def rows(self, src, j):
        k = self.k
        return remote(src, k.CR.at[tokens_at(j)], k.cross_send.at[j], k.cross_recv.at[j], self.spot.mate)

    def numbers(self, j):
        k = self.k
        return remote(k.SS.at[j], k.SR.at[j], k.score_send.at[j], k.score_recv.at[j], self.spot.mate)

    def send(self, src, numbers, j):
        self.k.SS[j] = flat(numbers)
        self.numbers(j).start()
        self.rows(src, j).start()

    def wait_recv(self, src, j):
        self.numbers(j).wait_recv()
        self.rows(src, j).wait_recv()

    def wait_send(self, src, j):
        self.numbers(j).wait_send()
        self.rows(src, j).wait_send()


def greet(spot):
    barrier = pltpu.get_barrier_semaphore()
    for who in (spot.next, spot.prev, spot.sib, spot.mate):
        pl.semaphore_signal(barrier, inc=1, device_id=who, device_id_type=MESH)
    pl.semaphore_wait(barrier, 4)


def greet_all(spot):
    barrier = pltpu.get_barrier_semaphore()
    others = [(2 * spot.x + spot.c, lax.rem(spot.f + i, spot.n)) for i in range(1, spot.n)]
    for who in [spot.sib, spot.mate] + others:
        pl.semaphore_signal(barrier, inc=1, device_id=who, device_id_type=MESH)
    pl.semaphore_wait(barrier, spot.n + 1)
    return others


class Products:
    def __init__(self, spot, k, tiles):
        self.spot, self.k, self.tiles = spot, k, tiles
        self.busy = {}
        self.next = 0

    def tile(self, value, ref, at, index, away):
        k = self.k
        slot = self.next % k.DW.shape[0]
        self.next += 1
        if slot in self.busy:
            cp, was_away = self.busy.pop(slot)
            cp.wait_send() if was_away else cp.wait()
        buf = k.DW.at[slot, pl.ds(0, value.shape[0]), pl.ds(0, value.shape[1])]
        buf[...] = value.astype(BF)
        if away:
            cp = remote(buf, ref.at[at], k.dw.at[slot], k.dw_recv.at[index], self.spot.sib)
        else:
            cp = pltpu.make_async_copy(buf, ref.at[at], k.dw.at[slot])
        cp.start()
        self.busy[slot] = (cp, away)
        return cp

    def grid(self, left, right, first, cols, half_cols, step, ours, theirs, index, tick):
        c = self.spot.c
        waits = []
        for away in (True, False):
            side = (1 - c) if away else c
            for m in range(left.shape[1] // step):
                at_right = pl.ds(pl.multiple_of(side * half_cols + first, 256), cols)
                value = dot_tn(left[:, pl.ds(m * step, step)], right[:, at_right])
                at = (pl.ds(m * step, step), pl.ds(first, cols))
                cp = self.tile(value, theirs if away else ours, at, index + m, away)
                if away:
                    waits.append(cp)
                tick()
        return waits

    def settle(self):
        for cp, away in self.busy.values():
            cp.wait_send() if away else cp.wait()
        self.busy = {}


def backward_kernel(n, lanes, shard_rows, groups, landing, names, *refs):
    k = Refs(names, refs)
    spot = Spot(n)
    x, c = spot.x, spot.c
    tokens, width = k.GA.shape
    half, chunks = tokens // 2, tokens // CHUNK
    ff = k.GG.shape[1] // 2
    tiles = ff // 256
    scaling = 1.0 / math.sqrt(width // HEADS)
    loads = {}

    def load(name, src, dst, sem):
        cp = pltpu.make_async_copy(src, dst, sem)
        cp.start()
        loads[name] = cp

    def load_tile(t):
        slot = t % 2
        load(("wd", t), k.wd.at[pl.ds(t * 256, 256)], k.WT.at[slot], k.tile.at[slot, 0])
        for h in range(2):
            load(("gu", t, h), k.gu.at[h * tiles + t], k.GT.at[slot, h], k.tile.at[slot, 1 + h])

    load("gy", k.gy, k.GY, k.load.at[0])
    load_tile(0)
    load_tile(1)
    load("n2", k.n2, k.N2, k.load.at[1])
    load("gain", k.gain, k.G, k.load.at[2])
    load("p", k.p, k.P, k.load.at[3])
    load("wo", k.wo, k.Wo, k.load.at[4])
    head_table(k.E)
    k.GS[...] = jnp.zeros_like(k.GS)
    greet(spot)

    ring = Sums(
        spot, lanes, shard_rows, (width // 2, ff), (k.dwd, k.o_own), (k.sib, k.o_sib), (k.o_rwd, k.o_rwg),
        {p: getattr(k, name) for p, name in landing.items()}, k,
    )
    ring.offer([lane[0] for lane in lanes])
    swap = Exchange(spot, k)

    loads["gy"].wait()
    for t in range(tiles):
        slot = t % 2
        loads["wd", t].wait()
        for h in range(2):
            loads["gu", t, h].wait()
            rows = pl.ds(h * half, half)
            grad = dot_nt(k.GY[rows], k.WT[slot])
            gate, up = k.GT[slot, h, 0].astype(F32), k.GT[slot, h, 1].astype(F32)
            sigma = jax.nn.sigmoid(gate)
            k.GG[rows, pl.ds(t * 256, 256)] = (grad * up * sigma * (1.0 + gate * (1.0 - sigma))).astype(BF)
            k.GG[rows, pl.ds(ff + t * 256, 256)] = (grad * gate * sigma).astype(BF)
            if h or t % 2:
                ring.tick(1)
        if t + 2 < tiles:
            load_tile(t + 2)
        if t == 2:
            load("wg", k.wg, k.Wg, k.load.at[5])

    products = Products(spot, k, None)
    made = []

    def weight_group(g):
        first, cols = groups[g]
        made.append((g, products.grid(
            k.N2, k.GG, first, cols, ff, 512, k.o_own, k.o_sib, 2 * g, lambda: ring.tick(1)
        )))

    def offer_groups():
        if made:
            products.settle()
        while made:
            g, waits = made.pop(0)
            for cp in waits:
                cp.wait_recv()
            ring.offer([lanes[g][1]])

    def load_rows(j):
        load(("mid", j), k.mid.at[tokens_at(j)], k.MID, k.load.at[6])
        load(("v", j), k.qkv.at[tokens_at(j), pl.ds(2 * width, width)], k.V, k.load.at[7])

    load_rows(0)
    loads["gain"].wait()
    loads["wg"].wait()
    loads["wo"].wait()
    outs = {}

    def norm_chunk(j):
        rows = tokens_at(j)
        for m in range(4):
            part = pl.ds(m * 256, 256)
            k.GN[:, part] = dot_nt(k.GG[rows], k.Wg[part])
            if m % 2:
                ring.tick(1)
            if m == 0:
                offer_groups()
        for name in ("mid", "v"):
            loads[name, j].wait()
        middle, upstream = k.MID[...], k.GN[...]
        scale = rms_scale(middle)
        k.GS[0:1] += jnp.sum(upstream * middle * scale, axis=0, keepdims=True)
        grad = k.GY[rows].astype(F32) + norm_backward(middle, scale, k.G[1:2], upstream)
        if j:
            for cp in outs[j - 1]:
                cp.wait()
        k.GM[...] = grad
        k.GB[...] = grad.astype(BF)
        outs[j] = [
            pltpu.make_async_copy(k.GM, k.o_gm.at[rows], k.put.at[0]),
            pltpu.make_async_copy(k.GB, k.o_gb.at[rows], k.put.at[1]),
        ]
        for cp in outs[j]:
            cp.start()
        k.GA[rows] = dot_nt(k.GB[...], k.Wo[...]).astype(BF)
        numbers = per_head(k.GA[rows].astype(F32) * k.V[...].astype(F32), k.E)
        k.GP[rows] = numbers
        if j + 1 < chunks:
            load_rows(j + 1)

        @pl.when(x == 1)
        def _():
            swap.send(k.GA.at[rows], numbers, j)

        ring.tick(1)

    loads["n2"].wait()
    for g in range(4):
        weight_group(g)
        if g: offer_groups()
    for j in range(chunks):
        norm_chunk(j)
    loads["p"].wait()

    for j in range(chunks):
        rows = tokens_at(j)
        load(("qkv", j), k.qkv.at[rows], k.Wg.at[rows, pl.ds(0, 3 * width)], k.again.at[0, j])
        load(("cr", j), k.cr.at[rows], k.Wg.at[rows, pl.ds(3 * width, width)], k.again.at[1, j])

    def parts(rows):
        return (k.Wg[rows, i * width : (i + 1) * width].astype(F32) for i in range(3))

    def store(rows, j, *grads):
        for i, grad in enumerate(grads):
            k.Wg[rows, i * width : (i + 1) * width] = grad.astype(BF)
        pltpu.make_async_copy(k.Wg.at[rows, pl.ds(0, 3 * width)], k.o_gqkv.at[rows], k.back.at[j]).start()

    def serve(j):
        rows = tokens_at(j)

        @pl.when(x == 0)
        def _():
            swap.wait_recv(k.GA.at[rows], j)
            query, key, value = parts(rows)
            there = k.CR[rows].astype(F32)
            prob, prob_c, prob_d = k.P[0, rows], k.P[1, rows], k.P[2, rows]
            grad_c = per_head(there * value, k.E)
            total_c = prob_c * grad_c + prob_d * tall(k.SR[j])
            score_c = spread_two(prob_c * (grad_c - total_c) * scaling, k.E)
            k.CS[rows] = (score_c * key).astype(BF)
            swap.send(k.CS.at[rows], total_c, j)
            grad = k.GP[rows]
            score = spread_two(prob * (grad - prob * grad) * scaling, k.E)
            ours = k.GA[rows].astype(F32)
            store(
                rows, j, score * key, score * query + score_c * k.Wg[rows, 3 * width : 4 * width].astype(F32),
                spread(prob.astype(BF), k.E) * ours + spread(prob_c.astype(BF), k.E) * there,
            )

    def close(j):
        rows = tokens_at(j)

        @pl.when(x == 1)
        def _():
            swap.wait_recv(k.GA.at[rows], j)
            query, key, value = parts(rows)
            prob = k.P[0, rows]
            score = spread_two(prob * (k.GP[rows] - tall(k.SR[j])) * scaling, k.E)
            store(
                rows, j, score * key + k.CR[rows].astype(F32), score * query,
                spread(prob.astype(BF), k.E) * k.GA[rows].astype(F32),
            )

    for j in range(chunks):
        loads["qkv", j].wait()
        loads["cr", j].wait()
        serve(j)
        if j:
            close(j - 1)
        offer_groups()
        ring.tick(4)
    close(chunks - 1)
    while ring.queue:
        ring.tick(1, 1)
    ring.finish()
    for cp in outs[chunks - 1]:
        cp.wait()
    cp = pltpu.make_async_copy(k.GS, k.o_gain, k.load.at[0])
    cp.start()
    cp.wait()
    for j in range(chunks):
        rows = tokens_at(j)
        swap.wait_send(k.GA.at[rows], j)
        pltpu.make_async_copy(k.Wg.at[rows, pl.ds(0, 3 * width)], k.o_gqkv.at[rows], k.back.at[j]).wait()


def backward(n, fw):
    tokens, width = fw.o_x.shape
    ff = fw.o_hid.shape[1]
    chunks = tokens // CHUNK
    shard_rows = (ff // n, width // n)
    cuts = [256 * ((ff // 256 * i + 3) // 4) for i in range(5)]
    groups = [(cuts[i], cuts[i + 1] - cuts[i]) for i in range(4)]
    down = [p for p in pieces_of([(shard_rows[0], width)], (4,))]
    lanes = [
        [(0, down[i][1], down[i][2], 0, width // 2), (1, 0, shard_rows[1], groups[i][0], groups[i][1])] for i in range(4)
    ]
    most = (max(p[2] for lane in lanes for p in lane), max(p[4] for lane in lanes for p in lane))
    ring_vmem, ring_sems, landing = sum_scratch(n, lanes, most)
    square = (tokens, width)
    ins = dict(
        gy=fw.o_gy, n2=fw.o_n2, gu=fw.o_gu, wd=fw.o_wd, wg=fw.o_wg, wo=fw.o_wo, mid=fw.o_mid,
        qkv=fw.o_qkv, p=fw.o_p, cr=fw.o_cr, dwd=fw.o_dwd, sib=fw.o_sib, gain=fw.o_gain,
    )
    out = dict(
        o_gb=(square, BF), o_gm=(square, F32), o_gqkv=((tokens, 3 * width), BF), o_gain=((8, width), F32),
        o_own=((width, ff), BF), o_sib=((width, ff), BF), o_rwd=((2, shard_rows[0], width), BF),
        o_rwg=((2, shard_rows[1], 2 * ff), BF),
    )
    vmem = dict(
        GY=(square, BF), N2=(square, BF), GG=((tokens, 2 * ff), BF), Wg=((width, 2 * ff), BF),
        Wo=((width, width), BF), WT=((2, 256, width), BF), GT=((2, 2, 2, tokens // 2, 256), BF),
        DW=((3, 512, max(g[1] for g in groups)), BF), GN=((CHUNK, width), F32), MID=((CHUNK, width), F32),
        V=((CHUNK, width), BF), GM=((CHUNK, width), F32), GB=((CHUNK, width), BF), GA=(square, BF),
        CR=(square, BF), CS=(square, BF), P=((3, tokens, 128), F32), GP=((tokens, 128), F32),
        SS=((chunks, HEADS, CHUNK), F32), SR=((chunks, HEADS, CHUNK), F32), E=((width, 128), BF),
        G=((8, width), F32), GS=((8, width), F32), **ring_vmem,
    )
    sems = dict(
        tile=(2, 3), load=(8,), put=(2,), dw=(3,), dw_recv=(8,), again=(2, chunks), back=(chunks,),
        cross_send=(chunks,), cross_recv=(chunks,), score_send=(chunks,), score_recv=(chunks,), **ring_sems,
    )
    return call(backward_kernel, (n, lanes, shard_rows, groups, landing), ins, out, vmem, sems, 1)


def call(kernel, static, ins, out, vmem, sems, number):
    hbm = pl.BlockSpec(memory_space=pltpu.HBM)
    dma = pltpu.SemaphoreType.DMA
    names = list(ins) + list(out) + list(vmem) + list(sems)
    outs = pl.pallas_call(
        functools.partial(kernel, *static, names),
        out_shape=[jax.ShapeDtypeStruct(*o) for o in out.values()],
        in_specs=[hbm] * len(ins),
        out_specs=[hbm] * len(out),
        scratch_shapes=[pltpu.VMEM(*v) for v in vmem.values()] + [dma(v) for v in sems.values()],
        compiler_params=pltpu.CompilerParams(
            collective_id=number, has_side_effects=True, vmem_limit_bytes=64 * 2**20 - 2**16
        ),
        name=kernel.__name__,
    )(*ins.values())
    return Refs(list(out), outs)


def closing_kernel(n, lanes, shard_rows, landing, names, *refs):
    k = Refs(names, refs)
    spot = Spot(n)
    x, c = spot.x, spot.c
    tokens, width = k.N1.shape
    half, chunks = tokens // 2, tokens // CHUNK
    ff = k.HID.shape[1]
    loads = {}
    for i, (name, src, dst) in enumerate((
        ("att", k.att, k.ATT), ("gb", k.gb, k.GB), ("hid", k.hid, k.HID), ("wd", k.wd, k.Wd), ("n1", k.n1, k.N1),
        ("gqkv", k.gqkv, k.GQ), ("gain", k.gain, k.G), ("wq", k.wq, k.Wq), ("x", k.x, k.X), ("gs", k.gf, k.GF),
    )):
        loads[name] = pltpu.make_async_copy(src, dst, k.load.at[i])
        loads[name].start()
    k.GS[...] = jnp.zeros_like(k.GS)
    others = greet_all(spot)
    ring = Sums(
        spot, lanes, shard_rows, (width // 2, 3 * width // 2), (k.o_own, k.q_own), (k.o_sib, k.q_sib), (k.o_rwo, k.o_rwq),
        {p: getattr(k, name) for p, name in landing.items()}, k,
    )

    sends = []

    def row_chunk(i):
        j = i % (chunks // 2)
        block = (1 - x) if i < chunks // 2 else x
        return pl.ds(pl.multiple_of(block * half + j * CHUNK, CHUNK), CHUNK), pl.ds(j * CHUNK, CHUNK)

    def deliver(buf, whole, i, first):
        _, at = row_chunk(i)
        if i < chunks // 2:
            cp = remote(buf, whole.at[x, at], k.far_rows_send.at[first + i], k.far_rows_recv.at[first + i], spot.mate)
        else:
            cp = pltpu.make_async_copy(buf, whole.at[x, at], k.near_rows.at[first + i])
        cp.start()
        sends.append(cp)

    mids = {}

    def load_mid(i):
        rows, _ = row_chunk(i)
        mids[i] = pltpu.make_async_copy(k.mid.at[rows], k.MID.at[i % 2], k.rows.at[i % 2, 1])
        mids[i].start()

    grads_in = {}

    def load_grad(i):
        rows, _ = row_chunk(i)
        grads_in[i] = pltpu.make_async_copy(k.gm.at[rows], k.GM.at[i % 2], k.rows.at[i % 2, 0])
        grads_in[i].start()

    def output_chunk(i):
        rows, _ = row_chunk(i)
        for m in range(2):
            part = pl.ds(m * 512, 512)
            k.GN[:, part] = dot(k.HID[rows], k.Wd[:, part])
            ring.tick(1)
        mids[i].wait()
        k.OUT[i] = (k.MID[i % 2] + k.GN[...]).astype(BF)
        deliver(k.OUT.at[i], k.o_out, i, chunks)
        if i + 2 < chunks:
            load_mid(i + 2)

    def input_chunk(i):
        rows, _ = row_chunk(i)
        for m in range(4):
            part = pl.ds(m * 256, 256)
            k.GN[:, part] = dot_nt(k.GQ[rows], k.Wq[part])
            if m % 2:
                ring.tick(1)
        values, upstream = k.X[rows].astype(F32), k.GN[...]
        scale = rms_scale(values)
        k.GS[0:1] += jnp.sum(upstream * values * scale, axis=0, keepdims=True)
        grads_in[i].wait()
        k.IN[i] = (k.GM[i % 2] + norm_backward(values, scale, k.G[0:1], upstream)).astype(BF)
        deliver(k.IN.at[i], k.o_in, i, 0)
        ring.tick(1)
        if i + 2 < chunks:
            load_grad(i + 2)

    load_mid(0)
    load_mid(1)
    load_grad(0)
    load_grad(1)
    products = Products(spot, k, None)
    loads["att"].wait()
    loads["gb"].wait()
    waits = products.grid(k.ATT, k.GB, 0, width // 2, width // 2, 512, k.o_own, k.o_sib, 0, lambda: None)
    loads["hid"].wait()
    loads["wd"].wait()
    output_chunk(0)
    output_chunk(1)
    loads["n1"].wait()
    loads["gqkv"].wait()
    products.settle()
    for cp in waits:
        cp.wait_recv()
    ring.offer([p for lane in lanes for p in lane if p[0] == 0])
    queue = []
    cols = 3 * width // 4
    calls = []

    def offer_queued():
        products.settle()
        while queue:
            waits, pieces = queue.pop(0)
            for cp in waits:
                cp.wait_recv()
            ring.offer(pieces)

    def between():
        calls.append(0)
        if len(calls) == 6:
            offer_queued()
        ring.tick(1)

    for g in range(2):
        waits = products.grid(
            k.N1, k.GQ, g * cols, cols, 2 * cols, 512, k.q_own, k.q_sib, 2 + 2 * g, between
        )
        queue.append((waits, [p for lane in lanes for p in lane if p[0] == 1 and p[3] // cols == g]))
    offer_queued()

    loads["gain"].wait()
    loads["wq"].wait()
    loads["x"].wait()
    for i in range(chunks):
        input_chunk(i)
    for i in range(chunks // 2, chunks):
        output_chunk(i)
        ring.tick(2)
    part = width // n
    loads["gs"].wait()
    for j in range(n):
        k.GP[j] = jnp.zeros_like(k.GP[j])
        for row, ref in enumerate((k.GS, k.GF)):
            k.GP[j, pl.ds(row, 1)] = ref[0:1, j * part : (j + 1) * part]
    gains = []
    for i, who in enumerate(others):
        to = who[1]
        cp = remote(k.GP.at[to], k.GR.at[i], k.gain_send.at[i], k.gain_recv.at[i], who)
        cp.start()
        gains.append(cp)
    ring.tick(2)
    total = k.GP[spot.f]
    for i, cp in enumerate(gains):
        cp.wait()
        total = total + k.GR[i]
    k.GT[0] = total
    cp = remote(k.GT.at[0], k.GT.at[1], k.gain_send.at[n - 1], k.gain_recv.at[n - 1], spot.sib)
    cp.start()
    ring.tick(2)
    cp.wait()
    k.GT[2] = jnp.where(c == 0, k.GT[0], k.GT[1]) + jnp.where(c == 0, k.GT[1], k.GT[0])
    cp = remote(k.GT.at[2], k.o_gain.at[x], k.gain_send.at[n], k.gain_recv.at[n], spot.mate)
    cp.start()
    near = pltpu.make_async_copy(k.GT.at[2], k.o_gain.at[x], k.rows.at[0, 0])
    near.start()
    ring.finish()
    cp.wait()
    near.wait()
    for cp in sends:
        cp.wait()


def closing(n, fw, bw):
    tokens, width = fw.o_x.shape
    ff = fw.o_hid.shape[1]
    chunks = tokens // CHUNK
    shard_rows = (width // n, width // n)
    cols = 3 * width // 8
    lanes = [[(1, 0, shard_rows[1], i * cols, cols)] for i in range(4)] + [
        [(0, 0, shard_rows[0], i * width // 4, width // 4)] for i in range(2)
    ]
    most = (max(p[2] for lane in lanes for p in lane), max(p[4] for lane in lanes for p in lane))
    ring_vmem, ring_sems, landing = sum_scratch(n, lanes, most)
    square = (tokens, width)
    ins = dict(
        att=fw.o_att, gb=bw.o_gb, n1=fw.o_n1, gqkv=bw.o_gqkv, gain=fw.o_gain, wq=fw.o_wq, x=fw.o_x,
        hid=fw.o_hid, wd=fw.o_wd, gm=bw.o_gm, mid=fw.o_mid, gf=bw.o_gain,
    )
    out = dict(
        o_own=((width, width // 2), BF), o_sib=((width, width // 2), BF), q_own=((width, 3 * width // 2), BF),
        q_sib=((width, 3 * width // 2), BF), o_rwo=((2, shard_rows[0], width), BF),
        o_rwq=((2, shard_rows[1], 3 * width), BF), o_in=((2, tokens // 2, width), BF),
        o_out=((2, tokens // 2, width), BF), o_gain=((2, 8, width // n), F32),
    )
    vmem = dict(
        ATT=(square, BF), GB=(square, BF), N1=(square, BF), GQ=((tokens, 3 * width), BF), G=((8, width), F32),
        GS=((8, width), F32), GF=((8, width), F32), GP=((n, 8, width // n), F32), GR=((n - 1, 8, width // n), F32),
        GT=((3, 8, width // n), F32), Wq=((width, 3 * width), BF), X=(square, BF), HID=((tokens, ff), BF),
        Wd=((ff, width), BF), GN=((CHUNK, width), F32), GM=((2, CHUNK, width), F32), MID=((2, CHUNK, width), F32),
        IN=((chunks, CHUNK, width), BF), OUT=((chunks, CHUNK, width), BF), DW=((4, 512, 3 * width // 4), BF),
        **ring_vmem,
    )
    sems = dict(
        load=(10,), gain_send=(n + 1,), gain_recv=(n + 1,), rows=(2, 2), far_rows_send=(2 * chunks,), far_rows_recv=(2 * chunks,),
        near_rows=(2 * chunks,), dw=(4,), dw_recv=(6,), **ring_sems,
    )
    return call(closing_kernel, (n, lanes, shard_rows, landing), ins, out, vmem, sems, 2)


def valid_rows(item_lengths, frame_offsets):
    slot = jnp.arange(ITEM_SLOTS)[None, None, :]
    first = frame_offsets[:, :, None]
    valid = (slot >= first) & (slot < first + item_lengths[:, :, None])
    return valid.reshape(-1)


def by_position(n, block_input, out_grad, item_lengths, frame_offsets, norm_attn, w_qkv, w_out, norm_ffn, w_gate_up, w_down):
    x, c, f, r = place(n)
    micro, frames, positions, width = block_input.shape
    rows = micro * frames
    valid = valid_rows(item_lengths, frame_offsets)[:, None]
    inputs = block_input.reshape(rows, positions, width)
    upstream = jnp.where(valid[..., None], out_grad.reshape(rows, positions, width), 0)

    def take(array, at):
        return lax.dynamic_index_in_dim(array, at, 1, keepdims=False)

    gn = jnp.stack([norm_attn, norm_ffn], axis=1)
    gn = jnp.pad(lax.dynamic_index_in_dim(gn, x, 0, keepdims=False), ((0, 14), (0, 0)))
    fw = forward(
        n, take(inputs, 1 - x), take(inputs, x), take(upstream, 1 - x), take(upstream, x), w_qkv, w_out, w_gate_up, w_down, gn
    )
    bw = backward(n, fw)
    cl = closing(n, fw, bw)
    grads = [g.astype(F32) for g in (cl.o_rwq, cl.o_rwo, bw.o_rwg, bw.o_rwd)]
    def home(array):
        return array.transpose(1, 0, 2).reshape(micro, frames, positions, width)

    return home(cl.o_out), home(cl.o_in), cl.o_gain[:, 0], grads[0], grads[1], cl.o_gain[:, 1], grads[2], grads[3]


def shortened(x):

    def short(part):
        return part.astype(jnp.bfloat16) if part.dtype == jnp.float32 else part

    return jax.tree.map(short, x)


PRECISE = lax.Precision.HIGHEST
matmul, times_transposed, contract_rows = dot, dot_nt, dot_tn


def by_weights(
    block_input,
    out_grad,
    item_lengths,
    frame_offsets,
    norm_attn,
    w_qkv,
    w_out,
    norm_ffn,
    w_gate_up,
    w_down,
):
    micro, frames, positions, model_width = block_input.shape
    head_dim = model_width // HEADS
    hidden_size = w_gate_up.shape[2] // 2
    head_shape = (frames, positions, HEADS, head_dim)
    slot_index = jnp.arange(ITEM_SLOTS)[None, None, :]
    first_slot = frame_offsets[:, :, None]
    valid_rows = (slot_index >= first_slot) & (slot_index < first_slot + item_lengths[:, :, None])
    valid_rows = valid_rows.astype(jnp.float32).reshape(micro, frames)
    causal = jnp.arange(positions)[:, None] >= jnp.arange(positions)[None, :]
    totals = (
        jnp.zeros((positions, model_width), jnp.float32),
        jnp.zeros((positions, model_width, 3 * model_width), jnp.float32),
        jnp.zeros((positions, model_width, model_width), jnp.float32),
        jnp.zeros((positions, model_width), jnp.float32),
        jnp.zeros((positions, model_width, 2 * hidden_size), jnp.float32),
        jnp.zeros((positions, hidden_size, model_width), jnp.float32),
    )
    output_list = []
    input_grad_list = []
    for batch_index in range(micro):
        inputs = block_input[batch_index].astype(jnp.float32)
        qkv_all, gain_in_all = (
            lax.all_gather(w_qkv, "fsdp", axis=1, tiled=True),
            lax.all_gather(norm_attn, "fsdp", axis=1, tiled=True),
        )
        first_saved = []
        qkv_list = []
        for place in range(positions):
            rows = inputs[:, place]
            scale_one = rms_scale(rows)
            normed = (rows * scale_one * gain_in_all[place]).astype(jnp.bfloat16)
            first_saved.append((scale_one, normed))
            qkv_list.append(matmul(normed, qkv_all[place]).astype(jnp.bfloat16))
        qkv_proj = jnp.stack(qkv_list, axis=1)
        query_heads = qkv_proj[..., :model_width].reshape(head_shape)
        key_heads = qkv_proj[..., model_width : 2 * model_width].reshape(head_shape)
        value_heads = qkv_proj[..., 2 * model_width :].reshape(head_shape)
        scores = jnp.einsum(
            "fihd,fjhd->fhij", query_heads, key_heads, preferred_element_type=jnp.float32
        ) / math.sqrt(head_dim)
        scores = jnp.where(causal, scores, -1e30)
        attention = jax.nn.softmax(scores, axis=-1)
        attention_low = attention.astype(jnp.bfloat16)
        mixed_heads = jnp.einsum(
            "fhij,fjhd->fihd", attention_low, value_heads, preferred_element_type=jnp.float32
        )
        mixed_heads = mixed_heads.reshape(frames, positions, model_width).astype(jnp.bfloat16)
        out_all, gain_two_all, gu_all, down_all = (
            lax.all_gather(w_out, "fsdp", axis=1, tiled=True),
            lax.all_gather(norm_ffn, "fsdp", axis=1, tiled=True),
            lax.all_gather(w_gate_up, "fsdp", axis=1, tiled=True),
            lax.all_gather(w_down, "fsdp", axis=1, tiled=True),
        )
        second_saved = []
        output_rows = []
        for place in range(positions):
            middle = inputs[:, place] + matmul(mixed_heads[:, place], out_all[place])
            scale_two = rms_scale(middle)
            normed_two = (middle * scale_two * gain_two_all[place]).astype(jnp.bfloat16)
            gate_up = matmul(normed_two, gu_all[place])
            hidden = (jax.nn.silu(gate_up[:, :hidden_size]) * gate_up[:, hidden_size:]).astype(
                jnp.bfloat16
            )
            second_saved.append((middle, scale_two, normed_two, gate_up, hidden))
            output_rows.append((middle + matmul(hidden, down_all[place])).astype(jnp.bfloat16))
        output_list.append(jnp.stack(output_rows, axis=1))
        upstream = (
            out_grad[batch_index].astype(jnp.float32) * valid_rows[batch_index][:, None, None]
        )
        out_all, gain_two_all, gu_all, down_all = (
            lax.all_gather(w_out, "fsdp", axis=1, tiled=True),
            lax.all_gather(norm_ffn, "fsdp", axis=1, tiled=True),
            lax.all_gather(w_gate_up, "fsdp", axis=1, tiled=True),
            lax.all_gather(w_down, "fsdp", axis=1, tiled=True),
        )
        out_grads = []
        gain_two_grads = []
        gu_grads = []
        down_grads = []
        middle_grads = []
        attn_grads = []
        for place in range(positions):
            middle, scale_two, normed_two, gate_up, hidden = second_saved[place]
            gate = gate_up[:, :hidden_size]
            up_part = gate_up[:, hidden_size:]
            grad_ffn = upstream[:, place].astype(jnp.bfloat16)
            down_grads.append(contract_rows(hidden, grad_ffn))
            grad_hidden = times_transposed(grad_ffn, down_all[place])
            sigma = jax.nn.sigmoid(gate)
            grad_gate = grad_hidden * up_part * sigma * (1.0 + gate * (1.0 - sigma))
            grad_up = grad_hidden * jax.nn.silu(gate)
            grad_gate_up = jnp.concatenate([grad_gate, grad_up], axis=-1).astype(jnp.bfloat16)
            gu_grads.append(contract_rows(normed_two, grad_gate_up))
            grad_normed_two = times_transposed(grad_gate_up, gu_all[place])
            gain_two_grads.append(jnp.sum(grad_normed_two * middle * scale_two, axis=0))
            grad_middle = upstream[:, place] + norm_backward(
                middle, scale_two, gain_two_all[place], grad_normed_two
            )
            grad_branch = grad_middle.astype(jnp.bfloat16)
            out_grads.append(contract_rows(mixed_heads[:, place], grad_branch))
            attn_grads.append(times_transposed(grad_branch, out_all[place]).astype(jnp.bfloat16))
            middle_grads.append(grad_middle)
        grad_mixed = jnp.stack(attn_grads, axis=1).reshape(head_shape)
        grad_attention = jnp.einsum(
            "fihd,fjhd->fhij", grad_mixed, value_heads, preferred_element_type=jnp.float32
        )
        grad_values = jnp.einsum(
            "fhij,fihd->fjhd", attention_low, grad_mixed, preferred_element_type=jnp.float32
        )
        grad_scores = attention * (
            grad_attention - jnp.sum(attention * grad_attention, axis=-1, keepdims=True)
        )
        grad_scores = grad_scores / math.sqrt(head_dim)
        grad_query = jnp.einsum(
            "fhij,fjhd->fihd", grad_scores, key_heads.astype(jnp.float32), precision=PRECISE
        )
        grad_keys = jnp.einsum(
            "fhij,fihd->fjhd", grad_scores, query_heads.astype(jnp.float32), precision=PRECISE
        )
        flat_shape = (frames, positions, model_width)
        grad_qkv = jnp.concatenate(
            [
                grad_query.reshape(flat_shape),
                grad_keys.reshape(flat_shape),
                grad_values.reshape(flat_shape),
            ],
            axis=-1,
        ).astype(jnp.bfloat16)
        qkv_all, gain_in_all = (
            lax.all_gather(w_qkv, "fsdp", axis=1, tiled=True),
            lax.all_gather(norm_attn, "fsdp", axis=1, tiled=True),
        )
        qkv_grads = []
        gain_one_grads = []
        input_rows = []
        for place in range(positions):
            scale_one, normed = first_saved[place]
            rows = inputs[:, place]
            qkv_grads.append(contract_rows(normed, grad_qkv[:, place]))
            grad_normed = times_transposed(grad_qkv[:, place], qkv_all[place])
            gain_one_grads.append(jnp.sum(grad_normed * rows * scale_one, axis=0))
            input_rows.append(
                (
                    middle_grads[place]
                    + norm_backward(rows, scale_one, gain_in_all[place], grad_normed)
                ).astype(jnp.bfloat16)
            )
        input_grad_list.append(jnp.stack(input_rows, axis=1))
        batch_grads = (
            jnp.stack(gain_one_grads),
            jnp.stack(qkv_grads),
            jnp.stack(out_grads),
            jnp.stack(gain_two_grads),
            jnp.stack(gu_grads),
            jnp.stack(down_grads),
        )
        totals = tuple((total + update for total, update in zip(totals, batch_grads)))
    totals = (
        lax.psum_scatter(totals[0], "fsdp", scatter_dimension=1, tiled=True),
        lax.psum_scatter(totals[1], "fsdp", scatter_dimension=1, tiled=True),
        lax.psum_scatter(totals[2], "fsdp", scatter_dimension=1, tiled=True),
        lax.psum_scatter(totals[3], "fsdp", scatter_dimension=1, tiled=True),
        lax.psum_scatter(totals[4], "fsdp", scatter_dimension=1, tiled=True),
        lax.psum_scatter(totals[5], "fsdp", scatter_dimension=1, tiled=True),
    )
    totals = jax.tree.map(lambda part: part.astype(jnp.float32), lax.psum(shortened(totals), "dp"))
    return (
        jnp.stack(output_list),
        jnp.stack(input_grad_list),
        totals[0],
        totals[1],
        totals[2],
        totals[3],
        totals[4],
        totals[5],
    )


def fits(mesh, shapes):
    return mesh.shape["dp"] == 4 and all(s[1] % 16 == 0 for s in shapes) and shapes[0][1] % 128 == 0


def solution(mesh):
    n = mesh.shape["fsdp"]

    def on_device(*args):
        if fits(mesh, [args[k].shape for k in (5, 6, 8, 9)]):
            return by_position(n, *args)
        return by_weights(*args)

    placed = (
        P(None, ("dp", "fsdp"), None, None),
        P(None, ("dp", "fsdp"), None, None),
        P(None, ("dp", "fsdp")),
        P(None, ("dp", "fsdp")),
        P(None, "fsdp"),
        P(None, "fsdp", None),
        P(None, "fsdp", None),
        P(None, "fsdp"),
        P(None, "fsdp", None),
        P(None, "fsdp", None),
    )
    return jax.shard_map(
        on_device,
        mesh=mesh,
        in_specs=placed,
        out_specs=(
            P(None, ("dp", "fsdp"), None, None),
            P(None, ("dp", "fsdp"), None, None),
            P(None, "fsdp"),
            P(None, "fsdp", None),
            P(None, "fsdp", None),
            P(None, "fsdp"),
            P(None, "fsdp", None),
            P(None, "fsdp", None),
        ),
        check_vma=False,
    )
```

```python
import functools
import math

import jax
import jax.numpy as jnp
from jax import lax
from jax.experimental import pallas as pl
from jax.experimental.pallas import tpu as pltpu
from jax.sharding import PartitionSpec as P

MESH = pl.DeviceIdType.MESH
BF = jnp.bfloat16
F32 = jnp.float32
HEADS = 16
ITEM_SLOTS = 32
EPSILON = 1e-05
LANES = 3
AXES = ("dp", "fsdp")


def rem(a, b):
    return a % b if isinstance(a, int) else lax.rem(a, b)


def div(a, b):
    return a // b if isinstance(a, int) else lax.div(a, b)


def place(n):
    dp, f = lax.axis_index("dp"), lax.axis_index("fsdp")
    x, c = lax.div(dp, 2), lax.rem(dp, 2)
    z, h = lax.div(f, 2), lax.rem(f, 2)
    r = z * (1 - h) + (n - 1 - z) * h
    return x, c, f, r


def ring_index(r, n):
    hh = lax.div(r, n // 2)
    return (2 * r) * (1 - hh) + (2 * (n - 1 - r) + 1) * hh


class Spot:
    def __init__(self, n):
        self.n = n
        x, c, f, r = place(n)
        self.x, self.c, self.f, self.r = x, c, f, r
        self.d = 1 - 2 * c
        dp = 2 * x + c
        self.next = (dp, ring_index(lax.rem(r + self.d + n, n), n))
        self.prev = (dp, ring_index(lax.rem(r - self.d + n, n), n))
        self.sib = (2 * x + 1 - c, f)
        self.mate = (2 * (1 - x) + c, f)

    def owner(self, hop):
        return ring_index(lax.rem(self.r - self.d * (hop + 1) + self.n, self.n), self.n)

    def greet(self):
        barrier = pltpu.get_barrier_semaphore()
        for who in (self.next, self.prev, self.sib, self.mate):
            pl.semaphore_signal(barrier, inc=1, device_id=who, device_id_type=MESH)
        pl.semaphore_wait(barrier, 4)


def remote(src, dst, send, recv, who):
    return pltpu.make_async_remote_copy(src, dst, send, recv, device_id=who, device_id_type=MESH)


def pieces_of(shapes, parts):
    out = []
    for a, (shape, count) in enumerate(zip(shapes, parts)):
        tiles = shape[0] // 16
        cuts = [16 * (tiles * k // count) for k in range(count + 1)]
        for k in range(count):
            out.append((a, cuts[k], cuts[k + 1] - cuts[k], shape[1] // 2))
    return out


def lanes_of(pieces):
    return [pieces[k::LANES] for k in range(LANES)]


class Weights:
    def __init__(self, spot, lanes, shard_rows, shards, wholes, ring_send, ring_recv, sib_send, sib_recv):
        self.spot, self.lanes, self.shard_rows = spot, lanes, shard_rows
        self.shards, self.wholes = shards, wholes
        self.sems = ring_send, ring_recv, sib_send, sib_recv
        self.hops = spot.n - 1
        self.total = [len(lane) * self.hops for lane in lanes]
        self.events = [(lane, t) for t in range(max(self.total)) for lane in range(len(lanes)) if t < self.total[lane]]
        self.flying, self.sent, self.handed = {}, [], []

    def block(self, piece, owner):
        a, first, rows, cols = piece
        return self.wholes[a].at[pl.ds(owner * self.shard_rows[a] + first, rows), pl.ds(self.spot.c * cols, cols)]

    def send(self, lane, t):
        piece, hop = self.lanes[lane][t // self.hops], t % self.hops
        a, first, rows, cols = piece
        spot = self.spot
        if hop == 0:
            src = self.shards[a].at[spot.x, pl.ds(first, rows), pl.ds(spot.c * cols, cols)]
            dst = self.block(piece, spot.f)
        else:
            src = dst = self.block(piece, spot.owner(hop - 1))
        cp = remote(src, dst, self.sems[0].at[lane, t], self.sems[1].at[lane, t], spot.next)
        cp.start()
        self.flying[lane] = cp

    def start(self):
        for lane in range(len(self.lanes)):
            self.send(lane, 0)

    def tick(self, count):
        for lane, t in self.events[:count]:
            self.flying[lane].wait_recv()
            self.sent.append(self.flying[lane])
            if t + 1 < self.total[lane]:
                self.send(lane, t + 1)
            piece, hop = self.lanes[lane][t // self.hops], t % self.hops
            here = self.block(piece, self.spot.owner(hop))
            cp = remote(here, here, self.sems[2].at[lane, t], self.sems[3].at[lane, t], self.spot.sib)
            cp.start()
            self.handed.append((piece[0], cp))
        self.events = self.events[count:]

    def until(self, array):
        while any(self.lanes[lane][t // self.hops][0] <= array for lane, t in self.events):
            self.tick(1)
        later = []
        for a, cp in self.handed:
            if a <= array:
                cp.wait_recv()
                self.sent.append(cp)
            else:
                later.append((a, cp))
        self.handed = later

    def finish(self):
        for cp in self.sent:
            cp.wait_send()


def dot(left, right):
    return jnp.dot(left, right, preferred_element_type=F32)


def dot_nt(left, right):
    return lax.dot_general(left, right, (((1,), (1,)), ((), ())), preferred_element_type=F32)


def dot_tn(left, right):
    return lax.dot_general(left, right, (((0,), (0,)), ((), ())), preferred_element_type=F32)


def rms_scale(values):
    return lax.rsqrt(jnp.mean(values * values, axis=-1, keepdims=True) + EPSILON)


def norm_backward(values, scale, gain, upstream):
    weighted = gain * upstream
    return scale * weighted - values * scale**3 * jnp.mean(values * weighted, axis=-1, keepdims=True)


def head_table(ref):
    width = ref.shape[0]
    rows = lax.broadcasted_iota(jnp.int32, ref.shape, 0)
    cols = lax.broadcasted_iota(jnp.int32, ref.shape, 1)
    ref[...] = (lax.div(rows, width // HEADS) == cols).astype(F32).astype(BF)


def per_head(product, table):
    high = product.astype(BF)
    rest = (product - high.astype(F32)).astype(BF)
    return dot(high, table[...]) + dot(rest, table[...])


def spread(per, table):
    return dot_nt(per, table[...])


def spread_two(per, table):
    high = per.astype(BF)
    rest = (per - high.astype(F32)).astype(BF)
    return dot_nt(high, table[...]) + dot_nt(rest, table[...])


def pair(a, b):
    top = jnp.maximum(a, b)
    ea, eb = jnp.exp(a - top), jnp.exp(b - top)
    return ea / (ea + eb), eb / (ea + eb)


def flat(scores):
    return scores.T[:HEADS]


def tall(scores):
    return jnp.concatenate([scores, jnp.zeros((128 - HEADS, scores.shape[1]), F32)], axis=0).T


CHUNK = 256


class Refs:
    def __init__(self, names, refs):
        assert len(names) == len(refs)
        self.__dict__.update(zip(names, refs))


def forward_kernel(n, lanes, shard_rows, names, *refs):
    k = Refs(names, refs)
    spot = Spot(n)
    x, c, f = spot.x, spot.c, spot.f
    tokens, width = k.X.shape
    half, chunks = tokens // 2, tokens // CHUNK
    ff = k.HID.shape[1]
    position_one = x == 1
    ring = Weights(
        spot, lanes, shard_rows, (k.wq, k.wo, k.wg, k.wd), (k.Wq, k.Wo, k.Wg, k.Wd),
        k.ring_send, k.ring_recv, k.sib_send, k.sib_recv,
    )

    local = []
    for i, (src, dst) in enumerate((
        (k.xo, k.X.at[pl.ds(x * half, half)]),
        (k.gn, k.GA.at[f]),
        (k.wq.at[x], k.Wq.at[pl.ds(f * shard_rows[0], shard_rows[0])]),
        (k.wo.at[x], k.Wo.at[pl.ds(f * shard_rows[1], shard_rows[1])]),
        (k.wg.at[x], k.Wg.at[pl.ds(f * shard_rows[2], shard_rows[2])]),
        (k.wd.at[x], k.Wd.at[pl.ds(f * shard_rows[3], shard_rows[3])]),
        (k.go, k.GY.at[pl.ds(x * half, half)]),
    )):
        cp = pltpu.make_async_copy(src, dst, k.loc.at[i])
        cp.start()
        local.append(cp)

    others = greet_all(spot)

    gains = []
    for i, who in enumerate(others):
        cp = remote(k.gn, k.GA.at[f], k.gain_send.at[i], k.gain_recv.at[i], who)
        cp.start()
        gains.append(cp)
    ring.start()
    swaps = [
        remote(src, dst.at[pl.ds(x * half, half)], k.swap_send.at[i], k.swap_recv.at[i], spot.mate)
        for i, (src, dst) in enumerate(((k.xs, k.X), (k.gs, k.GY)))
    ]
    swaps[0].start()

    @pl.when(x == 0)
    def _():
        swaps[1].start()

    outs = []

    def put(src, dst):
        cp = pltpu.make_async_copy(src, dst, k.put.at[len(outs)])
        cp.start()
        outs.append(cp)
        return cp

    head_table(k.E)
    k.G[...] = jnp.zeros_like(k.G)
    local[0].wait()
    local[1].wait()
    for cp in gains:
        cp.wait()
    for j in range(n):
        block = k.GA[j].astype(F32)
        for row in range(2):
            k.G[pl.ds(row, 1), pl.ds(j * 128, 128)] = block[row : row + 1]
    put(k.G, k.o_gain)

    def rows_of(j):
        return pl.ds(pl.multiple_of(j * CHUNK, CHUNK), CHUNK)

    def first_norm(at):
        def step(i, carry):
            rows = pl.ds(pl.multiple_of(at * half + i * CHUNK, CHUNK), CHUNK)
            values = k.X[rows].astype(F32)
            k.N1[rows] = (values * rms_scale(values) * k.G[0:1]).astype(BF)
            return carry

        lax.fori_loop(0, half // CHUNK, step, 0)

    ring.tick(4)
    first_norm(x)
    ring.tick(14)
    swaps[0].wait()
    first_norm(1 - x)
    put(k.X, k.o_x)
    put(k.N1, k.o_n1)
    local[2].wait()
    local[3].wait()
    ring.until(1)
    put(k.Wq, k.o_wq)
    put(k.Wo, k.o_wo)

    def project(first, count):
        def step(i, carry):
            cols = pl.ds(pl.multiple_of(first + i * 256, 256), 256)
            k.QKV[:, cols] = dot(k.N1[...], k.Wq[:, cols]).astype(BF)
            return carry

        lax.fori_loop(0, count // 256, step, 0)

    def across(src, j):
        return remote(src, k.CR.at[rows_of(j)], k.cross_send.at[j], k.cross_recv.at[j], spot.mate)

    def across_scores(j):
        return remote(k.SS.at[j], k.SR.at[j], k.score_send.at[j], k.score_recv.at[j], spot.mate)

    def query(j):
        return k.QKV.at[rows_of(j), pl.ds(0, width)]

    scaling = 1.0 / math.sqrt(width // HEADS)

    def own_score(j):
        rows = rows_of(j)
        q, key = k.QKV[rows, 0:width].astype(F32), k.QKV[rows, width : 2 * width].astype(F32)
        score = per_head(q * key, k.E) * scaling
        k.S[rows] = score

        @pl.when(position_one)
        def _():
            k.SS[j] = flat(score)
            across_scores(j).start()
            if j + 1 < chunks:
                across(query(j + 1), j + 1).start()
            else:
                swaps[1].start()

    def serve(j):
        @pl.when(x == 0)
        def _():
            rows = rows_of(j)
            across(query(j), j).wait_recv()
            across_scores(j).wait_recv()
            score = per_head(k.CR[rows].astype(F32) * k.QKV[rows, width : 2 * width].astype(F32), k.E) * scaling
            k.SS[j] = flat(score)
            across_scores(j).start()
            here, there = pair(score, tall(k.SR[j]))
            k.PR[1, rows] = here
            k.PR[2, rows] = there
            part = spread(here.astype(BF), k.E) * k.QKV[rows, 2 * width : 3 * width].astype(F32)
            k.CS[rows] = part.astype(BF)
            across(k.CS.at[rows], j).start()

    mids = {}

    def attend(j):
        rows = rows_of(j)

        @pl.when(position_one)
        def _():
            across(query(j), j).wait_recv()
            across_scores(j).wait_recv()

        other = jnp.where(position_one, tall(k.SR[j]), -1e30)
        here, there = pair(k.S[rows], other)
        k.PR[0, rows] = here
        mixed = spread(here.astype(BF), k.E) * k.QKV[rows, 2 * width : 3 * width].astype(F32)
        mixed = mixed + jnp.where(position_one, k.CR[rows].astype(F32), 0.0)
        k.ATT[rows] = mixed.astype(BF)
        if j - 2 in mids:
            mids[j - 2].wait()
        middle = k.X[rows].astype(F32) + dot(k.ATT[rows], k.Wo[...])
        k.MID[j % 2] = middle
        k.N2[rows] = (middle * rms_scale(middle) * k.G[1:2]).astype(BF)
        cp = pltpu.make_async_copy(k.MID.at[j % 2], k.o_mid.at[rows], k.mid.at[j % 2])
        cp.start()
        mids[j] = cp

    project(0, width // 2)
    ring.tick(1)
    project(width // 2, width // 2)

    @pl.when(position_one)
    def _():
        across(query(0), 0).start()

    ring.tick(2)
    project(width, width // 2)
    ring.tick(1)
    project(width + width // 2, width // 2)
    ring.tick(1)
    for j in range(chunks):
        own_score(j)
        ring.tick(1)
    project(2 * width, width)
    put(k.QKV, k.o_qkv)
    ring.tick(2)

    serve(0)
    ring.tick(4)
    serve(1)
    ring.tick(1)
    attend(0)
    ring.tick(4)
    serve(2)
    ring.tick(1)
    attend(1)
    ring.tick(4)
    local[4].wait()
    ring.until(2)
    put(k.Wg, k.o_wg)
    serve(3)

    def gate_copies(step):
        slot = rem(step, 2)
        for part in range(2):
            yield pltpu.make_async_copy(k.GU.at[slot, part], k.o_gu.at[step, part], k.gu.at[slot, part])

    def feed(h, first, last):
        def step(t, carry):
            rows = pl.ds(h * half, half)
            at = h * (ff // 256) + t
            slot = lax.rem(at, 2)
            gate = dot(k.N2[rows], k.Wg[:, pl.ds(pl.multiple_of(t * 256, 256), 256)])
            up = dot(k.N2[rows], k.Wg[:, pl.ds(pl.multiple_of(ff + t * 256, 256), 256)])
            k.HID[rows, pl.ds(pl.multiple_of(t * 256, 256), 256)] = (gate * jax.nn.sigmoid(gate) * up).astype(BF)

            @pl.when(at >= 2)
            def _():
                for cp in gate_copies(at - 2):
                    cp.wait()

            k.GU[slot, 0] = gate.astype(BF)
            k.GU[slot, 1] = up.astype(BF)
            for cp in gate_copies(at):
                cp.start()
            return carry

        lax.fori_loop(first, last, step, 0)

    tiles = ff // 256
    for t in range(tiles):
        feed(0, t, t + 1)
        ring.tick(1)
        if t == 7:
            attend(2)
            ring.tick(1)
    attend(3)
    put(k.N2, k.o_n2)
    put(k.ATT, k.o_att)
    put(k.PR, k.o_p)
    for t in range(tiles):
        feed(1, t, t + 1)
        ring.tick(1)
    put(k.HID, k.o_hid)
    local[6].wait()
    swaps[1].wait()
    put(k.GY, k.o_gy)

    cols = width // 2

    def down_copies(m):
        slot = rem(m, 4)
        rows = pl.ds(pl.multiple_of(m * 256, 256), 256)
        theirs = remote(
            k.DW.at[slot, :, pl.ds(pl.multiple_of((1 - c) * cols, cols), cols)],
            k.o_sib.at[rows], k.down_send.at[slot], k.down_recv.at[m], spot.sib,
        )
        ours = pltpu.make_async_copy(
            k.DW.at[slot, :, pl.ds(pl.multiple_of(c * cols, cols), cols)], k.o_dwd.at[rows], k.down.at[slot]
        )
        return theirs, ours

    def down_grad(first, last):
        def step(m, carry):
            part = dot_tn(k.HID[:, pl.ds(pl.multiple_of(m * 256, 256), 256)], k.GY[...]).astype(BF)

            @pl.when(m >= 4)
            def _():
                theirs, ours = down_copies(m - 4)
                theirs.wait_send()
                ours.wait()

            k.DW[lax.rem(m, 4)] = part
            for cp in down_copies(m):
                cp.start()
            return carry

        lax.fori_loop(first, last, step, 0)

    for m in range(tiles):
        down_grad(m, m + 1)
        ring.tick(1)
    local[5].wait()
    ring.until(3)
    put(k.Wd, k.o_wd)
    for m in range(tiles - 4, tiles):
        theirs, ours = down_copies(m)
        theirs.wait_send()
        ours.wait()
    for m in range(tiles):
        down_copies(m)[0].wait_recv()
    put(k.CR, k.o_cr)
    for at in (2 * tiles - 2, 2 * tiles - 1):
        for cp in gate_copies(at):
            cp.wait()
    for j in (chunks - 2, chunks - 1):
        mids[j].wait()
    for j in range(chunks):
        across(query(j), j).wait_send()
        across_scores(j).wait_send()
    ring.finish()
    for cp in outs:
        cp.wait()


def forward(n, xs, xo, gs, go, wq, wo, wg, wd, gn):
    weights = (wq, wo, wg, wd)
    shapes = [w.shape[1:] for w in weights]
    parts = [
        [p for p in pieces_of(shapes, (4, 1, 4, 4)) if p[0] == a] for a in range(4)
    ]
    lanes = [[parts[0][i], parts[2][i], parts[3][i]] for i in range(4)] + [parts[1]]
    steps = 3 * (n - 1)
    half, width = xo.shape
    tokens, ff = 2 * half, wd.shape[1] * n
    tiles, chunks = ff // 256, tokens // CHUNK
    wholes = [(s[0] * n, s[1]) for s in shapes]
    square = (tokens, width)
    out = dict(
        o_wq=(wholes[0], BF), o_wo=(wholes[1], BF), o_wg=(wholes[2], BF), o_wd=(wholes[3], BF),
        o_x=(square, BF), o_gy=(square, BF), o_n1=(square, BF), o_qkv=((tokens, 3 * width), BF),
        o_cr=(square, BF), o_p=((3, tokens, 128), F32), o_att=(square, BF), o_mid=(square, F32),
        o_n2=(square, BF), o_gu=((2 * tiles, 2, half, 256), BF), o_hid=((tokens, ff), BF),
        o_dwd=((ff, width // 2), BF), o_sib=((ff, width // 2), BF), o_gain=((8, width), F32),
    )
    vmem = dict(
        Wq=(wholes[0], BF), Wo=(wholes[1], BF), Wg=(wholes[2], BF), Wd=(wholes[3], BF),
        X=(square, BF), GY=(square, BF), N1=(square, BF), QKV=((tokens, 3 * width), BF),
        CR=(square, BF), CS=(square, BF), ATT=(square, BF), MID=((2, CHUNK, width), F32),
        N2=(square, BF), GU=((2, 2, half, 256), BF), HID=((tokens, ff), BF), DW=((4, 256, width), BF),
        E=((width, 128), BF), G=((8, width), F32), GA=((n, 16, 128), BF), S=((tokens, 128), F32),
        SS=((chunks, HEADS, CHUNK), F32), SR=((chunks, HEADS, CHUNK), F32), PR=((3, tokens, 128), F32),
    )
    sems = dict(
        ring_send=(len(lanes), steps), ring_recv=(len(lanes), steps), sib_send=(len(lanes), steps),
        sib_recv=(len(lanes), steps), loc=(7,), gain_send=(n - 1,), gain_recv=(n - 1,),
        swap_send=(2,), swap_recv=(2,), put=(20,), cross_send=(chunks,), cross_recv=(chunks,),
        score_send=(chunks,), score_recv=(chunks,), mid=(2,), gu=(2, 2), down_send=(4,),
        down_recv=(tiles,), down=(4,),
    )
    ins = dict(xs=xs, xo=xo, gs=gs, go=go, wq=wq, wo=wo, wg=wg, wd=wd, gn=gn)
    return call(forward_kernel, (n, lanes, [s[0] for s in shapes]), ins, out, vmem, sems, 0)


class Sums:
    def __init__(self, spot, lanes, shard_rows, half_cols, ours, theirs, outs, landing, k):
        self.spot, self.lanes, self.shard_rows, self.half_cols = spot, lanes, shard_rows, half_cols
        self.ours, self.theirs, self.outs, self.landing, self.k = ours, theirs, outs, landing, k
        self.hops = spot.n - 1
        self.ready = set()
        self.loaded = [0] * len(lanes)
        self.used = [0] * len(lanes)
        self.flying = [None] * len(lanes)
        self.at = [0] * len(lanes)
        self.first = [None] * len(lanes)
        self.queue, self.sent, self.tail, self.mates = [], [], [], []
        self.count = 0

    def term_copies(self, lane, u):
        piece = self.lanes[lane][u // (self.hops + 1)]
        a, row, rows, col, cols = piece
        owner = self.spot.owner(u % (self.hops + 1))
        at = (pl.ds(owner * self.shard_rows[a] + row, rows), pl.ds(col, cols))
        for side, ref in enumerate((self.ours[a], self.theirs[a])):
            dst = self.k.TERM.at[lane, u % 2, side, pl.ds(0, rows), pl.ds(0, cols)]
            yield pltpu.make_async_copy(ref.at[at], dst, self.k.term.at[lane, u % 2, side])

    def prefetch(self, lane):
        per = self.hops + 1
        while self.loaded[lane] < min(self.used[lane] + 2, per * len(self.lanes[lane])):
            u = self.loaded[lane]
            if self.lanes[lane][u // per] not in self.ready:
                return
            for cp in self.term_copies(lane, u):
                cp.start()
            self.loaded[lane] += 1

    def term(self, lane):
        u = self.used[lane]
        assert u < self.loaded[lane]
        _, _, rows, _, cols = self.lanes[lane][u // (self.hops + 1)]
        for cp in self.term_copies(lane, u):
            cp.wait()
        ours, theirs = (self.k.TERM[lane, u % 2, side, 0:rows, 0:cols].astype(F32) for side in range(2))
        return ours + theirs

    def step(self, lane):
        t = self.at[lane]
        if t == self.hops * len(self.lanes[lane]):
            return
        piece = self.lanes[lane][t // self.hops]
        if piece not in self.ready:
            self.flying[lane] = None
            return
        hop = t % self.hops
        slots = self.landing[piece]
        value = self.term(lane)
        if hop == 0:
            if self.first[lane] is not None:
                self.first[lane].wait_send()
            buf = self.k.FIRST.at[lane, pl.ds(0, piece[2]), pl.ds(0, piece[4])]
        else:
            buf = slots.at[hop - 1]
            value = value + buf[...].astype(F32)
        buf[...] = value.astype(BF)
        self.used[lane] += 1
        cp = remote(buf, slots.at[hop], self.k.ring_send.at[lane, t], self.k.ring_recv.at[lane, t], self.spot.next)
        cp.start()
        self.prefetch(lane)
        if hop == 0:
            self.first[lane] = cp
        else:
            self.sent.append(cp)
        self.flying[lane] = cp
        self.at[lane] += 1
        self.queue.append(lane)

    def offer(self, pieces):
        self.ready.update(pieces)
        for lane in range(len(self.lanes)):
            if self.flying[lane] is None and self.at[lane] < self.hops * len(self.lanes[lane]):
                self.prefetch(lane)
                self.step(lane)
            else:
                self.prefetch(lane)

    def finish_piece(self, lane, piece):
        a, row, rows, col, cols = piece
        spot, k, i = self.spot, self.k, self.count
        self.count += 1
        end = self.landing[piece].at[self.hops - 1]
        end[...] = (end[...].astype(F32) + self.term(lane)).astype(BF)
        self.used[lane] += 1
        self.prefetch(lane)
        at = (pl.ds(row, rows), pl.ds(spot.c * self.half_cols[a] + col, cols))
        place = self.outs[a].at[(spot.x,) + at]
        cp = pltpu.make_async_copy(end, place, k.end.at[i])
        cp.start()
        self.tail.append(cp)
        cp = remote(end, place, k.end_sib_send.at[i], k.end_sib_recv.at[i], spot.sib)
        cp.start()
        self.tail.append(cp)
        cp = remote(end, place, k.end_mate_send.at[i], k.end_mate_recv.at[i], spot.mate)
        cp.start()
        self.mates.append((cp, self.outs[a].at[(1 - spot.x,) + at], i))

    def pass_on(self, keep):
        while len(self.mates) > keep:
            cp, place, i = self.mates.pop(0)
            cp.wait()
            far = remote(place, place, self.k.far_send.at[i], self.k.far_recv.at[i], self.spot.sib)
            far.start()
            self.tail.append(far)

    def tick(self, count, least=3):
        for _ in range(count):
            if len(self.queue) < least:
                return
            lane = self.queue.pop(0)
            self.flying[lane].wait_recv()
            t = self.at[lane]
            if t % self.hops == 0:
                self.finish_piece(lane, self.lanes[lane][t // self.hops - 1])
            self.step(lane)

    def finish(self):
        while self.queue:
            self.tick(1, 1)
        self.pass_on(0)
        for cp in self.tail:
            cp.wait()
        for cp in self.sent + [cp for cp in self.first if cp is not None]:
            cp.wait_send()


def sum_scratch(n, lanes, most):
    count = sum(len(lane) for lane in lanes)
    steps = max(len(lane) for lane in lanes) * (n - 1)
    vmem = dict(TERM=((len(lanes), 2, 2) + most, BF), FIRST=((len(lanes),) + most, BF))
    sems = dict(
        term=(len(lanes), 2, 2), ring_send=(len(lanes), steps), ring_recv=(len(lanes), steps), end=(count,),
        end_sib_send=(count,), end_sib_recv=(count,), end_mate_send=(count,), end_mate_recv=(count,), far_send=(count,),
        far_recv=(count,),
    )
    landing = {p: ("L%d_%d" % (p[0], p[1] + p[3]), ((n - 1,) + (p[2], p[4]), BF)) for lane in lanes for p in lane}
    vmem.update(landing.values())
    return vmem, sems, {p: name for p, (name, _) in landing.items()}


def tokens_at(j):
    return pl.ds(pl.multiple_of(j * CHUNK, CHUNK), CHUNK)


class Exchange:
    def __init__(self, spot, k):
        self.spot, self.k = spot, k

    def rows(self, src, j):
        k = self.k
        return remote(src, k.CR.at[tokens_at(j)], k.cross_send.at[j], k.cross_recv.at[j], self.spot.mate)

    def numbers(self, j):
        k = self.k
        return remote(k.SS.at[j], k.SR.at[j], k.score_send.at[j], k.score_recv.at[j], self.spot.mate)

    def send(self, src, numbers, j):
        self.k.SS[j] = flat(numbers)
        self.numbers(j).start()
        self.rows(src, j).start()

    def wait_recv(self, src, j):
        self.numbers(j).wait_recv()
        self.rows(src, j).wait_recv()

    def wait_send(self, src, j):
        self.numbers(j).wait_send()
        self.rows(src, j).wait_send()


def greet(spot):
    barrier = pltpu.get_barrier_semaphore()
    for who in (spot.next, spot.prev, spot.sib, spot.mate):
        pl.semaphore_signal(barrier, inc=1, device_id=who, device_id_type=MESH)
    pl.semaphore_wait(barrier, 4)


def greet_all(spot):
    barrier = pltpu.get_barrier_semaphore()
    others = [(2 * spot.x + spot.c, lax.rem(spot.f + i, spot.n)) for i in range(1, spot.n)]
    for who in [spot.sib, spot.mate] + others:
        pl.semaphore_signal(barrier, inc=1, device_id=who, device_id_type=MESH)
    pl.semaphore_wait(barrier, spot.n + 1)
    return others


class Products:
    def __init__(self, spot, k, tiles):
        self.spot, self.k, self.tiles = spot, k, tiles
        self.busy = {}
        self.next = 0

    def tile(self, value, ref, at, index, away):
        k = self.k
        slot = self.next % k.DW.shape[0]
        self.next += 1
        if slot in self.busy:
            cp, was_away = self.busy.pop(slot)
            cp.wait_send() if was_away else cp.wait()
        buf = k.DW.at[slot, pl.ds(0, value.shape[0]), pl.ds(0, value.shape[1])]
        buf[...] = value.astype(BF)
        if away:
            cp = remote(buf, ref.at[at], k.dw.at[slot], k.dw_recv.at[index], self.spot.sib)
        else:
            cp = pltpu.make_async_copy(buf, ref.at[at], k.dw.at[slot])
        cp.start()
        self.busy[slot] = (cp, away)
        return cp

    def grid(self, left, right, first, cols, half_cols, step, ours, theirs, index, tick):
        c = self.spot.c
        waits = []
        for away in (True, False):
            side = (1 - c) if away else c
            for m in range(left.shape[1] // step):
                at_right = pl.ds(pl.multiple_of(side * half_cols + first, 256), cols)
                value = dot_tn(left[:, pl.ds(m * step, step)], right[:, at_right])
                at = (pl.ds(m * step, step), pl.ds(first, cols))
                cp = self.tile(value, theirs if away else ours, at, index + m, away)
                if away:
                    waits.append(cp)
                tick()
        return waits

    def settle(self):
        for cp, away in self.busy.values():
            cp.wait_send() if away else cp.wait()
        self.busy = {}


def backward_kernel(n, lanes, shard_rows, groups, landing, names, *refs):
    k = Refs(names, refs)
    spot = Spot(n)
    x, c = spot.x, spot.c
    tokens, width = k.GA.shape
    half, chunks = tokens // 2, tokens // CHUNK
    ff = k.GG.shape[1] // 2
    tiles = ff // 256
    scaling = 1.0 / math.sqrt(width // HEADS)
    loads = {}

    def load(name, src, dst, sem):
        cp = pltpu.make_async_copy(src, dst, sem)
        cp.start()
        loads[name] = cp

    def load_tile(t):
        slot = t % 2
        load(("wd", t), k.wd.at[pl.ds(t * 256, 256)], k.WT.at[slot], k.tile.at[slot, 0])
        for h in range(2):
            load(("gu", t, h), k.gu.at[h * tiles + t], k.GT.at[slot, h], k.tile.at[slot, 1 + h])

    load("gy", k.gy, k.GY, k.load.at[0])
    load_tile(0)
    load_tile(1)
    load("n2", k.n2, k.N2, k.load.at[1])
    load("gain", k.gain, k.G, k.load.at[2])
    load("p", k.p, k.P, k.load.at[3])
    load("wo", k.wo, k.Wo, k.load.at[4])
    head_table(k.E)
    k.GS[...] = jnp.zeros_like(k.GS)
    greet(spot)

    ring = Sums(
        spot, lanes, shard_rows, (width // 2, ff), (k.dwd, k.o_own), (k.sib, k.o_sib), (k.o_rwd, k.o_rwg),
        {p: getattr(k, name) for p, name in landing.items()}, k,
    )
    ring.offer([lane[0] for lane in lanes])
    swap = Exchange(spot, k)

    loads["gy"].wait()
    for t in range(tiles):
        slot = t % 2
        loads["wd", t].wait()
        for h in range(2):
            loads["gu", t, h].wait()
            rows = pl.ds(h * half, half)
            grad = dot_nt(k.GY[rows], k.WT[slot])
            gate, up = k.GT[slot, h, 0].astype(F32), k.GT[slot, h, 1].astype(F32)
            sigma = jax.nn.sigmoid(gate)
            k.GG[rows, pl.ds(t * 256, 256)] = (grad * up * sigma * (1.0 + gate * (1.0 - sigma))).astype(BF)
            k.GG[rows, pl.ds(ff + t * 256, 256)] = (grad * gate * sigma).astype(BF)
            if h:
                ring.tick(1)
        if t + 2 < tiles:
            load_tile(t + 2)
        if t == 2:
            load("wg", k.wg, k.Wg, k.load.at[5])

    products = Products(spot, k, None)
    made = []

    def weight_group(g):
        first, cols = groups[g]
        made.append((g, products.grid(
            k.N2, k.GG, first, cols, ff, 512, k.o_own, k.o_sib, 2 * g, lambda: ring.tick(1)
        )))

    def offer_groups():
        if made:
            products.settle()
        while made:
            g, waits = made.pop(0)
            for cp in waits:
                cp.wait_recv()
            ring.offer([lanes[g][1]])

    def load_rows(j):
        load(("mid", j), k.mid.at[tokens_at(j)], k.MID, k.load.at[6])
        load(("v", j), k.qkv.at[tokens_at(j), pl.ds(2 * width, width)], k.V, k.load.at[7])

    load_rows(0)
    loads["gain"].wait()
    loads["wg"].wait()
    loads["wo"].wait()
    outs = {}

    def norm_chunk(j):
        rows = tokens_at(j)
        for m in range(4):
            part = pl.ds(m * 256, 256)
            k.GN[:, part] = dot_nt(k.GG[rows], k.Wg[part])
            if m % 2:
                ring.tick(1)
            if m == 0:
                offer_groups()
        for name in ("mid", "v"):
            loads[name, j].wait()
        middle, upstream = k.MID[...], k.GN[...]
        scale = rms_scale(middle)
        k.GS[0:1] += jnp.sum(upstream * middle * scale, axis=0, keepdims=True)
        grad = k.GY[rows].astype(F32) + norm_backward(middle, scale, k.G[1:2], upstream)
        if j:
            for cp in outs[j - 1]:
                cp.wait()
        k.GM[...] = grad
        k.GB[...] = grad.astype(BF)
        outs[j] = [
            pltpu.make_async_copy(k.GM, k.o_gm.at[rows], k.put.at[0]),
            pltpu.make_async_copy(k.GB, k.o_gb.at[rows], k.put.at[1]),
        ]
        for cp in outs[j]:
            cp.start()
        k.GA[rows] = dot_nt(k.GB[...], k.Wo[...]).astype(BF)
        numbers = per_head(k.GA[rows].astype(F32) * k.V[...].astype(F32), k.E)
        k.GP[rows] = numbers
        if j + 1 < chunks:
            load_rows(j + 1)

        @pl.when(x == 1)
        def _():
            swap.send(k.GA.at[rows], numbers, j)

        ring.tick(1)

    loads["n2"].wait()
    for g in range(4):
        weight_group(g)
        if g: offer_groups()
    for j in range(chunks):
        norm_chunk(j)
    loads["p"].wait()

    for j in range(chunks):
        rows = tokens_at(j)
        load(("qkv", j), k.qkv.at[rows], k.Wg.at[rows, pl.ds(0, 3 * width)], k.again.at[0, j])
        load(("cr", j), k.cr.at[rows], k.Wg.at[rows, pl.ds(3 * width, width)], k.again.at[1, j])

    def parts(rows):
        return (k.Wg[rows, i * width : (i + 1) * width].astype(F32) for i in range(3))

    def store(rows, j, *grads):
        for i, grad in enumerate(grads):
            k.Wg[rows, i * width : (i + 1) * width] = grad.astype(BF)
        pltpu.make_async_copy(k.Wg.at[rows, pl.ds(0, 3 * width)], k.o_gqkv.at[rows], k.back.at[j]).start()

    def serve(j):
        rows = tokens_at(j)

        @pl.when(x == 0)
        def _():
            swap.wait_recv(k.GA.at[rows], j)
            query, key, value = parts(rows)
            there = k.CR[rows].astype(F32)
            prob, prob_c, prob_d = k.P[0, rows], k.P[1, rows], k.P[2, rows]
            grad_c = per_head(there * value, k.E)
            total_c = prob_c * grad_c + prob_d * tall(k.SR[j])
            score_c = spread_two(prob_c * (grad_c - total_c) * scaling, k.E)
            k.CS[rows] = (score_c * key).astype(BF)
            swap.send(k.CS.at[rows], total_c, j)
            grad = k.GP[rows]
            score = spread_two(prob * (grad - prob * grad) * scaling, k.E)
            ours = k.GA[rows].astype(F32)
            store(
                rows, j, score * key, score * query + score_c * k.Wg[rows, 3 * width : 4 * width].astype(F32),
                spread(prob.astype(BF), k.E) * ours + spread(prob_c.astype(BF), k.E) * there,
            )

    def close(j):
        rows = tokens_at(j)

        @pl.when(x == 1)
        def _():
            swap.wait_recv(k.GA.at[rows], j)
            query, key, value = parts(rows)
            prob = k.P[0, rows]
            score = spread_two(prob * (k.GP[rows] - tall(k.SR[j])) * scaling, k.E)
            store(
                rows, j, score * key + k.CR[rows].astype(F32), score * query,
                spread(prob.astype(BF), k.E) * k.GA[rows].astype(F32),
            )

    for j in range(chunks):
        loads["qkv", j].wait()
        loads["cr", j].wait()
        serve(j)
        if j:
            close(j - 1)
        offer_groups()
        ring.tick(4)
    close(chunks - 1)
    while ring.queue:
        ring.tick(1, 1)
    ring.finish()
    for cp in outs[chunks - 1]:
        cp.wait()
    cp = pltpu.make_async_copy(k.GS, k.o_gain, k.load.at[0])
    cp.start()
    cp.wait()
    for j in range(chunks):
        rows = tokens_at(j)
        swap.wait_send(k.GA.at[rows], j)
        pltpu.make_async_copy(k.Wg.at[rows, pl.ds(0, 3 * width)], k.o_gqkv.at[rows], k.back.at[j]).wait()


def backward(n, fw):
    tokens, width = fw.o_x.shape
    ff = fw.o_hid.shape[1]
    chunks = tokens // CHUNK
    shard_rows = (ff // n, width // n)
    cuts = [256 * ((ff // 256 * i + 3) // 4) for i in range(5)]
    groups = [(cuts[i], cuts[i + 1] - cuts[i]) for i in range(4)]
    down = [p for p in pieces_of([(shard_rows[0], width)], (4,))]
    lanes = [
        [(0, down[i][1], down[i][2], 0, width // 2), (1, 0, shard_rows[1], groups[i][0], groups[i][1])] for i in range(4)
    ]
    most = (max(p[2] for lane in lanes for p in lane), max(p[4] for lane in lanes for p in lane))
    ring_vmem, ring_sems, landing = sum_scratch(n, lanes, most)
    square = (tokens, width)
    ins = dict(
        gy=fw.o_gy, n2=fw.o_n2, gu=fw.o_gu, wd=fw.o_wd, wg=fw.o_wg, wo=fw.o_wo, mid=fw.o_mid,
        qkv=fw.o_qkv, p=fw.o_p, cr=fw.o_cr, dwd=fw.o_dwd, sib=fw.o_sib, gain=fw.o_gain,
    )
    out = dict(
        o_gb=(square, BF), o_gm=(square, F32), o_gqkv=((tokens, 3 * width), BF), o_gain=((8, width), F32),
        o_own=((width, ff), BF), o_sib=((width, ff), BF), o_rwd=((2, shard_rows[0], width), BF),
        o_rwg=((2, shard_rows[1], 2 * ff), BF),
    )
    vmem = dict(
        GY=(square, BF), N2=(square, BF), GG=((tokens, 2 * ff), BF), Wg=((width, 2 * ff), BF),
        Wo=((width, width), BF), WT=((2, 256, width), BF), GT=((2, 2, 2, tokens // 2, 256), BF),
        DW=((3, 512, max(g[1] for g in groups)), BF), GN=((CHUNK, width), F32), MID=((CHUNK, width), F32),
        V=((CHUNK, width), BF), GM=((CHUNK, width), F32), GB=((CHUNK, width), BF), GA=(square, BF),
        CR=(square, BF), CS=(square, BF), P=((3, tokens, 128), F32), GP=((tokens, 128), F32),
        SS=((chunks, HEADS, CHUNK), F32), SR=((chunks, HEADS, CHUNK), F32), E=((width, 128), BF),
        G=((8, width), F32), GS=((8, width), F32), **ring_vmem,
    )
    sems = dict(
        tile=(2, 3), load=(8,), put=(2,), dw=(3,), dw_recv=(8,), again=(2, chunks), back=(chunks,),
        cross_send=(chunks,), cross_recv=(chunks,), score_send=(chunks,), score_recv=(chunks,), **ring_sems,
    )
    return call(backward_kernel, (n, lanes, shard_rows, groups, landing), ins, out, vmem, sems, 1)


def call(kernel, static, ins, out, vmem, sems, number):
    hbm = pl.BlockSpec(memory_space=pltpu.HBM)
    dma = pltpu.SemaphoreType.DMA
    names = list(ins) + list(out) + list(vmem) + list(sems)
    outs = pl.pallas_call(
        functools.partial(kernel, *static, names),
        out_shape=[jax.ShapeDtypeStruct(*o) for o in out.values()],
        in_specs=[hbm] * len(ins),
        out_specs=[hbm] * len(out),
        scratch_shapes=[pltpu.VMEM(*v) for v in vmem.values()] + [dma(v) for v in sems.values()],
        compiler_params=pltpu.CompilerParams(
            collective_id=number, has_side_effects=True, vmem_limit_bytes=64 * 2**20 - 2**16
        ),
        name=kernel.__name__,
    )(*ins.values())
    return Refs(list(out), outs)


def closing_kernel(n, lanes, shard_rows, landing, names, *refs):
    k = Refs(names, refs)
    spot = Spot(n)
    x, c = spot.x, spot.c
    tokens, width = k.N1.shape
    half, chunks = tokens // 2, tokens // CHUNK
    ff = k.HID.shape[1]
    loads = {}
    for i, (name, src, dst) in enumerate((
        ("att", k.att, k.ATT), ("gb", k.gb, k.GB), ("hid", k.hid, k.HID), ("wd", k.wd, k.Wd), ("n1", k.n1, k.N1),
        ("gqkv", k.gqkv, k.GQ), ("gain", k.gain, k.G), ("wq", k.wq, k.Wq), ("x", k.x, k.X), ("gs", k.gf, k.GF),
    )):
        loads[name] = pltpu.make_async_copy(src, dst, k.load.at[i])
        loads[name].start()
    k.GS[...] = jnp.zeros_like(k.GS)
    others = greet_all(spot)
    ring = Sums(
        spot, lanes, shard_rows, (width // 2, 3 * width // 2), (k.o_own, k.q_own), (k.o_sib, k.q_sib), (k.o_rwo, k.o_rwq),
        {p: getattr(k, name) for p, name in landing.items()}, k,
    )

    sends = []

    def row_chunk(i):
        j = i % (chunks // 2)
        block = (1 - x) if i < chunks // 2 else x
        return pl.ds(pl.multiple_of(block * half + j * CHUNK, CHUNK), CHUNK), pl.ds(j * CHUNK, CHUNK)

    def deliver(buf, whole, i, first):
        _, at = row_chunk(i)
        if i < chunks // 2:
            cp = remote(buf, whole.at[x, at], k.far_rows_send.at[first + i], k.far_rows_recv.at[first + i], spot.mate)
        else:
            cp = pltpu.make_async_copy(buf, whole.at[x, at], k.near_rows.at[first + i])
        cp.start()
        sends.append(cp)

    mids = {}

    def load_mid(i):
        rows, _ = row_chunk(i)
        mids[i] = pltpu.make_async_copy(k.mid.at[rows], k.MID.at[i % 2], k.rows.at[i % 2, 1])
        mids[i].start()

    grads_in = {}

    def load_grad(i):
        rows, _ = row_chunk(i)
        grads_in[i] = pltpu.make_async_copy(k.gm.at[rows], k.GM.at[i % 2], k.rows.at[i % 2, 0])
        grads_in[i].start()

    def output_chunk(i):
        rows, _ = row_chunk(i)
        for m in range(2):
            part = pl.ds(m * 512, 512)
            k.GN[:, part] = dot(k.HID[rows], k.Wd[:, part])
            ring.tick(1)
        mids[i].wait()
        k.OUT[i] = (k.MID[i % 2] + k.GN[...]).astype(BF)
        deliver(k.OUT.at[i], k.o_out, i, chunks)
        if i + 2 < chunks:
            load_mid(i + 2)

    def input_chunk(i):
        rows, _ = row_chunk(i)
        for m in range(4):
            part = pl.ds(m * 256, 256)
            k.GN[:, part] = dot_nt(k.GQ[rows], k.Wq[part])
            if m % 2:
                ring.tick(1)
        values, upstream = k.X[rows].astype(F32), k.GN[...]
        scale = rms_scale(values)
        k.GS[0:1] += jnp.sum(upstream * values * scale, axis=0, keepdims=True)
        grads_in[i].wait()
        k.IN[i] = (k.GM[i % 2] + norm_backward(values, scale, k.G[0:1], upstream)).astype(BF)
        deliver(k.IN.at[i], k.o_in, i, 0)
        ring.tick(1)
        if i + 2 < chunks:
            load_grad(i + 2)

    load_mid(0)
    load_mid(1)
    load_grad(0)
    load_grad(1)
    products = Products(spot, k, None)
    loads["att"].wait()
    loads["gb"].wait()
    waits = products.grid(k.ATT, k.GB, 0, width // 2, width // 2, 512, k.o_own, k.o_sib, 0, lambda: None)
    loads["hid"].wait()
    loads["wd"].wait()
    output_chunk(0)
    output_chunk(1)
    loads["n1"].wait()
    loads["gqkv"].wait()
    products.settle()
    for cp in waits:
        cp.wait_recv()
    ring.offer([p for lane in lanes for p in lane if p[0] == 0])
    queue = []
    cols = 3 * width // 4
    calls = []

    def offer_queued():
        products.settle()
        while queue:
            waits, pieces = queue.pop(0)
            for cp in waits:
                cp.wait_recv()
            ring.offer(pieces)

    def between():
        calls.append(0)
        if len(calls) == 6:
            offer_queued()
        ring.tick(1)

    for g in range(2):
        waits = products.grid(
            k.N1, k.GQ, g * cols, cols, 2 * cols, 512, k.q_own, k.q_sib, 2 + 2 * g, between
        )
        queue.append((waits, [p for lane in lanes for p in lane if p[0] == 1 and p[3] // cols == g]))
    offer_queued()

    loads["gain"].wait()
    loads["wq"].wait()
    loads["x"].wait()
    for i in range(chunks):
        input_chunk(i)
    for i in range(chunks // 2, chunks):
        output_chunk(i)
        ring.tick(2)
    part = width // n
    loads["gs"].wait()
    for j in range(n):
        k.GP[j] = jnp.zeros_like(k.GP[j])
        for row, ref in enumerate((k.GS, k.GF)):
            k.GP[j, pl.ds(row, 1)] = ref[0:1, j * part : (j + 1) * part]
    gains = []
    for i, who in enumerate(others):
        to = who[1]
        cp = remote(k.GP.at[to], k.GR.at[i], k.gain_send.at[i], k.gain_recv.at[i], who)
        cp.start()
        gains.append(cp)
    ring.tick(2)
    total = k.GP[spot.f]
    for i, cp in enumerate(gains):
        cp.wait()
        total = total + k.GR[i]
    k.GT[0] = total
    cp = remote(k.GT.at[0], k.GT.at[1], k.gain_send.at[n - 1], k.gain_recv.at[n - 1], spot.sib)
    cp.start()
    ring.tick(2)
    cp.wait()
    k.GT[2] = jnp.where(c == 0, k.GT[0], k.GT[1]) + jnp.where(c == 0, k.GT[1], k.GT[0])
    cp = remote(k.GT.at[2], k.o_gain.at[x], k.gain_send.at[n], k.gain_recv.at[n], spot.mate)
    cp.start()
    near = pltpu.make_async_copy(k.GT.at[2], k.o_gain.at[x], k.rows.at[0, 0])
    near.start()
    ring.finish()
    cp.wait()
    near.wait()
    for cp in sends:
        cp.wait()


def closing(n, fw, bw):
    tokens, width = fw.o_x.shape
    ff = fw.o_hid.shape[1]
    chunks = tokens // CHUNK
    shard_rows = (width // n, width // n)
    cols = 3 * width // 8
    lanes = [[(1, 0, shard_rows[1], i * cols, cols)] for i in range(4)] + [
        [(0, 0, shard_rows[0], i * width // 4, width // 4)] for i in range(2)
    ]
    most = (max(p[2] for lane in lanes for p in lane), max(p[4] for lane in lanes for p in lane))
    ring_vmem, ring_sems, landing = sum_scratch(n, lanes, most)
    square = (tokens, width)
    ins = dict(
        att=fw.o_att, gb=bw.o_gb, n1=fw.o_n1, gqkv=bw.o_gqkv, gain=fw.o_gain, wq=fw.o_wq, x=fw.o_x,
        hid=fw.o_hid, wd=fw.o_wd, gm=bw.o_gm, mid=fw.o_mid, gf=bw.o_gain,
    )
    out = dict(
        o_own=((width, width // 2), BF), o_sib=((width, width // 2), BF), q_own=((width, 3 * width // 2), BF),
        q_sib=((width, 3 * width // 2), BF), o_rwo=((2, shard_rows[0], width), BF),
        o_rwq=((2, shard_rows[1], 3 * width), BF), o_in=((2, tokens // 2, width), BF),
        o_out=((2, tokens // 2, width), BF), o_gain=((2, 8, width // n), F32),
    )
    vmem = dict(
        ATT=(square, BF), GB=(square, BF), N1=(square, BF), GQ=((tokens, 3 * width), BF), G=((8, width), F32),
        GS=((8, width), F32), GF=((8, width), F32), GP=((n, 8, width // n), F32), GR=((n - 1, 8, width // n), F32),
        GT=((3, 8, width // n), F32), Wq=((width, 3 * width), BF), X=(square, BF), HID=((tokens, ff), BF),
        Wd=((ff, width), BF), GN=((CHUNK, width), F32), GM=((2, CHUNK, width), F32), MID=((2, CHUNK, width), F32),
        IN=((chunks, CHUNK, width), BF), OUT=((chunks, CHUNK, width), BF), DW=((4, 512, 3 * width // 4), BF),
        **ring_vmem,
    )
    sems = dict(
        load=(10,), gain_send=(n + 1,), gain_recv=(n + 1,), rows=(2, 2), far_rows_send=(2 * chunks,), far_rows_recv=(2 * chunks,),
        near_rows=(2 * chunks,), dw=(4,), dw_recv=(6,), **ring_sems,
    )
    return call(closing_kernel, (n, lanes, shard_rows, landing), ins, out, vmem, sems, 2)


def valid_rows(item_lengths, frame_offsets):
    slot = jnp.arange(ITEM_SLOTS)[None, None, :]
    first = frame_offsets[:, :, None]
    valid = (slot >= first) & (slot < first + item_lengths[:, :, None])
    return valid.reshape(-1)


def by_position(n, block_input, out_grad, item_lengths, frame_offsets, norm_attn, w_qkv, w_out, norm_ffn, w_gate_up, w_down):
    x, c, f, r = place(n)
    micro, frames, positions, width = block_input.shape
    rows = micro * frames
    valid = valid_rows(item_lengths, frame_offsets)[:, None]
    inputs = block_input.reshape(rows, positions, width)
    upstream = jnp.where(valid[..., None], out_grad.reshape(rows, positions, width), 0)

    def take(array, at):
        return lax.dynamic_index_in_dim(array, at, 1, keepdims=False)

    gn = jnp.stack([norm_attn, norm_ffn], axis=1)
    gn = jnp.pad(lax.dynamic_index_in_dim(gn, x, 0, keepdims=False), ((0, 14), (0, 0)))
    fw = forward(
        n, take(inputs, 1 - x), take(inputs, x), take(upstream, 1 - x), take(upstream, x), w_qkv, w_out, w_gate_up, w_down, gn
    )
    bw = backward(n, fw)
    cl = closing(n, fw, bw)
    grads = [g.astype(F32) for g in (cl.o_rwq, cl.o_rwo, bw.o_rwg, bw.o_rwd)]
    def home(array):
        return array.transpose(1, 0, 2).reshape(micro, frames, positions, width)

    return home(cl.o_out), home(cl.o_in), cl.o_gain[:, 0], grads[0], grads[1], cl.o_gain[:, 1], grads[2], grads[3]


def shortened(x):

    def short(part):
        return part.astype(jnp.bfloat16) if part.dtype == jnp.float32 else part

    return jax.tree.map(short, x)


PRECISE = lax.Precision.HIGHEST
matmul, times_transposed, contract_rows = dot, dot_nt, dot_tn


def by_weights(
    block_input,
    out_grad,
    item_lengths,
    frame_offsets,
    norm_attn,
    w_qkv,
    w_out,
    norm_ffn,
    w_gate_up,
    w_down,
):
    micro, frames, positions, model_width = block_input.shape
    head_dim = model_width // HEADS
    hidden_size = w_gate_up.shape[2] // 2
    head_shape = (frames, positions, HEADS, head_dim)
    slot_index = jnp.arange(ITEM_SLOTS)[None, None, :]
    first_slot = frame_offsets[:, :, None]
    valid_rows = (slot_index >= first_slot) & (slot_index < first_slot + item_lengths[:, :, None])
    valid_rows = valid_rows.astype(jnp.float32).reshape(micro, frames)
    causal = jnp.arange(positions)[:, None] >= jnp.arange(positions)[None, :]
    totals = (
        jnp.zeros((positions, model_width), jnp.float32),
        jnp.zeros((positions, model_width, 3 * model_width), jnp.float32),
        jnp.zeros((positions, model_width, model_width), jnp.float32),
        jnp.zeros((positions, model_width), jnp.float32),
        jnp.zeros((positions, model_width, 2 * hidden_size), jnp.float32),
        jnp.zeros((positions, hidden_size, model_width), jnp.float32),
    )
    output_list = []
    input_grad_list = []
    for batch_index in range(micro):
        inputs = block_input[batch_index].astype(jnp.float32)
        qkv_all, gain_in_all = (
            lax.all_gather(w_qkv, "fsdp", axis=1, tiled=True),
            lax.all_gather(norm_attn, "fsdp", axis=1, tiled=True),
        )
        first_saved = []
        qkv_list = []
        for place in range(positions):
            rows = inputs[:, place]
            scale_one = rms_scale(rows)
            normed = (rows * scale_one * gain_in_all[place]).astype(jnp.bfloat16)
            first_saved.append((scale_one, normed))
            qkv_list.append(matmul(normed, qkv_all[place]).astype(jnp.bfloat16))
        qkv_proj = jnp.stack(qkv_list, axis=1)
        query_heads = qkv_proj[..., :model_width].reshape(head_shape)
        key_heads = qkv_proj[..., model_width : 2 * model_width].reshape(head_shape)
        value_heads = qkv_proj[..., 2 * model_width :].reshape(head_shape)
        scores = jnp.einsum(
            "fihd,fjhd->fhij", query_heads, key_heads, preferred_element_type=jnp.float32
        ) / math.sqrt(head_dim)
        scores = jnp.where(causal, scores, -1e30)
        attention = jax.nn.softmax(scores, axis=-1)
        attention_low = attention.astype(jnp.bfloat16)
        mixed_heads = jnp.einsum(
            "fhij,fjhd->fihd", attention_low, value_heads, preferred_element_type=jnp.float32
        )
        mixed_heads = mixed_heads.reshape(frames, positions, model_width).astype(jnp.bfloat16)
        out_all, gain_two_all, gu_all, down_all = (
            lax.all_gather(w_out, "fsdp", axis=1, tiled=True),
            lax.all_gather(norm_ffn, "fsdp", axis=1, tiled=True),
            lax.all_gather(w_gate_up, "fsdp", axis=1, tiled=True),
            lax.all_gather(w_down, "fsdp", axis=1, tiled=True),
        )
        second_saved = []
        output_rows = []
        for place in range(positions):
            middle = inputs[:, place] + matmul(mixed_heads[:, place], out_all[place])
            scale_two = rms_scale(middle)
            normed_two = (middle * scale_two * gain_two_all[place]).astype(jnp.bfloat16)
            gate_up = matmul(normed_two, gu_all[place])
            hidden = (jax.nn.silu(gate_up[:, :hidden_size]) * gate_up[:, hidden_size:]).astype(
                jnp.bfloat16
            )
            second_saved.append((middle, scale_two, normed_two, gate_up, hidden))
            output_rows.append((middle + matmul(hidden, down_all[place])).astype(jnp.bfloat16))
        output_list.append(jnp.stack(output_rows, axis=1))
        upstream = (
            out_grad[batch_index].astype(jnp.float32) * valid_rows[batch_index][:, None, None]
        )
        out_all, gain_two_all, gu_all, down_all = (
            lax.all_gather(w_out, "fsdp", axis=1, tiled=True),
            lax.all_gather(norm_ffn, "fsdp", axis=1, tiled=True),
            lax.all_gather(w_gate_up, "fsdp", axis=1, tiled=True),
            lax.all_gather(w_down, "fsdp", axis=1, tiled=True),
        )
        out_grads = []
        gain_two_grads = []
        gu_grads = []
        down_grads = []
        middle_grads = []
        attn_grads = []
        for place in range(positions):
            middle, scale_two, normed_two, gate_up, hidden = second_saved[place]
            gate = gate_up[:, :hidden_size]
            up_part = gate_up[:, hidden_size:]
            grad_ffn = upstream[:, place].astype(jnp.bfloat16)
            down_grads.append(contract_rows(hidden, grad_ffn))
            grad_hidden = times_transposed(grad_ffn, down_all[place])
            sigma = jax.nn.sigmoid(gate)
            grad_gate = grad_hidden * up_part * sigma * (1.0 + gate * (1.0 - sigma))
            grad_up = grad_hidden * jax.nn.silu(gate)
            grad_gate_up = jnp.concatenate([grad_gate, grad_up], axis=-1).astype(jnp.bfloat16)
            gu_grads.append(contract_rows(normed_two, grad_gate_up))
            grad_normed_two = times_transposed(grad_gate_up, gu_all[place])
            gain_two_grads.append(jnp.sum(grad_normed_two * middle * scale_two, axis=0))
            grad_middle = upstream[:, place] + norm_backward(
                middle, scale_two, gain_two_all[place], grad_normed_two
            )
            grad_branch = grad_middle.astype(jnp.bfloat16)
            out_grads.append(contract_rows(mixed_heads[:, place], grad_branch))
            attn_grads.append(times_transposed(grad_branch, out_all[place]).astype(jnp.bfloat16))
            middle_grads.append(grad_middle)
        grad_mixed = jnp.stack(attn_grads, axis=1).reshape(head_shape)
        grad_attention = jnp.einsum(
            "fihd,fjhd->fhij", grad_mixed, value_heads, preferred_element_type=jnp.float32
        )
        grad_values = jnp.einsum(
            "fhij,fihd->fjhd", attention_low, grad_mixed, preferred_element_type=jnp.float32
        )
        grad_scores = attention * (
            grad_attention - jnp.sum(attention * grad_attention, axis=-1, keepdims=True)
        )
        grad_scores = grad_scores / math.sqrt(head_dim)
        grad_query = jnp.einsum(
            "fhij,fjhd->fihd", grad_scores, key_heads.astype(jnp.float32), precision=PRECISE
        )
        grad_keys = jnp.einsum(
            "fhij,fihd->fjhd", grad_scores, query_heads.astype(jnp.float32), precision=PRECISE
        )
        flat_shape = (frames, positions, model_width)
        grad_qkv = jnp.concatenate(
            [
                grad_query.reshape(flat_shape),
                grad_keys.reshape(flat_shape),
                grad_values.reshape(flat_shape),
            ],
            axis=-1,
        ).astype(jnp.bfloat16)
        qkv_all, gain_in_all = (
            lax.all_gather(w_qkv, "fsdp", axis=1, tiled=True),
            lax.all_gather(norm_attn, "fsdp", axis=1, tiled=True),
        )
        qkv_grads = []
        gain_one_grads = []
        input_rows = []
        for place in range(positions):
            scale_one, normed = first_saved[place]
            rows = inputs[:, place]
            qkv_grads.append(contract_rows(normed, grad_qkv[:, place]))
            grad_normed = times_transposed(grad_qkv[:, place], qkv_all[place])
            gain_one_grads.append(jnp.sum(grad_normed * rows * scale_one, axis=0))
            input_rows.append(
                (
                    middle_grads[place]
                    + norm_backward(rows, scale_one, gain_in_all[place], grad_normed)
                ).astype(jnp.bfloat16)
            )
        input_grad_list.append(jnp.stack(input_rows, axis=1))
        batch_grads = (
            jnp.stack(gain_one_grads),
            jnp.stack(qkv_grads),
            jnp.stack(out_grads),
            jnp.stack(gain_two_grads),
            jnp.stack(gu_grads),
            jnp.stack(down_grads),
        )
        totals = tuple((total + update for total, update in zip(totals, batch_grads)))
    totals = (
        lax.psum_scatter(totals[0], "fsdp", scatter_dimension=1, tiled=True),
        lax.psum_scatter(totals[1], "fsdp", scatter_dimension=1, tiled=True),
        lax.psum_scatter(totals[2], "fsdp", scatter_dimension=1, tiled=True),
        lax.psum_scatter(totals[3], "fsdp", scatter_dimension=1, tiled=True),
        lax.psum_scatter(totals[4], "fsdp", scatter_dimension=1, tiled=True),
        lax.psum_scatter(totals[5], "fsdp", scatter_dimension=1, tiled=True),
    )
    totals = jax.tree.map(lambda part: part.astype(jnp.float32), lax.psum(shortened(totals), "dp"))
    return (
        jnp.stack(output_list),
        jnp.stack(input_grad_list),
        totals[0],
        totals[1],
        totals[2],
        totals[3],
        totals[4],
        totals[5],
    )


def fits(mesh, shapes):
    return mesh.shape["dp"] == 4 and all(s[1] % 16 == 0 for s in shapes) and shapes[0][1] % 128 == 0


def solution(mesh):
    n = mesh.shape["fsdp"]

    def on_device(*args):
        if fits(mesh, [args[k].shape for k in (5, 6, 8, 9)]):
            return by_position(n, *args)
        return by_weights(*args)

    placed = (
        P(None, ("dp", "fsdp"), None, None),
        P(None, ("dp", "fsdp"), None, None),
        P(None, ("dp", "fsdp")),
        P(None, ("dp", "fsdp")),
        P(None, "fsdp"),
        P(None, "fsdp", None),
        P(None, "fsdp", None),
        P(None, "fsdp"),
        P(None, "fsdp", None),
        P(None, "fsdp", None),
    )
    return jax.shard_map(
        on_device,
        mesh=mesh,
        in_specs=placed,
        out_specs=(
            P(None, ("dp", "fsdp"), None, None),
            P(None, ("dp", "fsdp"), None, None),
            P(None, "fsdp"),
            P(None, "fsdp", None),
            P(None, "fsdp", None),
            P(None, "fsdp"),
            P(None, "fsdp", None),
            P(None, "fsdp", None),
        ),
        check_vma=False,
    )
```
